32 devices in a mesh: dp: 8 (over z, y), blk: 4 (over x, core).
Axes of the slice: x: 2, y: 2, z: 4, core: 2. Of those that a mesh axis runs over, the one named last changes fastest.
Arguments:
- patches: bfloat16 [4096, 1024], P(('dp', 'blk')), may hold values from -6 to 6
- lengths: int32 [8, 8], P('dp'), may hold values from 1 to 385, 512 in all within a row
- gsd_scale: float32 [8, 8], P('dp'), may hold values from 0.5 to 4
- visible: int32 [8, 512], P('dp'), may hold values from 0 to 1, as said below
- encoder_gain_first: bfloat16 [1024], P('dp'), may hold values from 0.5 to 1.5
- encoder_bias_first: bfloat16 [1024], P('dp'), may hold values from -1 to 1
- encoder_query: bfloat16 [1024, 1024], P('dp'), may hold values from -0.1875 to 0.1875
- encoder_key: bfloat16 [1024, 1024], P('dp'), may hold values from -0.1875 to 0.1875
- encoder_value: bfloat16 [1024, 1024], P('dp'), may hold values from -0.1875 to 0.1875
- encoder_output: bfloat16 [1024, 1024], P('dp'), may hold values from -0.5 to 0.5
- encoder_gain_second: bfloat16 [1024], P('dp'), may hold values from 0.5 to 1.5
- encoder_bias_second: bfloat16 [1024], P('dp'), may hold values from -1 to 1
- encoder_up: bfloat16 [1024, 4096], P('dp'), may hold values from -0.1875 to 0.1875
- encoder_down: bfloat16 [4096, 1024], P('dp'), may hold values from -0.09375 to 0.09375
- embed_proj: bfloat16 [1024, 512], P('dp'), may hold values from -0.1875 to 0.1875
- mask_token: bfloat16 [512], P('dp'), may hold values from -6 to 6
- decoder_gain_first: bfloat16 [512], P('dp'), may hold values from 0.5 to 1.5
- decoder_bias_first: bfloat16 [512], P('dp'), may hold values from -1 to 1
- decoder_query: bfloat16 [512, 512], P('dp'), may hold values from -0.25 to 0.25
- decoder_key: bfloat16 [512, 512], P('dp'), may hold values from -0.25 to 0.25
- decoder_value: bfloat16 [512, 512], P('dp'), may hold values from -0.25 to 0.25
- decoder_output: bfloat16 [512, 512], P('dp'), may hold values from -1 to 1
- decoder_gain_second: bfloat16 [512], P('dp'), may hold values from 0.5 to 1.5
- decoder_bias_second: bfloat16 [512], P('dp'), may hold values from -1 to 1
- decoder_up: bfloat16 [512, 2048], P('dp'), may hold values from -0.25 to 0.25
- decoder_down: bfloat16 [2048, 512], P('dp'), may hold values from -0.125 to 0.125
- cotangent: bfloat16 [4096, 512], P(('dp', 'blk')), may hold values from -6 to 6
Outputs:
- decoded_rows: bfloat16 [4096, 512], P(('dp', 'blk'))
- grad_patches: float32 [4096, 1024], P(('dp', 'blk'))
- grad_encoder_gain_first: float32 [1024], P('dp')
- grad_encoder_bias_first: float32 [1024], P('dp')
- grad_encoder_query: float32 [1024, 1024], P('dp')
- grad_encoder_key: float32 [1024, 1024], P('dp')
- grad_encoder_value: float32 [1024, 1024], P('dp')
- grad_encoder_output: float32 [1024, 1024], P('dp')
- grad_encoder_gain_second: float32 [1024], P('dp')
- grad_encoder_bias_second: float32 [1024], P('dp')
- grad_encoder_up: float32 [1024, 4096], P('dp')
- grad_encoder_down: float32 [4096, 1024], P('dp')
- grad_embed_proj: float32 [1024, 512], P('dp')
- grad_mask_token: float32 [512], P('dp')
- grad_decoder_gain_first: float32 [512], P('dp')
- grad_decoder_bias_first: float32 [512], P('dp')
- grad_decoder_query: float32 [512, 512], P('dp')
- grad_decoder_key: float32 [512, 512], P('dp')
- grad_decoder_value: float32 [512, 512], P('dp')
- grad_decoder_output: float32 [512, 512], P('dp')
- grad_decoder_gain_second: float32 [512], P('dp')
- grad_decoder_bias_second: float32 [512], P('dp')
- grad_decoder_up: float32 [512, 2048], P('dp')
- grad_decoder_down: float32 [2048, 512], P('dp')
The draws below stay inside these ranges and needn't reach their ends.
Inputs may be any that keep to these rules, and one draw needn't show every extreme that they name: `lengths`: each row lists the patch counts of the 8 images of one group in order; they sum to 512 and the largest is 385. `visible`: each row (one group) has exactly 128 ones, placed anywhere among its 512 patches.
All inputs are finite; a program needn't handle non-finite values.
Results may differ from the reference program's by a relative error of at most 0.023.
Values may be sent and summed in bfloat16 or wider, within the bound.
A program may use at most 384 MiB of HBM per device.

```python
import math
import jax
import jax.numpy as jnp
import numpy as np
from jax import lax

D = 1024
HEADS = 16
FF = 4096
DEC_D = 512
DEC_HEADS = 16
DEC_FF = 2048
IMAGES = 8
GROUP = 512
LONGEST = 385
TOKENS = 4096
N_DP = 8


def draw_visible(key, part):
    key = jax.random.fold_in(key, 11)
    group_keys = jax.random.split(key, N_DP)
    orders = jax.vmap(lambda one_key: jax.random.permutation(one_key, GROUP))(group_keys)
    return (orders < GROUP // 4).astype(jnp.int32)


def levels(stream_key, shape, shards, least, top_value):
    def one(axis_at, parts):
        steps = jax.random.uniform(jax.random.fold_in(jax.random.fold_in(stream_key, 6), axis_at), (parts,), jnp.float32, least / len(shards), top_value / len(shards))
        return jnp.repeat(jnp.exp(steps), shape[axis_at] // parts).reshape((-1,) + (1,) * (len(shape) - axis_at - 1))

    factor_of = one(*shards[0])
    for cut in shards[1:]:
        factor_of = factor_of * one(*cut)
    return factor_of


def profile(count, total, reach, skew):
    weights = [(1 << 20) // math.isqrt(rank ** skew) + 1 for rank in range(2, count + 1)]
    surplus, given = total - reach - (count - 1), [1] * (count - 1)
    while surplus > 0:
        free = [i for i in range(count - 1) if given[i] < reach]
        mass, budget = sum([weights[i] for i in free]), surplus
        for i in free:
            extra = min(reach - given[i], max(1, budget * weights[i] // mass), surplus)
            given[i] = given[i] + extra
            surplus = surplus - extra
    return np.array([reach] + given)


def uneven(stream_key, amount, total, most, slope):
    if amount == 2:
        one = jax.random.randint(stream_key, (), max(1, total - most), min(most, total - 1) + 1)
        return jnp.stack([one, total - one])
    tallies = jnp.asarray(profile(amount, total, most, slope), jnp.int32)
    pairs = (amount - 1) // 2
    source_of, taker = tallies[1:1 + 2 * pairs:2], tallies[2:2 + 2 * pairs:2]
    margin = jnp.minimum(source_of - 1, most - taker)
    shifted = jax.random.randint(jax.random.fold_in(stream_key, 1), (pairs,), 0, 1 << 20) % (margin + 1)
    tallies = tallies.at[1:1 + 2 * pairs:2].set(source_of - shifted).at[2:2 + 2 * pairs:2].set(taker + shifted)
    return tallies[jax.random.permutation(jax.random.fold_in(stream_key, 2), amount)]


def scatter_about(key, dims, scale, most, shards=(), kind=jnp.bfloat16):
    result = jax.random.normal(key, dims, jnp.float32) * scale
    if len(shards) > 0:
        result = levels(key, dims, shards, -0.22, 0.18) * result
    return jnp.clip(result, min=-most, max=most).astype(kind)


def setup_inputs(seed: int = 0) -> dict:
    splits = jax.random.split(jax.random.key(seed), 28)
    return {
        "patches": scatter_about(splits[0], (TOKENS, D), 1.0, 6.0, ((0, 32),)),
        "lengths": jax.vmap(lambda own: uneven(own, IMAGES, GROUP, LONGEST, 2))(jax.random.split(splits[1], N_DP)).reshape((N_DP, IMAGES)).astype(jnp.int32),
        "gsd_scale": jnp.clip(jnp.exp(math.log(4.0) - 2.0794415 * jax.random.uniform(splits[2], (N_DP, IMAGES), jnp.float32) ** levels(splits[2], (N_DP, IMAGES), ((0, 8),), -0.2, 0.2)), 0.5, 4.0),
        "visible": draw_visible(jax.random.fold_in(splits[27], 71), 0),
        "encoder_gain_first": jnp.clip(1.0 + 0.1 * jax.random.normal(splits[4], (D,), jnp.float32), 0.5, 1.5).astype(jnp.bfloat16),
        "encoder_bias_first": scatter_about(splits[5], (D,), 0.2, 1.0, ((0, 8),)),
        "encoder_query": scatter_about(splits[6], (D, D), D ** -0.5, 0.1875, ((0, 8),)),
        "encoder_key": scatter_about(splits[7], (D, D), D ** -0.5, 0.1875, ((0, 8),)),
        "encoder_value": scatter_about(splits[8], (D, D), D ** -0.5, 0.1875, ((0, 8),)),
        "encoder_output": scatter_about(splits[9], (D, D), (D // 8) ** -0.5, 0.5, ((0, 8),)),
        "encoder_gain_second": jnp.clip(1.0 + 0.1 * jax.random.normal(splits[10], (D,), jnp.float32), 0.5, 1.5).astype(jnp.bfloat16),
        "encoder_bias_second": scatter_about(splits[11], (D,), 0.2, 1.0, ((0, 8),)),
        "encoder_up": scatter_about(splits[12], (D, FF), D ** -0.5, 0.1875, ((0, 8),)),
        "encoder_down": scatter_about(splits[13], (FF, D), FF ** -0.5, 0.09375, ((0, 8),)),
        "embed_proj": scatter_about(splits[14], (D, DEC_D), D ** -0.5, 0.1875, ((0, 8),)),
        "mask_token": scatter_about(splits[15], (DEC_D,), 1.0, 6.0, ((0, 8),)),
        "decoder_gain_first": jnp.clip(1.0 + 0.1 * jax.random.normal(splits[16], (DEC_D,), jnp.float32), 0.5, 1.5).astype(jnp.bfloat16),
        "decoder_bias_first": scatter_about(splits[17], (DEC_D,), 0.2, 1.0, ((0, 8),)),
        "decoder_query": scatter_about(splits[18], (DEC_D, DEC_D), DEC_D ** -0.5, 0.25, ((0, 8),)),
        "decoder_key": scatter_about(splits[19], (DEC_D, DEC_D), DEC_D ** -0.5, 0.25, ((0, 8),)),
        "decoder_value": scatter_about(splits[20], (DEC_D, DEC_D), DEC_D ** -0.5, 0.25, ((0, 8),)),
        "decoder_output": scatter_about(splits[21], (DEC_D, DEC_D), (DEC_D // 16) ** -0.5, 1.0, ((0, 8),)),
        "decoder_gain_second": jnp.clip(1.0 + 0.1 * jax.random.normal(splits[22], (DEC_D,), jnp.float32), 0.5, 1.5).astype(jnp.bfloat16),
        "decoder_bias_second": scatter_about(splits[23], (DEC_D,), 0.2, 1.0, ((0, 8),)),
        "decoder_up": scatter_about(splits[24], (DEC_D, DEC_FF), DEC_D ** -0.5, 0.25, ((0, 8),)),
        "decoder_down": scatter_about(splits[25], (DEC_FF, DEC_D), DEC_FF ** -0.5, 0.125, ((0, 8),)),
        "cotangent": scatter_about(splits[26], (TOKENS, DEC_D), 1.0, 6.0, ((0, 32),)),
    }


@jax.custom_vjp
def low(v):
    return lax.optimization_barrier(v.astype(jnp.bfloat16)).astype(jnp.float32)

@jax.custom_vjp
def low_back(v):
    return v

def low_keep(v):
    return (low(v), None)

def low_pass(kept, grad):
    return (grad,)

def back_keep(v):
    return (v, None)

def back_low(kept, grad):
    return (low(grad),)
low.defvjp(low_keep, low_pass)
low_back.defvjp(back_keep, back_low)
EPSILON = 1e-06
MASKED_SCORE = -1e+30

def exact_product(left, right):
    return jnp.dot(left, right, precision=lax.Precision.HIGHEST, preferred_element_type=jnp.float32)

def layer_norm(values, gain, shift):
    center = values - lax.optimization_barrier(jnp.mean(values, axis=-1, keepdims=True))
    spread = lax.optimization_barrier(jnp.mean(center * center, axis=-1, keepdims=True))
    return center * lax.rsqrt(spread + EPSILON) * gain + shift

def sincos(scaled, width):
    half_width = width // 2
    frequency = jnp.exp(jnp.arange(half_width, dtype=jnp.float32) * (-math.log(10000.0) / half_width))
    angles = scaled[:, None] * frequency[None, :]
    return jnp.concatenate([jnp.sin(angles), jnp.cos(angles)], axis=1)

def image_layout(lengths_row, gsd_row, positions):
    image_ends = jnp.cumsum(lengths_row).astype(jnp.int32)
    image_starts = image_ends - lengths_row
    image_ids = lax.optimization_barrier(jnp.sum((positions[:, None] >= image_ends[None, :]).astype(jnp.int32), axis=1))
    onehot = image_ids[:, None] == jnp.arange(lengths_row.shape[0], dtype=jnp.int32)[None, :]
    first_row = lax.optimization_barrier(jnp.sum(jnp.where(onehot, image_starts[None, :], 0), axis=1))
    gsd_ratio = lax.optimization_barrier(jnp.sum(jnp.where(onehot, gsd_row[None, :], 0.0), axis=1))
    return (image_ids, (positions - first_row).astype(jnp.float32) * gsd_ratio)

def attend(normed, query_weight, key_weight, value_weight, output_weight, heads, allowed):
    row_count = normed.shape[0]
    lowered = low(normed)
    queries = low_back(low(exact_product(lowered, query_weight))).reshape(row_count, heads, -1)
    key_rows = low_back(low(exact_product(lowered, key_weight))).reshape(row_count, heads, -1)
    values = low_back(low(exact_product(lowered, value_weight))).reshape(row_count, heads, -1)
    scaling = 1.0 / math.sqrt(queries.shape[2])
    scores = jnp.einsum('ihd,jhd->hij', queries, key_rows, precision=lax.Precision.HIGHEST) * scaling
    scores = jnp.where(allowed[None], low_back(scores), MASKED_SCORE)
    largest = lax.optimization_barrier(jnp.max(scores, axis=-1, keepdims=True))
    exponent = jnp.exp(scores - largest)
    softmaxed = low(exponent / lax.optimization_barrier(jnp.sum(exponent, axis=-1, keepdims=True)))
    mixture = jnp.einsum('hij,jhd->ihd', softmaxed, values, precision=lax.Precision.HIGHEST).reshape(row_count, -1)
    return low_back(exact_product(low_back(low(mixture)), output_weight))

def residual_block(residual, params, heads, allowed):
    gain_first, bias_first, query_weight, key_weight, value_weight, output_weight, gain_second, bias_second, up_weight, down_weight = params
    residual = residual + attend(layer_norm(residual, gain_first, bias_first), query_weight, key_weight, value_weight, output_weight, heads, allowed)
    lifted = low(layer_norm(residual, gain_second, bias_second))
    hidden = low(jax.nn.gelu(low_back(exact_product(lifted, up_weight)), approximate=False))
    return residual + low_back(exact_product(hidden, down_weight))

def group_forward(weights, patch_rows, lengths_row, gsd_row, visible_row):
    encoder_params, embed_weight, mask_weight, decoder_params = weights
    positions = jnp.arange(GROUP, dtype=jnp.int32)
    image_ids, scaled = image_layout(lengths_row, gsd_row, positions)
    same_image = image_ids[:, None] == image_ids[None, :]
    allowed = same_image & ((visible_row[None, :] > 0) | (positions[:, None] == positions[None, :]))
    residual = patch_rows + sincos(scaled, D)
    residual = residual_block(residual, encoder_params, HEADS, allowed)
    embedded = low_back(exact_product(low(residual), embed_weight))
    shown_rows = visible_row[:, None] > 0
    start = jnp.where(shown_rows, embedded, mask_weight[None, :]) + sincos(scaled, DEC_D)
    return residual_block(start, decoder_params, DEC_HEADS, same_image)

def reference(patches, lengths, gsd_scale, visible, encoder_gain_first, encoder_bias_first, encoder_query, encoder_key, encoder_value, encoder_output, encoder_gain_second, encoder_bias_second, encoder_up, encoder_down, embed_proj, mask_token, decoder_gain_first, decoder_bias_first, decoder_query, decoder_key, decoder_value, decoder_output, decoder_gain_second, decoder_bias_second, decoder_up, decoder_down, cotangent):
    encoder_params = tuple((matrix.astype(jnp.float32) for matrix in (encoder_gain_first, encoder_bias_first, encoder_query, encoder_key, encoder_value, encoder_output, encoder_gain_second, encoder_bias_second, encoder_up, encoder_down)))
    decoder_params = tuple((matrix.astype(jnp.float32) for matrix in (decoder_gain_first, decoder_bias_first, decoder_query, decoder_key, decoder_value, decoder_output, decoder_gain_second, decoder_bias_second, decoder_up, decoder_down)))
    weights = (encoder_params, embed_proj.astype(jnp.float32), mask_token.astype(jnp.float32), decoder_params)
    inputs = patches.astype(jnp.float32).reshape(N_DP, GROUP, D)

    def forward(weights, inputs):

        def per_group(group_item):
            return group_forward(weights, group_item[0], group_item[1], group_item[2], group_item[3])
        return lax.map(jax.checkpoint(per_group), (inputs, lengths, gsd_scale, visible))
    outputs, pullback = jax.vjp(forward, weights, inputs)
    grad_weights, grad_inputs = pullback(cotangent.astype(jnp.float32).reshape(N_DP, GROUP, DEC_D))
    encoder_grads, embed_grad, mask_grad, decoder_grads = grad_weights
    return (outputs.reshape(TOKENS, DEC_D).astype(jnp.bfloat16), grad_inputs.reshape(TOKENS, D), encoder_grads[0], encoder_grads[1], encoder_grads[2], encoder_grads[3], encoder_grads[4], encoder_grads[5], encoder_grads[6], encoder_grads[7], encoder_grads[8], encoder_grads[9], embed_grad, mask_grad, decoder_grads[0], decoder_grads[1], decoder_grads[2], decoder_grads[3], decoder_grads[4], decoder_grads[5], decoder_grads[6], decoder_grads[7], decoder_grads[8], decoder_grads[9])
```

```python
import math

import jax
import jax.numpy as jnp
from jax import lax
from jax.sharding import PartitionSpec as P

HEADS = 16
EPSILON = 1e-06
MASKED_SCORE = -1e30
F32 = jnp.float32
BF16 = jnp.bfloat16


def dot(left, right):
    return lax.dot_general(left, right, (((1,), (0,)), ((), ())), preferred_element_type=F32)


def dot_t(left, right):
    return lax.dot_general(left, right, (((0,), (0,)), ((), ())), preferred_element_type=F32)


def dot_b(left, right):
    return lax.dot_general(left, right, (((1,), (1,)), ((), ())), preferred_element_type=F32)


def sincos(scaled, width):
    half_width = width // 2
    frequency = jnp.exp(
        jnp.arange(half_width, dtype=F32) * (-math.log(10000.0) / half_width)
    )
    angles = scaled[:, None] * frequency[None, :]
    return jnp.concatenate([jnp.sin(angles), jnp.cos(angles)], axis=1)


def norm_parts(values):
    center = values - jnp.mean(values, axis=-1, keepdims=True)
    spread = jnp.mean(center * center, axis=-1, keepdims=True)
    scale = lax.rsqrt(spread + EPSILON)
    return center * scale, scale


def norm_back(grad, unit, scale, gain):
    grad_gain = jnp.sum(grad * unit, axis=0, keepdims=True)
    grad_bias = jnp.sum(grad, axis=0, keepdims=True)
    inner = grad * gain
    mean_inner = jnp.mean(inner, axis=-1, keepdims=True)
    mean_cross = jnp.mean(inner * unit, axis=-1, keepdims=True)
    return scale * (inner - mean_inner - unit * mean_cross), grad_gain, grad_bias


def gelu_both(upper):
    phi = 0.5 * (1.0 + lax.erf(upper * math.sqrt(0.5)))
    density = jnp.exp(-0.5 * upper * upper) * (1.0 / math.sqrt(2.0 * math.pi))
    return upper * phi, phi + upper * density


def head_forward(queries, key_rows, values, allowed, scaling):
    scores = jnp.where(allowed, dot_b(queries, key_rows) * scaling, MASKED_SCORE)
    largest = jnp.max(scores, axis=-1, keepdims=True)
    exponent = jnp.exp(scores - largest)
    softmaxed = exponent / jnp.sum(exponent, axis=-1, keepdims=True)
    return softmaxed, dot(softmaxed.astype(BF16), values).astype(BF16)


def head_backward(queries, key_rows, values, softmaxed, grad_mixture, scaling):
    grad_values = dot_t(softmaxed.astype(BF16), grad_mixture).astype(BF16)
    grad_probs = dot_b(grad_mixture, values)
    delta = jnp.sum(softmaxed * grad_probs, axis=-1, keepdims=True)
    grad_scores = (softmaxed * (grad_probs - delta)).astype(BF16)
    grad_queries = (dot(grad_scores, key_rows) * scaling).astype(BF16)
    grad_keys = (dot_t(grad_scores, queries) * scaling).astype(BF16)
    return grad_queries, grad_keys, grad_values


def block_forward(residual, params, heads, allowed, total):
    gain_a, bias_a, w_query, w_key, w_value, w_out, gain_b, bias_b, w_up, w_down = params
    unit_a, scale_a = norm_parts(residual)
    normed = (unit_a * gain_a + bias_a).astype(BF16)
    queries = dot(normed, w_query).astype(BF16)
    key_rows = dot(normed, w_key).astype(BF16)
    values = dot(normed, w_value).astype(BF16)
    size = queries.shape[1] // heads
    scaling = 1.0 / math.sqrt(size)
    probs, mixed = [], []
    for head in range(heads):
        part = slice(head * size, (head + 1) * size)
        softmaxed, mixture = head_forward(
            queries[:, part], key_rows[:, part], values[:, part], allowed, scaling
        )
        probs.append(softmaxed)
        mixed.append(mixture)
    mixture = jnp.concatenate(mixed, axis=1)
    middle = residual + total(dot(mixture, w_out))
    unit_b, scale_b = norm_parts(middle)
    lifted = (unit_b * gain_b + bias_b).astype(BF16)
    hidden, slope = gelu_both(dot(lifted, w_up))
    hidden = hidden.astype(BF16)
    result = middle + total(dot(hidden, w_down))
    return result, (
        unit_a, scale_a, normed, queries, key_rows, values, probs, mixture,
        unit_b, scale_b, lifted, slope, hidden,
    )


def block_backward(grad_result, params, heads, saved, total):
    gain_a, bias_a, w_query, w_key, w_value, w_out, gain_b, bias_b, w_up, w_down = params
    (unit_a, scale_a, normed, queries, key_rows, values, probs, mixture,
     unit_b, scale_b, lifted, slope, hidden) = saved
    size = queries.shape[1] // heads
    scaling = 1.0 / math.sqrt(size)
    grad_branch = grad_result.astype(BF16)
    grad_down = dot_t(hidden, grad_branch)
    grad_upper = (dot_b(grad_branch, w_down) * slope).astype(BF16)
    grad_up = dot_t(lifted, grad_upper)
    grad_lifted = total(dot_b(grad_upper, w_up))
    grad_in, grad_gain_b, grad_bias_b = norm_back(grad_lifted, unit_b, scale_b, gain_b)
    grad_middle = grad_result + grad_in
    grad_attention = grad_middle.astype(BF16)
    grad_out = dot_t(mixture, grad_attention)
    grad_mixture = dot_b(grad_attention, w_out).astype(BF16)
    pieces = []
    for head in range(heads):
        part = slice(head * size, (head + 1) * size)
        pieces.append(
            head_backward(
                queries[:, part], key_rows[:, part], values[:, part], probs[head],
                grad_mixture[:, part], scaling,
            )
        )
    grad_queries, grad_keys, grad_values = (
        jnp.concatenate([piece[at] for piece in pieces], axis=1) for at in range(3)
    )
    grad_normed = total(
        dot_b(grad_queries, w_query) + dot_b(grad_keys, w_key) + dot_b(grad_values, w_value)
    )
    grad_in, grad_gain_a, grad_bias_a = norm_back(grad_normed, unit_a, scale_a, gain_a)
    return grad_middle + grad_in, (
        grad_gain_a, grad_bias_a, dot_t(normed, grad_queries), dot_t(normed, grad_keys),
        dot_t(normed, grad_values), grad_out, grad_gain_b, grad_bias_b, grad_up, grad_down,
    )


def layout(lengths_row, gsd_row, visible_row):
    count = visible_row.shape[0]
    positions = jnp.arange(count, dtype=jnp.int32)
    image_ends = jnp.cumsum(lengths_row)
    image_starts = image_ends - lengths_row
    image_ids = jnp.sum((positions[:, None] >= image_ends[None, :]).astype(jnp.int32), axis=1)
    onehot = image_ids[:, None] == jnp.arange(lengths_row.shape[0], dtype=jnp.int32)[None, :]
    first_row = jnp.sum(jnp.where(onehot, image_starts[None, :], 0), axis=1)
    ratio = jnp.sum(jnp.where(onehot, gsd_row[None, :], 0.0), axis=1)
    scaled = (positions - first_row).astype(F32) * ratio
    shown = visible_row > 0
    earlier = (positions[None, :] <= positions[:, None]) & shown[None, :]
    rank = jnp.where(shown, jnp.sum(earlier.astype(jnp.int32), axis=1) - 1, -1)
    return image_ids, scaled, rank


def spread_rows(grad, rank, offset, rows):
    own = lax.dynamic_slice_in_dim(rank, offset, rows)
    place = (own[:, None] == jnp.arange(grad.shape[0], dtype=jnp.int32)[None, :]).astype(BF16)
    high = grad.astype(BF16)
    low = (grad - high.astype(F32)).astype(BF16)
    return dot(place, high) + dot(place, low)


SHOWN = 128


def local(*arguments):
    patches, lengths, gsd_scale, visible = arguments[:4]
    encoder_shards = arguments[4:14]
    embed_shard, mask_shard = arguments[14:16]
    decoder_shards = arguments[16:26]
    cotangent = arguments[26]
    dp_count = lax.axis_size("dp")
    blk_count = lax.axis_size("blk")
    blk = lax.axis_index("blk")
    dp = lax.axis_index("dp")
    rows = patches.shape[0]
    offset = blk * rows
    heads = HEADS // blk_count
    image_ids, scaled, rank = layout(lengths[0], gsd_scale[0], visible[0])
    shown = rank >= 0
    places = rank[None, :] == jnp.arange(SHOWN, dtype=jnp.int32)[:, None]
    packed_ids = jnp.sum(jnp.where(places, image_ids[None, :], 0), axis=1)
    packed_scaled = jnp.sum(jnp.where(places, scaled[None, :], 0.0), axis=1)

    def gather(shard):
        return lax.all_gather(shard, "dp", axis=0, tiled=True)

    def by_columns(shard):
        width = shard.shape[1] // blk_count
        return gather(lax.dynamic_slice_in_dim(shard, blk * width, width, axis=1))

    def by_rows(shard):
        whole = gather(shard)
        height = whole.shape[0] // blk_count
        return lax.dynamic_slice_in_dim(whole, blk * height, height, axis=0)

    def vector(shard):
        return gather(shard).astype(F32)[None, :]

    def load(shards):
        kinds = (vector, vector, by_columns, by_columns, by_columns, by_rows,
                 vector, vector, by_columns, by_rows)
        return tuple(kind(shard) for kind, shard in zip(kinds, shards))

    def total(partial):
        return lax.psum(partial, "blk")

    def sum_columns(grad):
        summed = lax.psum_scatter(grad.astype(BF16), "dp", scatter_dimension=0, tiled=True)
        return lax.all_gather(summed, "blk", axis=1, tiled=True).astype(F32)

    def sum_rows(grad):
        whole = lax.all_gather(grad.astype(BF16), "blk", axis=0, tiled=True)
        return lax.psum_scatter(whole, "dp", scatter_dimension=0, tiled=True).astype(F32)

    def sum_vector(grad):
        return lax.psum_scatter(grad[0], "dp", scatter_dimension=0, tiled=True)

    def reduce(grads):
        kinds = (sum_vector, sum_vector, sum_columns, sum_columns, sum_columns, sum_rows,
                 sum_vector, sum_vector, sum_columns, sum_rows)
        return tuple(kind(grad) for kind, grad in zip(kinds, grads))

    group = lax.all_gather(patches, "blk", axis=0, tiled=True)
    picked = dot(places.astype(BF16), group)
    encoder = load(encoder_shards)
    residual = picked + sincos(packed_scaled, patches.shape[1])
    encoded, encoder_saved = block_forward(
        residual, encoder, heads, packed_ids[:, None] == packed_ids[None, :], total
    )
    embed = gather(embed_shard)
    lowered = encoded.astype(BF16)
    embedded = dot(lowered, embed)
    high = embedded.astype(BF16)
    low = (embedded - high.astype(F32)).astype(BF16)
    places_b = places.astype(BF16)
    start = jnp.where(
        shown[:, None], dot_t(places_b, high) + dot_t(places_b, low), vector(mask_shard)
    ) + sincos(scaled, embed.shape[1])
    decoder = load(decoder_shards)
    decoded, decoder_saved = block_forward(
        start, decoder, heads, image_ids[:, None] == image_ids[None, :], total
    )
    decoded_rows = lax.dynamic_slice_in_dim(decoded, offset, rows).astype(BF16)
    grad_out = lax.all_gather(cotangent, "blk", axis=0, tiled=True).astype(F32)
    grad_start, decoder_grads = block_backward(grad_out, decoder, heads, decoder_saved, total)
    grad_mask = jnp.sum(jnp.where(shown[:, None], 0.0, grad_start), axis=0, keepdims=True)
    grad_embedded = dot(places_b, grad_start.astype(BF16)).astype(BF16)
    width = embed.shape[1] // blk_count
    grad_embed = dot_t(
        lowered, lax.dynamic_slice_in_dim(grad_embedded, blk * width, width, axis=1)
    )
    grad_encoded = dot_b(grad_embedded, embed)
    grad_residual, encoder_grads = block_backward(
        grad_encoded, encoder, heads, encoder_saved, total
    )
    grad_patches = spread_rows(grad_residual, rank, offset, rows)
    return (
        (decoded_rows, grad_patches) + reduce(encoder_grads)
        + (sum_columns(grad_embed), sum_vector(grad_mask)) + reduce(decoder_grads)
    )


def solution(mesh):
    both, vec, mat = P(("dp", "blk"), None), P("dp"), P("dp", None)
    block = (vec, vec, mat, mat, mat, mat, vec, vec, mat, mat)
    in_specs = (both, mat, mat, mat) + block + (mat, vec) + block + (both,)
    out_specs = (both, both) + block + (mat, vec) + block
    return jax.shard_map(local, mesh=mesh, in_specs=in_specs, out_specs=out_specs, check_vma=False)
```

```python
import functools
import math

import jax
import jax.numpy as jnp
from jax import lax
from jax.experimental import pallas as pl
from jax.experimental.pallas import tpu as pltpu
from jax.sharding import PartitionSpec as P

HEADS = 16
EPSILON = 1e-06
MASKED_SCORE = -1e30
F32 = jnp.float32
BF16 = jnp.bfloat16


def dot(left, right):
    return lax.dot_general(left, right, (((1,), (0,)), ((), ())), preferred_element_type=F32)


def dot_t(left, right):
    return lax.dot_general(left, right, (((0,), (0,)), ((), ())), preferred_element_type=F32)


def dot_b(left, right):
    return lax.dot_general(left, right, (((1,), (1,)), ((), ())), preferred_element_type=F32)


def sincos(scaled, width):
    half_width = width // 2
    frequency = jnp.exp(
        jnp.arange(half_width, dtype=F32) * (-math.log(10000.0) / half_width)
    )
    angles = scaled[:, None] * frequency[None, :]
    return jnp.concatenate([jnp.sin(angles), jnp.cos(angles)], axis=1)


def norm_parts(values):
    center = values - jnp.mean(values, axis=-1, keepdims=True)
    spread = jnp.mean(center * center, axis=-1, keepdims=True)
    scale = lax.rsqrt(spread + EPSILON)
    return center * scale, scale


def norm_back(grad, unit, scale, gain):
    grad_gain = jnp.sum(grad * unit, axis=0, keepdims=True)
    grad_bias = jnp.sum(grad, axis=0, keepdims=True)
    inner = grad * gain
    mean_inner = jnp.mean(inner, axis=-1, keepdims=True)
    mean_cross = jnp.mean(inner * unit, axis=-1, keepdims=True)
    return scale * (inner - mean_inner - unit * mean_cross), grad_gain, grad_bias


def gelu_both(upper):
    phi = 0.5 * (1.0 + lax.erf(upper * math.sqrt(0.5)))
    density = jnp.exp(-0.5 * upper * upper) * (1.0 / math.sqrt(2.0 * math.pi))
    return upper * phi, phi + upper * density


def head_forward(queries, key_rows, values, allowed, scaling):
    scores = jnp.where(allowed, dot_b(queries, key_rows) * scaling, MASKED_SCORE)
    largest = jnp.max(scores, axis=-1, keepdims=True)
    exponent = jnp.exp(scores - largest)
    softmaxed = exponent / jnp.sum(exponent, axis=-1, keepdims=True)
    return softmaxed, dot(softmaxed.astype(BF16), values).astype(BF16)


def head_backward(queries, key_rows, values, softmaxed, grad_mixture, scaling):
    grad_values = dot_t(softmaxed.astype(BF16), grad_mixture).astype(BF16)
    grad_probs = dot_b(grad_mixture, values)
    delta = jnp.sum(softmaxed * grad_probs, axis=-1, keepdims=True)
    grad_scores = (softmaxed * (grad_probs - delta)).astype(BF16)
    grad_queries = (dot(grad_scores, key_rows) * scaling).astype(BF16)
    grad_keys = (dot_t(grad_scores, queries) * scaling).astype(BF16)
    return grad_queries, grad_keys, grad_values


def block_forward(residual, params, heads, allowed, total):
    gain_a, bias_a, w_query, w_key, w_value, w_out, gain_b, bias_b, w_up, w_down = params
    unit_a, scale_a = norm_parts(residual)
    normed = (unit_a * gain_a + bias_a).astype(BF16)
    queries = dot(normed, w_query).astype(BF16)
    key_rows = dot(normed, w_key).astype(BF16)
    values = dot(normed, w_value).astype(BF16)
    size = queries.shape[1] // heads
    scaling = 1.0 / math.sqrt(size)
    probs, mixed = [], []
    for head in range(heads):
        part = slice(head * size, (head + 1) * size)
        softmaxed, mixture = head_forward(
            queries[:, part], key_rows[:, part], values[:, part], allowed, scaling
        )
        probs.append(softmaxed)
        mixed.append(mixture)
    mixture = jnp.concatenate(mixed, axis=1)
    middle = residual + total(dot(mixture, w_out))
    unit_b, scale_b = norm_parts(middle)
    lifted = (unit_b * gain_b + bias_b).astype(BF16)
    hidden, slope = gelu_both(dot(lifted, w_up))
    hidden = hidden.astype(BF16)
    result = middle + total(dot(hidden, w_down))
    return result, (
        unit_a, scale_a, normed, queries, key_rows, values, probs, mixture,
        unit_b, scale_b, lifted, slope, hidden,
    )


def block_backward(grad_result, params, heads, saved, total):
    gain_a, bias_a, w_query, w_key, w_value, w_out, gain_b, bias_b, w_up, w_down = params
    (unit_a, scale_a, normed, queries, key_rows, values, probs, mixture,
     unit_b, scale_b, lifted, slope, hidden) = saved
    size = queries.shape[1] // heads
    scaling = 1.0 / math.sqrt(size)
    grad_branch = grad_result.astype(BF16)
    grad_down = dot_t(hidden, grad_branch)
    grad_upper = (dot_b(grad_branch, w_down) * slope).astype(BF16)
    grad_up = dot_t(lifted, grad_upper)
    grad_lifted = total(dot_b(grad_upper, w_up))
    grad_in, grad_gain_b, grad_bias_b = norm_back(grad_lifted, unit_b, scale_b, gain_b)
    grad_middle = grad_result + grad_in
    grad_attention = grad_middle.astype(BF16)
    grad_out = dot_t(mixture, grad_attention)
    grad_mixture = dot_b(grad_attention, w_out).astype(BF16)
    pieces = []
    for head in range(heads):
        part = slice(head * size, (head + 1) * size)
        pieces.append(
            head_backward(
                queries[:, part], key_rows[:, part], values[:, part], probs[head],
                grad_mixture[:, part], scaling,
            )
        )
    grad_queries, grad_keys, grad_values = (
        jnp.concatenate([piece[at] for piece in pieces], axis=1) for at in range(3)
    )
    grad_normed = total(
        dot_b(grad_queries, w_query) + dot_b(grad_keys, w_key) + dot_b(grad_values, w_value)
    )
    grad_in, grad_gain_a, grad_bias_a = norm_back(grad_normed, unit_a, scale_a, gain_a)
    return grad_middle + grad_in, (
        grad_gain_a, grad_bias_a, dot_t(normed, grad_queries), dot_t(normed, grad_keys),
        dot_t(normed, grad_values), grad_out, grad_gain_b, grad_bias_b, grad_up, grad_down,
    )


def layout(lengths_row, gsd_row, visible_row):
    count = visible_row.shape[0]
    positions = jnp.arange(count, dtype=jnp.int32)
    image_ends = jnp.cumsum(lengths_row)
    image_starts = image_ends - lengths_row
    image_ids = jnp.sum((positions[:, None] >= image_ends[None, :]).astype(jnp.int32), axis=1)
    onehot = image_ids[:, None] == jnp.arange(lengths_row.shape[0], dtype=jnp.int32)[None, :]
    first_row = jnp.sum(jnp.where(onehot, image_starts[None, :], 0), axis=1)
    ratio = jnp.sum(jnp.where(onehot, gsd_row[None, :], 0.0), axis=1)
    scaled = (positions - first_row).astype(F32) * ratio
    shown = visible_row > 0
    earlier = (positions[None, :] <= positions[:, None]) & shown[None, :]
    rank = jnp.where(shown, jnp.sum(earlier.astype(jnp.int32), axis=1) - 1, -1)
    return image_ids, scaled, rank


def spread_rows(grad, rank, offset, rows):
    own = lax.dynamic_slice_in_dim(rank, offset, rows)
    place = (own[:, None] == jnp.arange(grad.shape[0], dtype=jnp.int32)[None, :]).astype(BF16)
    high = grad.astype(BF16)
    low = (grad - high.astype(F32)).astype(BF16)
    return dot(place, high) + dot(place, low)


SHOWN = 128


def local(*arguments):
    patches, lengths, gsd_scale, visible = arguments[:4]
    encoder_shards = arguments[4:14]
    embed_shard, mask_shard = arguments[14:16]
    decoder_shards = arguments[16:26]
    cotangent = arguments[26]
    dp_count = lax.axis_size("dp")
    blk_count = lax.axis_size("blk")
    blk = lax.axis_index("blk")
    dp = lax.axis_index("dp")
    rows = patches.shape[0]
    offset = blk * rows
    heads = HEADS // blk_count
    image_ids, scaled, rank = layout(lengths[0], gsd_scale[0], visible[0])
    shown = rank >= 0
    places = rank[None, :] == jnp.arange(SHOWN, dtype=jnp.int32)[:, None]
    packed_ids = jnp.sum(jnp.where(places, image_ids[None, :], 0), axis=1)
    packed_scaled = jnp.sum(jnp.where(places, scaled[None, :], 0.0), axis=1)

    def gather(shard):
        return lax.all_gather(shard, "dp", axis=0, tiled=True)

    def by_columns(shard):
        width = shard.shape[1] // blk_count
        return gather(lax.dynamic_slice_in_dim(shard, blk * width, width, axis=1))

    def by_rows(shard):
        whole = gather(shard)
        height = whole.shape[0] // blk_count
        return lax.dynamic_slice_in_dim(whole, blk * height, height, axis=0)

    def vector(shard):
        return gather(shard).astype(F32)[None, :]

    def load(shards):
        kinds = (vector, vector, by_columns, by_columns, by_columns, by_rows,
                 vector, vector, by_columns, by_rows)
        return tuple(kind(shard) for kind, shard in zip(kinds, shards))

    def total(partial):
        return lax.psum(partial, "blk")

    def sum_columns(grad):
        summed = lax.psum_scatter(grad.astype(BF16), "dp", scatter_dimension=0, tiled=True)
        return lax.all_gather(summed, "blk", axis=1, tiled=True).astype(F32)

    def sum_rows(grad):
        whole = lax.all_gather(grad.astype(BF16), "blk", axis=0, tiled=True)
        return lax.psum_scatter(whole, "dp", scatter_dimension=0, tiled=True).astype(F32)

    def sum_vector(grad):
        return lax.psum_scatter(grad[0], "dp", scatter_dimension=0, tiled=True)

    def reduce(grads):
        kinds = (sum_vector, sum_vector, sum_columns, sum_columns, sum_columns, sum_rows,
                 sum_vector, sum_vector, sum_columns, sum_rows)
        return tuple(kind(grad) for kind, grad in zip(kinds, grads))

    group = lax.all_gather(patches, "blk", axis=0, tiled=True)
    picked = dot(places.astype(BF16), group)
    encoder = load(encoder_shards)
    residual = picked + sincos(packed_scaled, patches.shape[1])
    encoded, encoder_saved = block_forward(
        residual, encoder, heads, packed_ids[:, None] == packed_ids[None, :], total
    )
    embed = gather(embed_shard)
    lowered = encoded.astype(BF16)
    embedded = dot(lowered, embed)
    high = embedded.astype(BF16)
    low = (embedded - high.astype(F32)).astype(BF16)
    places_b = places.astype(BF16)
    start = jnp.where(
        shown[:, None], dot_t(places_b, high) + dot_t(places_b, low), vector(mask_shard)
    ) + sincos(scaled, embed.shape[1])
    decoder = load(decoder_shards)
    decoded, decoder_saved = block_forward(
        start, decoder, heads, image_ids[:, None] == image_ids[None, :], total
    )
    decoded_rows = lax.dynamic_slice_in_dim(decoded, offset, rows).astype(BF16)
    grad_out = lax.all_gather(cotangent, "blk", axis=0, tiled=True).astype(F32)
    grad_start, decoder_grads = block_backward(grad_out, decoder, heads, decoder_saved, total)
    grad_mask = jnp.sum(jnp.where(shown[:, None], 0.0, grad_start), axis=0, keepdims=True)
    grad_embedded = dot(places_b, grad_start.astype(BF16)).astype(BF16)
    width = embed.shape[1] // blk_count
    grad_embed = dot_t(
        lowered, lax.dynamic_slice_in_dim(grad_embedded, blk * width, width, axis=1)
    )
    grad_encoded = dot_b(grad_embedded, embed)
    grad_residual, encoder_grads = block_backward(
        grad_encoded, encoder, heads, encoder_saved, total
    )
    grad_patches = spread_rows(grad_residual, rank, offset, rows)
    return (
        (decoded_rows, grad_patches) + reduce(encoder_grads)
        + (sum_columns(grad_embed), sum_vector(grad_mask)) + reduce(decoder_grads)
    )


MIB = 2**20
DECODER_ROWS = 512
PARTS = 4
SIDES = 2
VECTORS = 16


class Split:
    def __init__(self):
        self.dp = lax.axis_index("dp")
        self.blk = lax.axis_index("blk")
        self.z = lax.div(self.dp, 2)
        self.y = lax.rem(self.dp, 2)
        self.x = lax.div(self.blk, 2)
        self.core = lax.rem(self.blk, 2)
        self.part = lax.rem(3 * self.blk, PARTS)
        self.y_peer = (self.z * 2 + 1 - self.y, self.blk)
        self.core_peer = (self.dp, self.x * 2 + 1 - self.core)
        self.x_peer = (self.dp, (1 - self.x) * 2 + self.core)
        self.far_peer = (self.dp, (1 - self.x) * 2 + 1 - self.core)
        self.blk_peers = (self.core_peer, self.x_peer, self.far_peer)

    def ahead(self, step):
        return lax.rem(self.z + step, PARTS)

    def behind(self, step):
        return lax.rem(self.z + PARTS - step, PARTS)

    def z_peer(self, step):
        return (self.ahead(step) * 2 + self.y, self.blk)


def remote(source, target, sent, received, device):
    return pltpu.make_async_remote_copy(
        src_ref=source, dst_ref=target, send_sem=sent, recv_sem=received,
        device_id=device, device_id_type=pl.DeviceIdType.MESH,
    )


def span(at, size):
    return pl.ds(pl.multiple_of(at, size), size)


class Columns:
    def __init__(self, split, whole, rows, local, sems, columns=None):
        self.split, self.whole, self.rows, self.local = split, whole, rows, local
        self.columns = columns
        self.z_sent, self.z_got, self.y_sent, self.y_got = sems

    def block(self, z, y):
        rows = span((z * 2 + y) * self.rows, self.rows)
        if self.columns is None:
            return self.whole.at[rows]
        return self.whole.at[rows, self.columns]

    def own(self):
        return self.block(self.split.z, self.split.y)

    def z_copy(self, step):
        s = self.split
        return remote(self.own(), self.own(), self.z_sent.at[step - 1],
                      self.z_got.at[step - 1], s.z_peer(step))

    def z_arrival(self, step):
        s = self.split
        block = self.block(s.behind(step), s.y)
        return remote(block, block, self.z_sent.at[step - 1], self.z_got.at[step - 1],
                      s.z_peer(step))

    def y_copy(self, step):
        s = self.split
        block = self.block(s.behind(step), s.y)
        return remote(block, block, self.y_sent.at[step], self.y_got.at[step], s.y_peer)

    def y_arrival(self, step):
        s = self.split
        block = self.block(s.behind(step), 1 - s.y)
        return remote(block, block, self.y_sent.at[step], self.y_got.at[step], s.y_peer)

    def fetch(self):
        for copy in self.local:
            copy.start()

    def send(self):
        for copy in self.local:
            copy.wait()
        for step in (1, 2, 3):
            self.z_copy(step).start()
        self.y_copy(0).start()

    def forward(self):
        for step in (1, 2, 3):
            self.z_arrival(step).wait_recv()
            self.y_copy(step).start()

    def finish(self):
        for step in range(PARTS):
            self.y_arrival(step).wait_recv()

    def drain(self):
        for step in (1, 2, 3):
            self.z_copy(step).wait_send()
        for step in range(PARTS):
            self.y_copy(step).wait_send()


class Rows:
    def __init__(self, split, whole, rows, local, sems):
        self.split, self.whole, self.rows, self.local = split, whole, rows, local
        self.z_sent, self.z_got, self.y_sent, self.y_got = sems

    def block(self, y):
        return self.whole.at[span(y * self.rows, self.rows)]

    def z_copy(self, step):
        s = self.split
        return remote(self.block(s.y), self.block(s.y), self.z_sent.at[step - 1],
                      self.z_got.at[0], s.z_peer(step))

    def y_copy(self):
        s = self.split
        return remote(self.block(s.y), self.block(s.y), self.y_sent.at[0],
                      self.y_got.at[0], s.y_peer)

    def fetch(self):
        @pl.when(self.split.z == self.split.part)
        def _():
            self.local.start()

    def send(self):
        @pl.when(self.split.z == self.split.part)
        def _():
            self.local.wait()
            for step in (1, 2, 3):
                self.z_copy(step).start()

    def forward(self):
        @pl.when(self.split.z != self.split.part)
        def _():
            self.z_copy(1).wait_recv()
        self.y_copy().start()

    def finish(self):
        s = self.split
        block = self.block(1 - s.y)
        remote(block, block, self.y_sent.at[0], self.y_got.at[0], s.y_peer).wait_recv()

    def drain(self):
        @pl.when(self.split.z == self.split.part)
        def _():
            for step in (1, 2, 3):
                self.z_copy(step).wait_send()
        self.y_copy().wait_send()


def each(count, step, body):
    @pl.loop(0, count // step)
    def _(at):
        body(pl.ds(pl.multiple_of(at * step, step), step))


class ColumnSum:
    def __init__(self, split, grad, met, came, done, sems, step):
        self.split, self.grad, self.met, self.came, self.done = split, grad, met, came, done
        self.y_sent, self.y_got, self.z_sent, self.z_got, self.b_sent, self.b_got = sems
        self.step = step

    def y_copy(self):
        s = self.split
        return remote(self.grad.at[:, 1 - s.y], self.met, self.y_sent, self.y_got, s.y_peer)

    def z_copy(self, step):
        s = self.split
        return remote(self.met.at[s.ahead(step)], self.came.at[step - 1],
                      self.z_sent.at[step - 1], self.z_got.at[step - 1], s.z_peer(step))

    def b_copy(self, which):
        s = self.split
        block = self.done.at[s.blk]
        return remote(block, block, self.b_sent.at[which], self.b_got.at[which],
                      s.blk_peers[which])

    def b_arrival(self, which):
        s = self.split
        block = self.done.at[s.blk_peers[which][1]]
        return remote(block, block, self.b_sent.at[which], self.b_got.at[which],
                      s.blk_peers[which])

    def start(self):
        self.y_copy().start()

    def add(self, z):
        def body(rows):
            both = self.grad[z, self.split.y, rows].astype(F32) + self.met[z, rows].astype(F32)
            self.met[z, rows] = both.astype(self.met.dtype)
        each(self.met.shape[1], self.step, body)

    def middle(self):
        self.y_copy().wait_recv()
        for step in (1, 2, 3):
            self.add(self.split.ahead(step))
            self.z_copy(step).start()

    def total(self, store):
        s = self.split
        for step in (1, 2, 3):
            self.z_copy(step).wait_recv()

        def body(rows):
            whole = self.grad[s.z, s.y, rows].astype(F32) + self.met[s.z, rows].astype(F32)
            for step in range(3):
                whole = whole + self.came[step, rows].astype(F32)
            store(rows, whole)
        each(self.met.shape[1], self.step, body)

    def last(self):
        def store(rows, whole):
            self.done[self.split.blk, rows] = whole.astype(self.done.dtype)
        self.total(store)
        for which in range(3):
            self.b_copy(which).start()

    def close(self):
        for which in range(3):
            self.b_arrival(which).wait_recv()
        for which in range(3):
            self.b_copy(which).wait_send()
        self.drain()

    def drain(self):
        self.y_copy().wait_send()
        for step in (1, 2, 3):
            self.z_copy(step).wait_send()


class RowSum:
    def __init__(self, split, grad, met, came, done, sems, step):
        self.split, self.grad, self.met, self.came, self.done = split, grad, met, came, done
        self.y_sent, self.y_got, self.z_sent, self.z_got, self.b_sent, self.b_got = sems
        self.step = step
        s = split
        self.slot = lax.rem(s.part + PARTS - s.z + 3, PARTS)
        self.home = (s.part * 2 + s.y, s.blk)

    def y_copy(self):
        s = self.split
        return remote(self.grad.at[1 - s.y], self.met, self.y_sent, self.y_got, s.y_peer)

    def z_copy(self):
        return remote(self.met, self.came.at[self.slot], self.z_sent.at[0],
                      self.z_got.at[self.slot], self.home)

    def b_copy(self, which):
        return remote(self.done, self.done, self.b_sent.at[which], self.b_got.at[0],
                      self.split.blk_peers[which])

    def start(self):
        self.y_copy().start()

    def middle(self):
        s = self.split
        self.y_copy().wait_recv()

        @pl.when(s.z != s.part)
        def _():
            def body(rows):
                both = self.grad[s.y, rows].astype(F32) + self.met[rows].astype(F32)
                self.met[rows] = both.astype(self.met.dtype)
            each(self.met.shape[0], self.step, body)
            self.z_copy().start()

    def last(self):
        s = self.split

        @pl.when(s.z == s.part)
        def _():
            for step in range(3):
                remote(self.met, self.came.at[step], self.z_sent.at[0],
                       self.z_got.at[step], s.y_peer).wait_recv()

            def body(rows):
                whole = self.grad[s.y, rows].astype(F32) + self.met[rows].astype(F32)
                for step in range(3):
                    whole = whole + self.came[step, rows].astype(F32)
                self.done[rows] = whole.astype(self.done.dtype)
            each(self.met.shape[0], self.step, body)
            for which in range(3):
                self.b_copy(which).start()

    def close(self):
        s = self.split
        self.y_copy().wait_send()

        @pl.when(s.z == s.part)
        def _():
            for which in range(3):
                self.b_copy(which).wait_send()

        @pl.when(s.z != s.part)
        def _():
            self.z_copy().wait_send()
            self.b_copy(0).wait_recv()


class Total:
    def __init__(self, split, part, met, out, came, whole, sems, slot):
        self.split, self.part, self.met, self.out = split, part, met, out
        self.came, self.whole = came.at[slot], whole
        self.sent, self.got = sems

    def first_copy(self):
        s = self.split
        return remote(self.part.at[1 - s.core], self.met, self.sent.at[0], self.got.at[0],
                      s.core_peer)

    def second_copy(self):
        return remote(self.out, self.came, self.sent.at[1], self.got.at[1], self.split.x_peer)

    def third_copy(self, half):
        s = self.split
        return remote(self.whole.at[half], self.whole.at[half], self.sent.at[2],
                      self.got.at[2], s.core_peer)

    def start(self):
        self.first_copy().start()

    def middle(self):
        s = self.split
        self.first_copy().wait_recv()

        def body(rows):
            self.out[rows] = (self.part[s.core, rows] + self.met[rows]).astype(BF16)
        each(self.out.shape[0], 32, body)
        self.second_copy().start()

    def end(self):
        s = self.split
        self.second_copy().wait_recv()

        def body(rows):
            self.whole[s.core, rows] = self.out[rows].astype(F32) + self.came[rows].astype(F32)
        each(self.out.shape[0], 32, body)
        self.third_copy(s.core).start()
        self.third_copy(1 - s.core).wait_recv()
        self.first_copy().wait_send()
        self.second_copy().wait_send()
        self.third_copy(s.core).wait_send()


def head_mask(width, size, head):
    lanes = lax.broadcasted_iota(jnp.int32, (1, width), 1)
    return lax.div(lanes, size) == head


def keep(mask, values):
    return jnp.where(mask, values, jnp.zeros_like(values))


class Block:
    def __init__(self, rows, width, heads, size, names, refs, vectors):
        self.rows, self.width, self.heads, self.size = rows, width, heads, size
        self.share = heads * size
        self.scaling = 1.0 / math.sqrt(size)
        self.refs = refs
        self.vectors = vectors
        self.name = names
        self.tile = 32 * 1024 // width

    def ref(self, name):
        return self.refs[self.name + name]

    def row(self, at):
        return self.refs["gains"][self.vectors + at:self.vectors + at + 1, 0:self.width]

    def norm(self, first):
        unit, scale = self.ref("unit_a" if first else "unit_b"), self.ref(
            "scale_a" if first else "scale_b")
        out = self.ref("normed" if first else "lifted")
        gain, bias = self.row(0 if first else 2), self.row(1 if first else 3)
        residual = self.ref("residual")

        def body(rows):
            one, size = norm_parts(residual[rows])
            unit[rows] = one
            scale[rows] = size
            out[rows] = (one * gain + bias).astype(BF16)
        each(self.rows, self.tile, body)

    def project(self):
        normed, mixed, weight = self.ref("normed"), self.ref("qkv"), self.ref("w_qkv")

        def body(rows):
            mixed[rows] = dot(normed[rows], weight[...]).astype(BF16)
        each(self.rows, 128, body)

    def parts(self, rows):
        share, qkv = self.share, self.ref("qkv")
        return (qkv[rows, 0:share], qkv[rows, share:2 * share], qkv[rows, 2 * share:3 * share])

    def attend(self, ids_column, ids_row):
        probs, mixture = self.ref("probs"), self.ref("mixture")
        everything = pl.ds(0, self.rows)

        def body(queries):
            query = self.parts(queries)[0]
            unused, key_rows, values = self.parts(everything)
            allowed = ids_column[...] == ids_row[:, queries]

            def one(head, mixed):
                mask = head_mask(self.share, self.size, head)
                scores = jnp.where(
                    allowed, dot_b(keep(mask, key_rows), query) * self.scaling, MASKED_SCORE
                )
                exponent = jnp.exp(scores - jnp.max(scores, axis=0, keepdims=True))
                softmaxed = exponent * (1.0 / jnp.sum(exponent, axis=0, keepdims=True))
                probs[head, :, queries] = softmaxed
                return mixed + dot_t(keep(mask, values), softmaxed.astype(BF16))

            mixed = lax.fori_loop(0, self.heads, one, jnp.zeros((self.share, 128), F32))
            mixture[queries] = mixed.T.astype(BF16)
        each(self.rows, 128, body)

    def product(self, left, weight, target, back=False):
        shape = target.shape
        half = shape[1]

        def body(rows):
            made = (dot_b if back else dot)(left[rows], weight[...])
            at = lax.div(rows.start, half)
            target[at, pl.ds(pl.multiple_of(lax.rem(rows.start, half), 64), 64)] = made
        each(self.rows, 64, body)

    def half(self, ref, rows):
        size = ref.shape[1]
        start = pl.multiple_of(lax.rem(rows.start, size), rows.size)
        return ref[lax.div(rows.start, size), pl.ds(start, rows.size)]

    def add_total(self, whole):
        residual = self.ref("residual")

        def body(rows):
            residual[rows] = residual[rows] + self.half(whole, rows)
        each(self.rows, self.tile, body)

    def expand(self):
        lifted, weight = self.ref("lifted"), self.ref("w_up")
        hidden, slope = self.ref("hidden"), self.ref("slope")

        def body(rows):
            def inner(columns):
                made, gradient = gelu_both(dot(lifted[rows], weight[:, columns]))
                hidden[rows, columns] = made.astype(BF16)
                slope[rows, columns] = gradient
            each(weight.shape[1], 256, inner)
        each(self.rows, 128, body)

    def back_hidden(self, branch):
        weight, slope, grad = self.ref("w_down"), self.ref("slope"), self.ref("grad_upper")

        def body(rows):
            def inner(columns):
                made = dot_b(branch[rows], weight[columns])
                grad[rows, columns] = (made * slope[rows, columns]).astype(BF16)
            each(weight.shape[0], 256, inner)
        each(self.rows, 128, body)

    def norm_back(self, whole, first, out):
        unit, scale = self.ref("unit_a" if first else "unit_b"), self.ref(
            "scale_a" if first else "scale_b")
        gain, grad = self.row(0 if first else 2), self.ref("grad")

        def body(at, sums):
            rows = pl.ds(pl.multiple_of(at * self.tile, self.tile), self.tile)
            moved, gains, biases = norm_back(self.half(whole, rows), unit[rows], scale[rows], gain)
            new = grad[rows] + moved
            grad[rows] = new
            out[rows] = new.astype(BF16)
            return sums[0] + gains, sums[1] + biases
        zero = jnp.zeros((1, self.width), F32)
        return lax.fori_loop(0, self.rows // self.tile, body, (zero, zero))

    def back_mixture(self, branch):
        weight, grad = self.ref("w_out"), self.ref("grad_mixture")

        def body(rows):
            grad[rows] = dot_b(branch[rows], weight[...]).astype(BF16)
        each(self.rows, 128, body)

    def attend_back(self):
        probs, grad_mixture, grads = self.ref("probs"), self.ref("grad_mixture"), self.ref(
            "grad_qkv")
        key_sum, value_sum = self.ref("key_sum"), self.ref("value_sum")
        share, everything = self.share, pl.ds(0, self.rows)
        key_sum[...] = jnp.zeros(key_sum.shape, F32)
        value_sum[...] = jnp.zeros(value_sum.shape, F32)

        def body(queries):
            query = self.parts(queries)[0]
            unused, key_rows, values = self.parts(everything)
            grad_rows = grad_mixture[queries]

            def one(head, total):
                mask = head_mask(share, self.size, head)
                softmaxed = probs[head, :, queries]
                grad_probs = dot_b(keep(mask, values), grad_rows)
                value_sum[...] += dot(softmaxed.astype(BF16), keep(mask, grad_rows))
                delta = jnp.sum(softmaxed * grad_probs, axis=0, keepdims=True)
                grad_scores = (softmaxed * (grad_probs - delta)).astype(BF16)
                key_sum[...] += dot(grad_scores, keep(mask, query))
                return total + dot_t(keep(mask, key_rows), grad_scores)

            total = lax.fori_loop(0, self.heads, one, jnp.zeros((share, 128), F32))
            grads[queries, 0:share] = (total.T * self.scaling).astype(BF16)
        each(self.rows, 128, body)

        def close(rows):
            grads[rows, share:2 * share] = (key_sum[rows] * self.scaling).astype(BF16)
            grads[rows, 2 * share:3 * share] = value_sum[rows].astype(BF16)
        each(self.rows, 128, close)


def weight_grad(left, right, target):
    if len(target.shape) == 4:
        parts, sides, rows, width = target.shape
        if rows >= 128:
            @pl.loop(0, parts * sides)
            def _(at):
                block = dot_t(left[:, span(at * rows, rows)], right[...])
                target[lax.div(at, sides), lax.rem(at, sides)] = block.astype(BF16)
        else:
            @pl.loop(0, parts)
            def _(at):
                block = dot_t(left[:, span(at * sides * rows, sides * rows)], right[...])
                target[at] = block.reshape(sides, rows, width).astype(BF16)
    else:
        sides, rows, width = target.shape
        if rows >= 128:
            @pl.loop(0, sides)
            def _(at):
                block = dot_t(left[:, span(at * rows, rows)], right[...])
                target[at] = block.astype(BF16)
        else:
            block = dot_t(left[...], right[...])
            target[...] = block.reshape(sides, rows, width).astype(BF16)


def vector_store(target, at, row, whole):
    for owner in range(8):
        block = owner if whole else owner // 2
        target[owner // 2, owner % 2, at:at + 1, :] = row[:, 128 * block:128 * block + 128]


COLUMN_UNITS = ("e_qkv", "e_up", "e_down", "embed", "d_qkv", "d_up")
ROW_UNITS = ("e_out", "d_out", "d_down")
MESSAGES = COLUMN_UNITS + ROW_UNITS


def unit_shapes(width, dec_width, hidden, dec_hidden):
    return {
        "e_qkv": (width // 8, 3 * width // 4),
        "e_up": (width // 8, hidden // 4),
        "e_down": (hidden // 32, width),
        "embed": (width // 8, dec_width // 4),
        "d_qkv": (dec_width // 8, 3 * dec_width // 4),
        "d_up": (dec_width // 8, dec_hidden // 4),
        "e_out": (width // 8, width),
        "d_out": (dec_width // 8, dec_width),
        "d_down": (dec_hidden // 8, dec_width),
    }


def scratch_table(width, dec_width, hidden, dec_hidden, rows, shown):
    units = unit_shapes(width, dec_width, hidden, dec_hidden)
    table = {}
    for name in COLUMN_UNITS:
        height, columns = units[name]
        if name != "embed":
            table["w_" + name] = ((8 * height, columns), BF16)
        table["g_" + name] = ((PARTS, SIDES, height, columns), BF16)
        table["m_" + name] = ((PARTS, height, columns), BF16)
        table["c_" + name] = ((3, height, columns), BF16)
    table["w_embed"] = ((width, dec_width), BF16)
    for name in ROW_UNITS:
        height, columns = units[name]
        table["w_" + name] = ((2 * height, columns), BF16)
        table["g_" + name] = ((SIDES, height, columns), BF16)
        table["m_" + name] = ((height, columns), BF16)
        table["c_" + name] = ((3, height, columns), BF16)
    table["w_vector"] = ((8 * VECTORS, 128), BF16)
    table["g_vector"] = ((PARTS, SIDES, VECTORS, 128), F32)
    table["m_vector"] = ((PARTS, VECTORS, 128), F32)
    table["c_vector"] = ((3, VECTORS, 128), F32)
    table["gains"] = ((VECTORS, width), F32)
    table["group"] = ((rows, width), BF16)
    table["cotangents"] = ((rows, dec_width), BF16)
    for key, count, wide, deep, heads, size in (
        ("e_", shown, width, hidden // 4, 4, 64), ("d_", rows, dec_width, dec_hidden // 4, 4, 32)
    ):
        share = heads * size
        for name, shape, kind in (
            ("residual", (count, wide), F32), ("unit_a", (count, wide), F32),
            ("unit_b", (count, wide), F32), ("scale_a", (count, 1), F32),
            ("scale_b", (count, 1), F32), ("normed", (count, wide), BF16),
            ("lifted", (count, wide), BF16), ("qkv", (count, 3 * share), BF16),
            ("probs", (heads, count, count), F32), ("mixture", (count, share), BF16),
            ("hidden", (count, deep), BF16), ("slope", (count, deep), F32),
            ("grad_upper", (count, deep), BF16), ("grad", (count, wide), F32),
            ("grad_mixture", (count, share), BF16), ("grad_qkv", (count, 3 * share), BF16),
            ("key_sum", (count, share), F32), ("value_sum", (count, share), F32),
            ("branch", (count, wide), BF16),
            ("part", (2, count // 2, wide), F32), ("met", (count // 2, wide), F32),
            ("out", (count // 2, wide), BF16), ("came", (2, count // 2, wide), BF16),
            ("whole", (2, count // 2, wide), F32),
        ):
            table[key + name] = (shape, kind)
    table["last_part"] = ((2, 2, rows // 4, dec_width), F32)
    table["last_met"] = ((2, rows // 4, dec_width), F32)
    table["last_out"] = ((rows // 4, dec_width), BF16)
    table["last_came"] = ((rows // 4, dec_width), BF16)
    table["lowered"] = ((shown, width), BF16)
    table["picked"] = ((shown, dec_width), BF16)
    return table


INPUTS = (
    "rank_row", "rank_column", "ids_row", "ids_column", "packed_row", "packed_column",
    "code", "dec_code", "vector",
    "patches", "cotangent", "query", "key", "value", "out", "up", "down", "embed",
    "dec_query", "dec_key", "dec_value", "dec_out", "dec_up", "dec_down",
)
RESULTS = ("decoded", "grad_patches", "grad_vector") + MESSAGES
SEMAPHORES = {
    "local": (40,),
    "z_sent": (10, 3), "z_got": (10, 3), "y_sent": (10, 4), "y_got": (10, 4),
    "gy_sent": (10,), "gy_got": (10,), "gz_sent": (10, 3), "gz_got": (10, 3),
    "gb_sent": (10, 3), "gb_got": (10, 3),
    "p_sent": (3,), "p_got": (3,), "c_sent": (3,), "c_got": (3,),
    "e_sent": (3,), "e_got": (3,), "t_sent": (8, 3), "t_got": (8, 3),
}


def main_kernel(names, *refs):
    ref = dict(zip(names, refs))
    s = Split()
    shown, width = ref["code"].shape
    rows, dec_width = ref["dec_code"].shape
    own = ref["patches"].shape[0]
    sem = {name: ref["s_" + name] for name in SEMAPHORES}
    counter = [0]

    def local(source, target):
        at = counter[0]
        counter[0] = at + 1
        return pltpu.make_async_copy(source, target, sem["local"].at[at])

    barrier = pltpu.get_barrier_semaphore()
    peers = [s.z_peer(step) for step in (1, 2, 3)] + [s.y_peer] + list(s.blk_peers)
    for peer in peers:
        pl.semaphore_signal(barrier, inc=1, device_id=peer, device_id_type=pl.DeviceIdType.MESH)

    order = ("vector",) + MESSAGES
    units = {}
    for at, name in enumerate(order):
        sems = tuple(sem[kind].at[at] for kind in ("z_sent", "z_got", "y_sent", "y_got"))
        whole = ref["w_" + name]
        if name == "vector":
            copies = [local(ref["vector"], whole.at[span(s.dp * VECTORS, VECTORS)])]
            units[name] = Columns(s, whole, VECTORS, copies, sems)
        elif name in ROW_UNITS:
            source = ref[{"e_out": "out", "d_out": "dec_out", "d_down": "dec_down"}[name]]
            height = source.shape[0]
            copy = local(source, whole.at[span(s.y * height, height)])
            units[name] = Rows(s, whole, height, copy, sems)
        else:
            height = ref["g_" + name].shape[2]
            mine = span(s.dp * height, height)
            columns = None
            if name in ("e_qkv", "d_qkv"):
                kinds = ("query", "key", "value")
                if name == "d_qkv":
                    kinds = ("dec_query", "dec_key", "dec_value")
                size = ref[kinds[0]].shape[1] // PARTS
                copies = [
                    local(ref[kind].at[:, span(s.part * size, size)],
                          whole.at[mine, pl.ds(place * size, size)])
                    for place, kind in enumerate(kinds)
                ]
            elif name == "e_up":
                size = height
                copies = [
                    local(ref["up"].at[:, span((owner * PARTS + s.blk) * size, size)],
                          whole.at[mine, pl.ds(owner * size, size)])
                    for owner in range(8)
                ]
            elif name == "e_down":
                copies = [local(ref["down"].at[span(s.blk * height, height)], whole.at[mine])]
            elif name == "embed":
                size = dec_width // PARTS
                columns = span(s.part * size, size)
                copies = [local(ref["embed"].at[:, columns], whole.at[mine, columns])]
            else:
                size = ref["dec_up"].shape[1] // PARTS
                copies = [local(ref["dec_up"].at[:, span(s.part * size, size)], whole.at[mine])]
            units[name] = Columns(s, whole, height, copies, sems, columns)

    sums = {}
    for at, name in enumerate(order):
        sems = tuple(
            sem[kind].at[at]
            for kind in ("gy_sent", "gy_got", "gz_sent", "gz_got", "gb_sent", "gb_got")
        )
        kind = RowSum if name in ROW_UNITS else ColumnSum
        done = None if name == "vector" else ref["o_" + name]
        wide = ref["g_" + name].shape[-1]
        sums[name] = kind(s, ref["g_" + name], ref["m_" + name], ref["c_" + name], done, sems,
                          16 if wide > 512 else 32 if name != "vector" else 8)

    totals = []
    for at in range(7):
        key, slot = ("e_", at % 2) if at in (0, 1, 5, 6) else ("d_", at % 2)
        totals.append(Total(
            s, *(ref[key + name] for name in ("part", "met", "out", "came", "whole")),
            (sem["t_sent"].at[at], sem["t_got"].at[at]), slot,
        ))

    encoder = Block(shown, width, 4, 64, "e_", ref, 0)
    decoder = Block(rows, dec_width, 4, 32, "d_", ref, 5)
    for block, key in ((encoder, "e_"), (decoder, "d_")):
        for short, long in (("w_qkv", "qkv"), ("w_out", "out"), ("w_up", "up"),
                            ("w_down", "down")):
            ref[key + short] = ref["w_" + key + long]

    first = ("vector", "e_qkv", "e_out", "embed", "e_up")
    for name in first:
        units[name].fetch()
    mine = span(s.blk * own, own)
    own_patches = local(ref["patches"], ref["group"].at[mine])
    own_cotangents = local(ref["cotangent"], ref["cotangents"].at[mine])
    own_patches.start()
    own_cotangents.start()
    for name in ("e_down", "d_qkv", "d_out", "d_up", "d_down"):
        units[name].fetch()

    pl.semaphore_wait(barrier, len(peers))

    def shares(source, target, kind, which):
        return remote(source, target.at[mine], sem[kind + "_sent"].at[which],
                      sem[kind + "_got"].at[which], s.blk_peers[which])

    def shares_arrival(source, target, kind, which):
        place = span(s.blk_peers[which][1] * own, own)
        return remote(source, target.at[place], sem[kind + "_sent"].at[which],
                      sem[kind + "_got"].at[which], s.blk_peers[which])

    for name in ("vector", "e_qkv", "e_out"):
        units[name].send()
    for which in range(3):
        shares(ref["patches"], ref["group"], "p", which).start()
    for name in ("embed", "e_up"):
        units[name].send()
    own_patches.wait()
    for which in range(3):
        shares_arrival(ref["patches"], ref["group"], "p", which).wait_recv()

    places = (
        lax.broadcasted_iota(jnp.int32, (shown, rows), 0) == ref["rank_row"][...]
    ).astype(BF16)
    residual = ref["e_residual"]

    def place_patches(columns):
        residual[:, columns] = dot(places, ref["group"][:, columns]) + ref["code"][:, columns]
    each(width, 256, place_patches)

    units["vector"].forward()
    units["vector"].finish()
    vectors = ref["w_vector"][...].astype(F32)
    gains = ref["gains"]
    for at in range(9):
        for owner in range(8):
            row = vectors[VECTORS * owner + at:VECTORS * owner + at + 1, :]
            if at < 4:
                gains[at:at + 1, 128 * owner:128 * owner + 128] = row
            elif owner % 2 == 0:
                pair = VECTORS * (owner + 1) + at
                gains[at:at + 1, 64 * owner:64 * owner + 128] = row + vectors[pair:pair + 1, :]
    encoder.norm(True)
    for name in ("e_qkv", "e_out", "embed"):
        units[name].forward()
    units["e_qkv"].finish()
    encoder.project()
    encoder.attend(ref["packed_column"], ref["packed_row"])
    units["e_out"].finish()
    encoder.product(ref["e_mixture"], ref["w_e_out"], ref["e_part"])
    totals[0].start()
    units["e_down"].send()
    for which in range(3):
        shares(ref["cotangent"], ref["cotangents"], "c", which).start()
    totals[0].middle()
    units["embed"].finish()
    totals[0].end()
    encoder.add_total(ref["e_whole"])
    encoder.norm(False)
    columns = span(s.part * (dec_width // PARTS), dec_width // PARTS)

    def embed_copy(which):
        block = ref["w_embed"].at[:, columns]
        return remote(block, block, sem["e_sent"].at[which], sem["e_got"].at[which],
                      s.blk_peers[which])

    def embed_arrival(which):
        size = dec_width // PARTS
        place = span(lax.rem(3 * s.blk_peers[which][1], PARTS) * size, size)
        block = ref["w_embed"].at[:, place]
        return remote(block, block, sem["e_sent"].at[which], sem["e_got"].at[which],
                      s.blk_peers[which])

    for which in range(3):
        embed_copy(which).start()
    units["e_up"].forward()
    units["d_qkv"].send()
    units["e_up"].finish()
    encoder.expand()
    units["e_down"].forward()
    for name in ("d_out", "d_up"):
        units[name].send()
    units["e_down"].finish()
    encoder.product(ref["e_hidden"], ref["w_e_down"], ref["e_part"])
    totals[1].start()
    units["d_qkv"].forward()
    totals[1].middle()
    units["d_down"].send()
    units["d_out"].forward()
    for which in range(3):
        embed_arrival(which).wait_recv()
    totals[1].end()
    encoder.add_total(ref["e_whole"])

    lowered = ref["lowered"]

    def lower(part):
        lowered[part] = residual[part].astype(BF16)
    each(shown, 32, lower)
    embedded = dot(lowered[...], ref["w_embed"][...])
    high = embedded.astype(BF16)
    low = (embedded - high.astype(F32)).astype(BF16)
    token = gains[4:5, 0:dec_width]
    start = ref["d_residual"]

    def place_rows(part):
        rank = ref["rank_column"][part]
        here = (lax.broadcasted_iota(jnp.int32, (128, shown), 1) == rank).astype(BF16)
        made = jnp.where(rank >= 0, dot(here, high) + dot(here, low), token)
        start[part] = made + ref["dec_code"][part]
    each(rows, 128, place_rows)
    decoder.norm(True)
    units["d_qkv"].finish()
    decoder.project()
    decoder.attend(ref["ids_column"], ref["ids_row"])
    units["d_up"].forward()
    units["d_out"].finish()
    decoder.product(ref["d_mixture"], ref["w_d_out"], ref["d_part"])
    totals[2].start()
    totals[2].middle()
    units["d_down"].forward()
    totals[2].end()
    decoder.add_total(ref["d_whole"])
    decoder.norm(False)
    units["d_up"].finish()
    decoder.expand()
    units["d_down"].finish()
    quarter = rows // 4
    last_part, last_met = ref["last_part"], ref["last_met"]

    def last_product(part):
        at = lax.div(part.start, 64)
        made = dot(ref["d_hidden"][part], ref["w_d_down"][...])
        per = quarter // 64
        place = pl.ds(pl.multiple_of(lax.rem(at, per) * 64, 64), 64)
        block = lax.div(at, per)
        last_part[lax.div(block, 2), lax.rem(block, 2), place] = made
    each(rows, 64, last_product)
    last_sent, last_got = sem["t_sent"].at[7], sem["t_got"].at[7]
    last_first = remote(last_part.at[:, 1 - s.core], last_met, last_sent.at[0], last_got.at[0],
                        s.core_peer)
    last_second = remote(ref["last_out"], ref["last_came"], last_sent.at[1], last_got.at[1],
                         s.x_peer)
    last_first.start()

    own_cotangents.wait()
    for which in range(3):
        shares_arrival(ref["cotangent"], ref["cotangents"], "c", which).wait_recv()
    cotangents, grad = ref["cotangents"], ref["d_grad"]
    decoder.back_hidden(cotangents)
    decoder.product(ref["d_grad_upper"], ref["w_d_up"], ref["d_part"], back=True)
    totals[3].start()
    last_first.wait_recv()

    def last_add(part):
        made = last_part[1 - s.x, s.core, part] + last_met[1 - s.x, part]
        ref["last_out"][part] = made.astype(BF16)
    each(quarter, 64, last_add)
    totals[3].middle()
    last_second.start()

    def copy_grad(part):
        grad[part] = cotangents[part].astype(F32)
    each(rows, 64, copy_grad)
    weight_grad(ref["d_hidden"], cotangents, ref["g_d_down"])
    sums["d_down"].start()
    weight_grad(ref["d_lifted"], ref["d_grad_upper"], ref["g_d_up"])
    sums["d_up"].start()
    totals[3].end()
    vector_grad = ref["g_vector"]
    vector_grad[...] = jnp.zeros(vector_grad.shape, F32)
    gain, bias = decoder.norm_back(ref["d_whole"], False, ref["d_branch"])
    vector_store(vector_grad, 7, gain, False)
    vector_store(vector_grad, 8, bias, False)
    decoder.back_mixture(ref["d_branch"])
    decoder.attend_back()
    sums["d_down"].middle()
    decoder.product(ref["d_grad_qkv"], ref["w_d_qkv"], ref["d_part"], back=True)
    totals[4].start()
    sums["d_up"].middle()
    totals[4].middle()
    last_second.wait_recv()

    def last_close(part):
        made = last_part[s.x, s.core, part] + last_met[s.x, part]
        before = ref["d_residual"][pl.ds(pl.multiple_of(s.blk * own + part.start, 64), 64)]
        whole = made + ref["last_came"][part].astype(F32) + before
        ref["decoded"][part] = whole.astype(BF16)
    each(quarter, 64, last_close)
    weight_grad(ref["d_mixture"], ref["d_branch"], ref["g_d_out"])
    sums["d_out"].start()
    weight_grad(ref["d_normed"], ref["d_grad_qkv"], ref["g_d_qkv"])
    sums["d_qkv"].start()
    totals[4].end()
    gain, bias = decoder.norm_back(ref["d_whole"], True, ref["d_branch"])
    vector_store(vector_grad, 5, gain, False)
    vector_store(vector_grad, 6, bias, False)

    def mask_sum(at, total):
        part = pl.ds(pl.multiple_of(at * 64, 64), 64)
        hidden_row = ref["rank_column"][part] < 0
        return total + jnp.sum(jnp.where(hidden_row, grad[part], 0.0), axis=0, keepdims=True)
    token_grad = lax.fori_loop(0, rows // 64, mask_sum, jnp.zeros((1, dec_width), F32))
    vector_store(vector_grad, 4, token_grad, False)
    picked = ref["picked"]
    picked[...] = dot(places, ref["d_branch"][...]).astype(BF16)
    grad = ref["e_grad"]

    def back_embed(part):
        made = dot_b(picked[...], ref["w_embed"][part])
        grad[:, part] = made
        ref["e_branch"][:, part] = made.astype(BF16)
    each(width, 256, back_embed)

    encoder.back_hidden(ref["e_branch"])
    encoder.product(ref["e_grad_upper"], ref["w_e_up"], ref["e_part"], back=True)
    totals[5].start()
    for name in ("d_out", "d_qkv"):
        sums[name].middle()
    totals[5].middle()
    for name in ("d_down", "d_up"):
        sums[name].last()
    weight_grad(ref["e_hidden"], ref["e_branch"], ref["g_e_down"])
    sums["e_down"].start()
    weight_grad(ref["e_lifted"], ref["e_grad_upper"], ref["g_e_up"])
    sums["e_up"].start()
    embed_columns = picked.at[:, columns]
    weight_grad(lowered, embed_columns, ref["g_embed"])
    sums["embed"].start()
    totals[5].end()
    gain, bias = encoder.norm_back(ref["e_whole"], False, ref["e_branch"])
    vector_store(vector_grad, 2, gain, True)
    vector_store(vector_grad, 3, bias, True)
    encoder.back_mixture(ref["e_branch"])
    encoder.attend_back()
    encoder.product(ref["e_grad_qkv"], ref["w_e_qkv"], ref["e_part"], back=True)
    totals[6].start()
    weight_grad(ref["e_mixture"], ref["e_branch"], ref["g_e_out"])
    sums["e_out"].start()
    totals[6].middle()
    weight_grad(ref["e_normed"], ref["e_grad_qkv"], ref["g_e_qkv"])
    sums["e_qkv"].start()
    totals[6].end()
    gain, bias = encoder.norm_back(ref["e_whole"], True, ref["e_branch"])
    vector_store(vector_grad, 0, gain, True)
    vector_store(vector_grad, 1, bias, True)
    sums["vector"].start()
    sums["e_down"].middle()
    for name in ("d_out", "d_qkv"):
        sums[name].last()
    rank = ref["rank_column"][mine]
    here = (lax.broadcasted_iota(jnp.int32, (own, shown), 1) == rank).astype(BF16)

    def place_grad(part):
        values = grad[:, part]
        top = values.astype(BF16)
        rest = (values - top.astype(F32)).astype(BF16)
        ref["grad_patches"][:, part] = dot(here, top) + dot(here, rest)
    each(width, 256, place_grad)
    for name in ("e_up", "embed", "e_out", "e_qkv", "vector"):
        sums[name].middle()
    for name in ("e_down", "e_up", "embed", "e_out", "e_qkv"):
        sums[name].last()

    def vector_out(part, whole):
        ref["grad_vector"][part] = whole
    sums["vector"].total(vector_out)
    sums["vector"].drain()
    for name in MESSAGES:
        sums[name].close()
    last_first.wait_send()
    last_second.wait_send()
    for name in order:
        units[name].drain()
    for which in range(3):
        shares(ref["patches"], ref["group"], "p", which).wait_send()
        shares(ref["cotangent"], ref["cotangents"], "c", which).wait_send()
        embed_copy(which).wait_send()


def unpack_kernel(names, *refs):
    ref = dict(zip(names, refs))
    side = lax.rem(lax.axis_index("dp"), 2)
    ref["decoded"][...] = ref["i_decoded"][...]
    ref["grad_patches"][...] = ref["i_grad_patches"][...]
    vectors = ref["i_grad_vector"][...]
    for at, name in enumerate(("e_gain_a", "e_bias_a", "e_gain_b", "e_bias_b")):
        ref[name][...] = vectors[at:at + 1, :]
    for at, name in enumerate(("mask", "d_gain_a", "d_bias_a", "d_gain_b", "d_bias_b")):
        row = vectors[at + 4:at + 5, :]
        ref[name][...] = jnp.where(side == 0, row[:, 0:64], row[:, 64:128])
    for blk in range(PARTS):
        part = 3 * blk % PARTS
        for key in ("e_", "d_"):
            size = ref[key + "query"].shape[1] // PARTS
            for place, kind in enumerate(("query", "key", "value")):
                ref[key + kind][:, part * size:(part + 1) * size] = ref["i_" + key + "qkv"][
                    blk, :, place * size:(place + 1) * size].astype(F32)
        size = ref["i_e_up"].shape[1]
        for owner in range(8):
            column = (owner * PARTS + blk) * size
            ref["e_up"][:, column:column + size] = ref["i_e_up"][
                blk, :, owner * size:(owner + 1) * size].astype(F32)
        size = ref["i_e_down"].shape[1]
        ref["e_down"][blk * size:(blk + 1) * size, :] = ref["i_e_down"][blk].astype(F32)
        for name in ("embed", "d_up"):
            size = ref["i_" + name].shape[2]
            ref[name][:, part * size:(part + 1) * size] = ref["i_" + name][blk].astype(F32)
    for name in ROW_UNITS:
        ref[name][...] = ref["i_" + name][...].astype(F32)


def local_kernel(*arguments):
    (patches, lengths, gsd_scale, visible,
     e_gain_a, e_bias_a, e_query, e_key, e_value, e_out, e_gain_b, e_bias_b, e_up, e_down,
     embed, mask,
     d_gain_a, d_bias_a, d_query, d_key, d_value, d_out, d_gain_b, d_bias_b, d_up, d_down,
     cotangent) = arguments
    width, dec_width = patches.shape[1], cotangent.shape[1]
    hidden, dec_hidden = e_up.shape[1], d_up.shape[1]
    rows = visible.shape[1]
    image_ids, scaled, rank = layout(lengths[0], gsd_scale[0], visible[0])
    places = rank[None, :] == jnp.arange(SHOWN, dtype=jnp.int32)[:, None]
    packed_ids = jnp.sum(jnp.where(places, image_ids[None, :], 0), axis=1)
    packed_scaled = jnp.sum(jnp.where(places, scaled[None, :], 0.0), axis=1)
    side = lax.rem(lax.axis_index("dp"), 2)
    zero = jnp.zeros((1, 64), BF16)

    def half(vector):
        row = vector[None, :]
        return jnp.where(side == 0, jnp.concatenate([row, zero], 1),
                         jnp.concatenate([zero, row], 1))

    vector = jnp.concatenate(
        [e_gain_a[None, :], e_bias_a[None, :], e_gain_b[None, :], e_bias_b[None, :], half(mask),
         half(d_gain_a), half(d_bias_a), half(d_gain_b), half(d_bias_b),
         jnp.zeros((VECTORS - 9, 128), BF16)], axis=0)
    inputs = {
        "rank_row": rank[None, :], "rank_column": rank[:, None],
        "ids_row": image_ids[None, :], "ids_column": image_ids[:, None],
        "packed_row": packed_ids[None, :], "packed_column": packed_ids[:, None],
        "code": sincos(packed_scaled, width), "dec_code": sincos(scaled, dec_width),
        "vector": vector, "patches": patches, "cotangent": cotangent,
        "query": e_query, "key": e_key, "value": e_value, "out": e_out, "up": e_up,
        "down": e_down, "embed": embed, "dec_query": d_query, "dec_key": d_key,
        "dec_value": d_value, "dec_out": d_out, "dec_up": d_up, "dec_down": d_down,
    }
    units = unit_shapes(width, dec_width, hidden, dec_hidden)
    shapes = {
        "decoded": (cotangent.shape, BF16), "grad_patches": (patches.shape, F32),
        "grad_vector": ((VECTORS, 128), F32),
    }
    for name in COLUMN_UNITS:
        shapes[name] = ((PARTS,) + units[name], BF16)
    for name in ROW_UNITS:
        shapes[name] = (units[name], BF16)
    table = scratch_table(width, dec_width, hidden, dec_hidden, rows, SHOWN)
    names = INPUTS + tuple("o_" + name if name in MESSAGES else name for name in RESULTS)
    names = names + tuple(table) + tuple("s_" + name for name in SEMAPHORES)
    in_vmem = INPUTS[:9]
    results = pl.pallas_call(
        functools.partial(main_kernel, names),
        out_shape=[jax.ShapeDtypeStruct(*shapes[name]) for name in RESULTS],
        in_specs=[
            pl.BlockSpec(memory_space=pltpu.VMEM if name in in_vmem else pl.ANY)
            for name in INPUTS
        ],
        out_specs=[pl.BlockSpec(memory_space=pltpu.VMEM) for name in RESULTS],
        scratch_shapes=[pltpu.VMEM(*entry) for entry in table.values()]
        + [pltpu.SemaphoreType.DMA(shape) for shape in SEMAPHORES.values()],
        compiler_params=pltpu.CompilerParams(
            collective_id=0, has_side_effects=True, vmem_limit_bytes=62 * MIB
        ),
    )(*(inputs[name] for name in INPUTS))
    made = {"i_" + name: result for name, result in zip(RESULTS, results)}
    finals = {
        "decoded": (cotangent.shape, BF16), "grad_patches": (patches.shape, F32),
    }
    for key, wide, deep in (("e_", width, hidden), ("d_", dec_width, dec_hidden)):
        small, tall = wide // 8, deep // 8
        if key == "d_":
            finals["embed"] = ((width // 8, dec_width), F32)
            finals["mask"] = ((1, small), F32)
        for name, shape in (
            ("gain_a", (1, small)), ("bias_a", (1, small)), ("query", (small, wide)),
            ("key", (small, wide)), ("value", (small, wide)), ("out", (small, wide)),
            ("gain_b", (1, small)), ("bias_b", (1, small)), ("up", (small, deep)),
            ("down", (tall, wide)),
        ):
            finals[key + name] = (shape, F32)
    outputs = pl.pallas_call(
        functools.partial(unpack_kernel, tuple(made) + tuple(finals)),
        out_shape=[jax.ShapeDtypeStruct(*entry) for entry in finals.values()],
        in_specs=[pl.BlockSpec(memory_space=pltpu.VMEM)] * len(made),
        out_specs=[pl.BlockSpec(memory_space=pltpu.VMEM)] * len(finals),
        compiler_params=pltpu.CompilerParams(vmem_limit_bytes=40 * MIB),
    )(*made.values())
    return tuple(
        output.reshape(-1) if output.shape[0] == 1 else output for output in outputs
    )


def solution(mesh):
    both, vec, mat = P(("dp", "blk"), None), P("dp"), P("dp", None)
    block = (vec, vec, mat, mat, mat, mat, vec, vec, mat, mat)
    in_specs = (both, mat, mat, mat) + block + (mat, vec) + block + (both,)
    out_specs = (both, both) + block + (mat, vec) + block
    body = local_kernel if mesh.shape["dp"] == 8 and mesh.shape["blk"] == 4 else local
    return jax.shard_map(body, mesh=mesh, in_specs=in_specs, out_specs=out_specs, check_vma=False)
```

```python
import functools
import math

import jax
import jax.numpy as jnp
from jax import lax
from jax.experimental import pallas as pl
from jax.experimental.pallas import tpu as pltpu
from jax.sharding import PartitionSpec as P

HEADS = 16
EPSILON = 1e-06
MASKED_SCORE = -1e30
F32 = jnp.float32
BF16 = jnp.bfloat16


def dot(left, right):
    return lax.dot_general(left, right, (((1,), (0,)), ((), ())), preferred_element_type=F32)


def dot_t(left, right):
    return lax.dot_general(left, right, (((0,), (0,)), ((), ())), preferred_element_type=F32)


def dot_b(left, right):
    return lax.dot_general(left, right, (((1,), (1,)), ((), ())), preferred_element_type=F32)


def sincos(scaled, width):
    half_width = width // 2
    frequency = jnp.exp(
        jnp.arange(half_width, dtype=F32) * (-math.log(10000.0) / half_width)
    )
    angles = scaled[:, None] * frequency[None, :]
    return jnp.concatenate([jnp.sin(angles), jnp.cos(angles)], axis=1)


def norm_parts(values):
    center = values - jnp.mean(values, axis=-1, keepdims=True)
    spread = jnp.mean(center * center, axis=-1, keepdims=True)
    scale = lax.rsqrt(spread + EPSILON)
    return center * scale, scale


def norm_back(grad, unit, scale, gain):
    grad_gain = jnp.sum(grad * unit, axis=0, keepdims=True)
    grad_bias = jnp.sum(grad, axis=0, keepdims=True)
    inner = grad * gain
    mean_inner = jnp.mean(inner, axis=-1, keepdims=True)
    mean_cross = jnp.mean(inner * unit, axis=-1, keepdims=True)
    return scale * (inner - mean_inner - unit * mean_cross), grad_gain, grad_bias


def gelu_both(upper):
    phi = 0.5 * (1.0 + lax.erf(upper * math.sqrt(0.5)))
    density = jnp.exp(-0.5 * upper * upper) * (1.0 / math.sqrt(2.0 * math.pi))
    return upper * phi, phi + upper * density


def head_forward(queries, key_rows, values, allowed, scaling):
    scores = jnp.where(allowed, dot_b(queries, key_rows) * scaling, MASKED_SCORE)
    largest = jnp.max(scores, axis=-1, keepdims=True)
    exponent = jnp.exp(scores - largest)
    softmaxed = exponent / jnp.sum(exponent, axis=-1, keepdims=True)
    return softmaxed, dot(softmaxed.astype(BF16), values).astype(BF16)


def head_backward(queries, key_rows, values, softmaxed, grad_mixture, scaling):
    grad_values = dot_t(softmaxed.astype(BF16), grad_mixture).astype(BF16)
    grad_probs = dot_b(grad_mixture, values)
    delta = jnp.sum(softmaxed * grad_probs, axis=-1, keepdims=True)
    grad_scores = (softmaxed * (grad_probs - delta)).astype(BF16)
    grad_queries = (dot(grad_scores, key_rows) * scaling).astype(BF16)
    grad_keys = (dot_t(grad_scores, queries) * scaling).astype(BF16)
    return grad_queries, grad_keys, grad_values


def block_forward(residual, params, heads, allowed, total):
    gain_a, bias_a, w_query, w_key, w_value, w_out, gain_b, bias_b, w_up, w_down = params
    unit_a, scale_a = norm_parts(residual)
    normed = (unit_a * gain_a + bias_a).astype(BF16)
    queries = dot(normed, w_query).astype(BF16)
    key_rows = dot(normed, w_key).astype(BF16)
    values = dot(normed, w_value).astype(BF16)
    size = queries.shape[1] // heads
    scaling = 1.0 / math.sqrt(size)
    probs, mixed = [], []
    for head in range(heads):
        part = slice(head * size, (head + 1) * size)
        softmaxed, mixture = head_forward(
            queries[:, part], key_rows[:, part], values[:, part], allowed, scaling
        )
        probs.append(softmaxed)
        mixed.append(mixture)
    mixture = jnp.concatenate(mixed, axis=1)
    middle = residual + total(dot(mixture, w_out))
    unit_b, scale_b = norm_parts(middle)
    lifted = (unit_b * gain_b + bias_b).astype(BF16)
    hidden, slope = gelu_both(dot(lifted, w_up))
    hidden = hidden.astype(BF16)
    result = middle + total(dot(hidden, w_down))
    return result, (
        unit_a, scale_a, normed, queries, key_rows, values, probs, mixture,
        unit_b, scale_b, lifted, slope, hidden,
    )


def block_backward(grad_result, params, heads, saved, total):
    gain_a, bias_a, w_query, w_key, w_value, w_out, gain_b, bias_b, w_up, w_down = params
    (unit_a, scale_a, normed, queries, key_rows, values, probs, mixture,
     unit_b, scale_b, lifted, slope, hidden) = saved
    size = queries.shape[1] // heads
    scaling = 1.0 / math.sqrt(size)
    grad_branch = grad_result.astype(BF16)
    grad_down = dot_t(hidden, grad_branch)
    grad_upper = (dot_b(grad_branch, w_down) * slope).astype(BF16)
    grad_up = dot_t(lifted, grad_upper)
    grad_lifted = total(dot_b(grad_upper, w_up))
    grad_in, grad_gain_b, grad_bias_b = norm_back(grad_lifted, unit_b, scale_b, gain_b)
    grad_middle = grad_result + grad_in
    grad_attention = grad_middle.astype(BF16)
    grad_out = dot_t(mixture, grad_attention)
    grad_mixture = dot_b(grad_attention, w_out).astype(BF16)
    pieces = []
    for head in range(heads):
        part = slice(head * size, (head + 1) * size)
        pieces.append(
            head_backward(
                queries[:, part], key_rows[:, part], values[:, part], probs[head],
                grad_mixture[:, part], scaling,
            )
        )
    grad_queries, grad_keys, grad_values = (
        jnp.concatenate([piece[at] for piece in pieces], axis=1) for at in range(3)
    )
    grad_normed = total(
        dot_b(grad_queries, w_query) + dot_b(grad_keys, w_key) + dot_b(grad_values, w_value)
    )
    grad_in, grad_gain_a, grad_bias_a = norm_back(grad_normed, unit_a, scale_a, gain_a)
    return grad_middle + grad_in, (
        grad_gain_a, grad_bias_a, dot_t(normed, grad_queries), dot_t(normed, grad_keys),
        dot_t(normed, grad_values), grad_out, grad_gain_b, grad_bias_b, grad_up, grad_down,
    )


def layout(lengths_row, gsd_row, visible_row):
    count = visible_row.shape[0]
    positions = jnp.arange(count, dtype=jnp.int32)
    image_ends = jnp.cumsum(lengths_row)
    image_starts = image_ends - lengths_row
    image_ids = jnp.sum((positions[:, None] >= image_ends[None, :]).astype(jnp.int32), axis=1)
    onehot = image_ids[:, None] == jnp.arange(lengths_row.shape[0], dtype=jnp.int32)[None, :]
    first_row = jnp.sum(jnp.where(onehot, image_starts[None, :], 0), axis=1)
    ratio = jnp.sum(jnp.where(onehot, gsd_row[None, :], 0.0), axis=1)
    scaled = (positions - first_row).astype(F32) * ratio
    shown = visible_row > 0
    earlier = (positions[None, :] <= positions[:, None]) & shown[None, :]
    rank = jnp.where(shown, jnp.sum(earlier.astype(jnp.int32), axis=1) - 1, -1)
    return image_ids, scaled, rank


def spread_rows(grad, rank, offset, rows):
    own = lax.dynamic_slice_in_dim(rank, offset, rows)
    place = (own[:, None] == jnp.arange(grad.shape[0], dtype=jnp.int32)[None, :]).astype(BF16)
    high = grad.astype(BF16)
    low = (grad - high.astype(F32)).astype(BF16)
    return dot(place, high) + dot(place, low)


SHOWN = 128


def local(*arguments):
    patches, lengths, gsd_scale, visible = arguments[:4]
    encoder_shards = arguments[4:14]
    embed_shard, mask_shard = arguments[14:16]
    decoder_shards = arguments[16:26]
    cotangent = arguments[26]
    dp_count = lax.axis_size("dp")
    blk_count = lax.axis_size("blk")
    blk = lax.axis_index("blk")
    dp = lax.axis_index("dp")
    rows = patches.shape[0]
    offset = blk * rows
    heads = HEADS // blk_count
    image_ids, scaled, rank = layout(lengths[0], gsd_scale[0], visible[0])
    shown = rank >= 0
    places = rank[None, :] == jnp.arange(SHOWN, dtype=jnp.int32)[:, None]
    packed_ids = jnp.sum(jnp.where(places, image_ids[None, :], 0), axis=1)
    packed_scaled = jnp.sum(jnp.where(places, scaled[None, :], 0.0), axis=1)

    def gather(shard):
        return lax.all_gather(shard, "dp", axis=0, tiled=True)

    def by_columns(shard):
        width = shard.shape[1] // blk_count
        return gather(lax.dynamic_slice_in_dim(shard, blk * width, width, axis=1))

    def by_rows(shard):
        whole = gather(shard)
        height = whole.shape[0] // blk_count
        return lax.dynamic_slice_in_dim(whole, blk * height, height, axis=0)

    def vector(shard):
        return gather(shard).astype(F32)[None, :]

    def load(shards):
        kinds = (vector, vector, by_columns, by_columns, by_columns, by_rows,
                 vector, vector, by_columns, by_rows)
        return tuple(kind(shard) for kind, shard in zip(kinds, shards))

    def total(partial):
        return lax.psum(partial, "blk")

    def sum_columns(grad):
        summed = lax.psum_scatter(grad.astype(BF16), "dp", scatter_dimension=0, tiled=True)
        return lax.all_gather(summed, "blk", axis=1, tiled=True).astype(F32)

    def sum_rows(grad):
        whole = lax.all_gather(grad.astype(BF16), "blk", axis=0, tiled=True)
        return lax.psum_scatter(whole, "dp", scatter_dimension=0, tiled=True).astype(F32)

    def sum_vector(grad):
        return lax.psum_scatter(grad[0], "dp", scatter_dimension=0, tiled=True)

    def reduce(grads):
        kinds = (sum_vector, sum_vector, sum_columns, sum_columns, sum_columns, sum_rows,
                 sum_vector, sum_vector, sum_columns, sum_rows)
        return tuple(kind(grad) for kind, grad in zip(kinds, grads))

    group = lax.all_gather(patches, "blk", axis=0, tiled=True)
    picked = dot(places.astype(BF16), group)
    encoder = load(encoder_shards)
    residual = picked + sincos(packed_scaled, patches.shape[1])
    encoded, encoder_saved = block_forward(
        residual, encoder, heads, packed_ids[:, None] == packed_ids[None, :], total
    )
    embed = gather(embed_shard)
    lowered = encoded.astype(BF16)
    embedded = dot(lowered, embed)
    high = embedded.astype(BF16)
    low = (embedded - high.astype(F32)).astype(BF16)
    places_b = places.astype(BF16)
    start = jnp.where(
        shown[:, None], dot_t(places_b, high) + dot_t(places_b, low), vector(mask_shard)
    ) + sincos(scaled, embed.shape[1])
    decoder = load(decoder_shards)
    decoded, decoder_saved = block_forward(
        start, decoder, heads, image_ids[:, None] == image_ids[None, :], total
    )
    decoded_rows = lax.dynamic_slice_in_dim(decoded, offset, rows).astype(BF16)
    grad_out = lax.all_gather(cotangent, "blk", axis=0, tiled=True).astype(F32)
    grad_start, decoder_grads = block_backward(grad_out, decoder, heads, decoder_saved, total)
    grad_mask = jnp.sum(jnp.where(shown[:, None], 0.0, grad_start), axis=0, keepdims=True)
    grad_embedded = dot(places_b, grad_start.astype(BF16)).astype(BF16)
    width = embed.shape[1] // blk_count
    grad_embed = dot_t(
        lowered, lax.dynamic_slice_in_dim(grad_embedded, blk * width, width, axis=1)
    )
    grad_encoded = dot_b(grad_embedded, embed)
    grad_residual, encoder_grads = block_backward(
        grad_encoded, encoder, heads, encoder_saved, total
    )
    grad_patches = spread_rows(grad_residual, rank, offset, rows)
    return (
        (decoded_rows, grad_patches) + reduce(encoder_grads)
        + (sum_columns(grad_embed), sum_vector(grad_mask)) + reduce(decoder_grads)
    )


MIB = 2**20
DECODER_ROWS = 512
PARTS = 4
SIDES = 2
VECTORS = 16


class Split:
    def __init__(self):
        self.dp = lax.axis_index("dp")
        self.blk = lax.axis_index("blk")
        self.z = lax.div(self.dp, 2)
        self.y = lax.rem(self.dp, 2)
        self.x = lax.div(self.blk, 2)
        self.core = lax.rem(self.blk, 2)
        self.part = lax.rem(3 * self.blk, PARTS)
        self.y_peer = (self.z * 2 + 1 - self.y, self.blk)
        self.core_peer = (self.dp, self.x * 2 + 1 - self.core)
        self.x_peer = (self.dp, (1 - self.x) * 2 + self.core)
        self.far_peer = (self.dp, (1 - self.x) * 2 + 1 - self.core)
        self.blk_peers = (self.core_peer, self.x_peer, self.far_peer)

    def ahead(self, step):
        return lax.rem(self.z + step, PARTS)

    def behind(self, step):
        return lax.rem(self.z + PARTS - step, PARTS)

    def z_peer(self, step):
        return (self.ahead(step) * 2 + self.y, self.blk)

    def at_z(self, z):
        return (z * 2 + self.y, self.blk)

    def inward(self, step):
        high = lax.div(self.z, 2)
        return lax.rem(self.z + high * (PARTS - step) + (1 - high) * step, PARTS)

    @property
    def inner(self):
        return jnp.logical_or(self.z == 1, self.z == 2)

    @property
    def near_end(self):
        return jnp.where(self.inner, 3 * self.z - 3, lax.div(self.z, 3) + 1)

    @property
    def far_end(self):
        return 6 - 3 * self.z


def remote(source, target, sent, received, device):
    return pltpu.make_async_remote_copy(
        src_ref=source, dst_ref=target, send_sem=sent, recv_sem=received,
        device_id=device, device_id_type=pl.DeviceIdType.MESH,
    )


def span(at, size):
    return pl.ds(pl.multiple_of(at, size), size)


class Columns:
    def __init__(self, split, whole, rows, local, sems, columns=None):
        self.split, self.whole, self.rows, self.local = split, whole, rows, local
        self.columns = columns
        self.z_sent, self.z_got, self.y_sent, self.y_got = sems

    def block(self, z, y):
        rows = span((z * 2 + y) * self.rows, self.rows)
        if self.columns is None:
            return self.whole.at[rows]
        return self.whole.at[rows, self.columns]

    def z_copy(self, step, y=None):
        s = self.split
        block = self.block(s.z, s.y if y is None else y)
        at = 0 if y is None else 1
        return remote(block, block, self.z_sent.at[at, step - 1], self.z_got.at[at, s.z],
                      s.at_z(s.inward(step)))

    def z_arrival(self, z, y=None):
        s = self.split
        block = self.block(z, s.y if y is None else y)
        at = 0 if y is None else 1
        return remote(block, block, self.z_sent.at[at, 0], self.z_got.at[at, z], s.y_peer)

    def relay(self, y=None):
        s = self.split
        block = self.block(s.far_end, s.y if y is None else y)
        at = 0 if y is None else 1
        return remote(block, block, self.z_sent.at[at, 3], self.z_got.at[at, s.far_end],
                      s.at_z(s.near_end))

    def y_copy(self, z, at):
        s = self.split
        block = self.block(z, s.y)
        return remote(block, block, self.y_sent.at[at], self.y_got.at[at], s.y_peer)

    def y_arrival(self, z, at):
        s = self.split
        block = self.block(z, 1 - s.y)
        return remote(block, block, self.y_sent.at[at], self.y_got.at[at], s.y_peer)

    def fetch(self):
        for copy in self.local:
            copy.start()

    def spread(self, y=None):
        self.z_copy(1, y).start()
        self.z_copy(2, y).start()

        @pl.when(self.split.inner)
        def _():
            self.z_copy(3, y).start()

    def collect(self, step, y=None):
        s = self.split
        z = s.inward(step)
        self.z_arrival(z, y).wait_recv()
        if step == 2:
            @pl.when(s.inner)
            def _():
                self.relay(y).start()
        return z

    def send(self):
        for copy in self.local:
            copy.wait()
        self.spread()
        self.y_copy(self.split.z, 0).start()

    def forward(self):
        for step in (1, 2, 3):
            self.y_copy(self.collect(step), step).start()

    def finish(self):
        for step in range(PARTS):
            self.y_arrival(self.split.inward(step), step).wait_recv()

    def drain_z(self, y=None):
        self.z_copy(1, y).wait_send()
        self.z_copy(2, y).wait_send()

        @pl.when(self.split.inner)
        def _():
            self.z_copy(3, y).wait_send()
            self.relay(y).wait_send()

    def drain(self):
        self.drain_z()
        for step in range(PARTS):
            self.y_copy(self.split.inward(step), step).wait_send()


class EarlyColumns(Columns):
    def cross(self):
        s = self.split
        self.y_arrival(s.z, 0).wait_recv()
        self.spread(1 - s.y)

    def forward(self):
        for step in (1, 2, 3):
            self.collect(step)

    def finish(self):
        for step in (1, 2, 3):
            self.collect(step, 1 - self.split.y)

    def drain(self):
        self.drain_z()
        self.drain_z(1 - self.split.y)
        self.y_copy(self.split.z, 0).wait_send()


class Rows:
    def __init__(self, split, whole, rows, local, sems):
        self.split, self.whole, self.rows, self.local = split, whole, rows, local
        self.z_sent, self.z_got, self.y_sent, self.y_got = sems

    def block(self, y):
        return self.whole.at[span(y * self.rows, self.rows)]

    def z_copy(self, way):
        s = self.split
        return remote(self.block(s.y), self.block(s.y), self.z_sent.at[0, way],
                      self.z_got.at[0, 0], s.at_z(s.z + 1 - 2 * way))

    def pass_on(self, act):
        s = self.split

        @pl.when(jnp.logical_and(s.z >= s.part, s.z < PARTS - 1))
        def _():
            act(self.z_copy(0))

        @pl.when(jnp.logical_and(s.z <= s.part, s.z > 0))
        def _():
            act(self.z_copy(1))

    def y_copy(self):
        s = self.split
        return remote(self.block(s.y), self.block(s.y), self.y_sent.at[0],
                      self.y_got.at[0], s.y_peer)

    def fetch(self):
        @pl.when(self.split.z == self.split.part)
        def _():
            self.local.start()

    def send(self):
        @pl.when(self.split.z == self.split.part)
        def _():
            self.local.wait()
            self.pass_on(lambda copy: copy.start())
            self.y_copy().start()

    def forward(self):
        s = self.split

        @pl.when(s.z != s.part)
        def _():
            remote(self.block(s.y), self.block(s.y), self.z_sent.at[0, 0],
                   self.z_got.at[0, 0], s.y_peer).wait_recv()
            self.pass_on(lambda copy: copy.start())
            self.y_copy().start()

    def finish(self):
        s = self.split
        block = self.block(1 - s.y)
        remote(block, block, self.y_sent.at[0], self.y_got.at[0], s.y_peer).wait_recv()

    def drain(self):
        self.pass_on(lambda copy: copy.wait_send())
        self.y_copy().wait_send()


def each(count, step, body, base=0):
    @pl.loop(0, count // step)
    def _(at):
        body(pl.ds(pl.multiple_of(base + at * step, step), step))


class ColumnSum:
    def __init__(self, split, grad, met, came, done, sems, step):
        self.split, self.grad, self.met, self.came, self.done = split, grad, met, came, done
        self.y_sent, self.y_got, self.z_sent, self.z_got, self.b_sent, self.b_got = sems
        self.step = step

    def y_copy(self):
        s = self.split
        return remote(self.grad.at[:, 1 - s.y], self.met, self.y_sent, self.y_got, s.y_peer)

    def z_copy(self, step):
        s = self.split
        target = s.inward(step)
        return remote(self.met.at[target], self.came.at[s.z], self.z_sent.at[step - 1],
                      self.z_got.at[s.z], s.at_z(target))

    def z_arrival(self, z):
        s = self.split
        return remote(self.met.at[z], self.came.at[z], self.z_sent.at[0], self.z_got.at[z],
                      s.y_peer)

    def relay(self):
        s = self.split
        return remote(self.met.at[3 - s.z], self.came.at[s.near_end], self.z_sent.at[2],
                      self.z_got.at[s.near_end], s.at_z(s.near_end))

    def b_copy(self, which):
        s = self.split
        if which == 2:
            block = self.done.at[s.x_peer[1]]
            return remote(block, block, self.b_sent.at[2], self.b_got.at[2], s.core_peer)
        return remote(self.met.at[s.z], self.done.at[s.blk], self.b_sent.at[which],
                      self.b_got.at[which], s.blk_peers[which])

    def b_arrival(self, which):
        s = self.split
        block = self.done.at[s.blk_peers[which][1]]
        return remote(block, block, self.b_sent.at[which], self.b_got.at[which],
                      s.blk_peers[which])

    def own_copy(self):
        s = self.split
        return pltpu.make_async_copy(self.met.at[s.z], self.done.at[s.blk], self.b_sent.at[3])

    def start(self):
        self.y_copy().start()

    def add(self, z):
        def body(rows):
            both = self.grad[z, self.split.y, rows].astype(F32) + self.met[z, rows].astype(F32)
            self.met[z, rows] = both.astype(self.met.dtype)
        each(self.met.shape[1], self.step, body)

    def arrive(self):
        self.y_copy().wait_recv()

    def middle(self):
        s = self.split
        self.arrive()

        @pl.when(s.inner)
        def _():
            self.add(s.inward(1))
            self.z_copy(1).start()
            self.add(s.inward(3))
            self.z_copy(3).start()
            self.add(s.inward(2))

        @pl.when(jnp.logical_not(s.inner))
        def _():
            self.add(3 - s.z)
            self.relay().start()
            self.add(s.inward(2))
            self.z_copy(2).start()
            self.add(s.inward(1))
            self.z_copy(1).start()
        self.add(s.z)

    def join(self):
        s = self.split

        @pl.when(s.inner)
        def _():
            target = s.inward(2)
            self.z_arrival(s.z).wait_recv()

            def body(rows):
                both = self.met[target, rows].astype(F32) + self.came[s.z, rows].astype(F32)
                self.met[target, rows] = both.astype(self.met.dtype)
            each(self.met.shape[1], self.step, body)
            self.z_copy(2).start()

    def total(self, store):
        s = self.split

        @pl.when(s.inner)
        def _():
            sources = (0, 3, 3 - s.z)
            for z in sources:
                self.z_arrival(z).wait_recv()

            def body(rows):
                whole = self.met[s.z, rows].astype(F32)
                for z in sources:
                    whole = whole + self.came[z, rows].astype(F32)
                store(rows, whole)
            each(self.met.shape[1], self.step, body)

        @pl.when(jnp.logical_not(s.inner))
        def _():
            for z in (1, 2):
                self.z_arrival(z).wait_recv()

            def body(rows):
                whole = self.met[s.z, rows].astype(F32)
                for z in (1, 2):
                    whole = whole + self.came[z, rows].astype(F32)
                store(rows, whole)
            each(self.met.shape[1], self.step, body)

    def last(self):
        s = self.split

        def store(rows, whole):
            self.met[s.z, rows] = whole.astype(self.met.dtype)
        self.total(store)
        self.b_copy(1).start()
        self.b_copy(0).start()
        self.own_copy().start()

    def pass_on(self):
        self.b_arrival(1).wait_recv()
        self.b_copy(2).start()

    def close(self):
        self.b_arrival(0).wait_recv()
        self.b_arrival(2).wait_recv()
        for which in range(3):
            self.b_copy(which).wait_send()
        self.own_copy().wait()
        self.drain()

    def drain_y(self):
        self.y_copy().wait_send()

    def drain(self):
        self.drain_y()
        for step in (1, 2, 3):
            self.z_copy(step).wait_send()


class ProductSum(ColumnSum):
    def trade(self, left, right, their_left, their_right, sems):
        self.left, self.right = left, right
        self.their_left, self.their_right = their_left, their_right
        self.t_sent, self.t_got = sems
        self.width = their_left.shape[2]

    def columns(self, z, y):
        return self.left.at[:, span((z * 2 + y) * self.width, self.width)]

    def left_copy(self, z):
        s = self.split
        return remote(self.columns(z, 1 - s.y), self.their_left.at[z], self.t_sent.at[z],
                      self.t_got.at[z], s.y_peer)

    def right_copy(self):
        return remote(self.right, self.their_right, self.t_sent.at[PARTS],
                      self.t_got.at[PARTS], self.split.y_peer)

    def copies(self):
        return [self.right_copy()] + [self.left_copy(z) for z in range(PARTS)]

    def start(self):
        for copy in self.copies():
            copy.start()

    def add(self, z):
        both = dot_t(self.columns(z, self.split.y)[...], self.right[...]) + dot_t(
            self.their_left[z], self.their_right[...])
        self.met[z] = both.astype(self.met.dtype)

    def arrive(self):
        for copy in self.copies():
            copy.wait_recv()

    def drain_y(self):
        for copy in self.copies():
            copy.wait_send()


class RowSum:
    def __init__(self, split, grad, met, came, done, sems, step):
        self.split, self.grad, self.met, self.came, self.done = split, grad, met, came, done
        self.y_sent, self.y_got, self.z_sent, self.z_got, self.b_sent, self.b_got = sems
        self.step = step
        s = split
        self.home = lax.rem(3 * s.z, PARTS)
        self.at_home = s.z == s.part
        self.below = s.z < s.part
        self.above = s.z > s.part
        self.beside = s.x_peer[1] == self.home

    def y_copy(self):
        s = self.split
        return remote(self.grad.at[1 - s.y], self.met, self.y_sent, self.y_got, s.y_peer)

    def z_copy(self, way):
        s = self.split
        return remote(self.met, self.came.at[way], self.z_sent.at[way], self.z_got.at[way],
                      s.at_z(s.z + 1 - 2 * way))

    def z_arrival(self, way):
        return remote(self.met, self.came.at[way], self.z_sent.at[way], self.z_got.at[way],
                      self.split.y_peer)

    def b_copy(self, which):
        s = self.split
        source = self.done if which == 2 else self.met
        device = s.core_peer if which == 2 else s.blk_peers[which]
        return remote(source, self.done, self.b_sent.at[which], self.b_got.at[0], device)

    def own_copy(self):
        return pltpu.make_async_copy(self.met, self.done, self.b_sent.at[3])

    def start(self):
        self.y_copy().start()

    def send(self, act):
        @pl.when(self.below)
        def _():
            act(self.z_copy(0))

        @pl.when(self.above)
        def _():
            act(self.z_copy(1))

    def take(self, way):
        self.z_arrival(way).wait_recv()

        def body(rows):
            both = self.met[rows].astype(F32) + self.came[way, rows].astype(F32)
            self.met[rows] = both.astype(self.met.dtype)
        each(self.met.shape[0], self.step, body)

    def middle(self):
        s = self.split
        self.y_copy().wait_recv()

        def body(rows):
            both = self.grad[s.y, rows].astype(F32) + self.met[rows].astype(F32)
            self.met[rows] = both.astype(self.met.dtype)
        each(self.met.shape[0], self.step, body)

        @pl.when(jnp.logical_not(s.inner))
        def _():
            self.send(lambda copy: copy.start())

    def join(self):
        s = self.split

        @pl.when(s.inner)
        def _():
            @pl.when(self.below)
            def _():
                self.take(0)

            @pl.when(self.above)
            def _():
                self.take(1)
            self.send(lambda copy: copy.start())

    def last(self):
        s = self.split

        @pl.when(self.at_home)
        def _():
            @pl.when(s.z > 0)
            def _():
                self.take(0)

            @pl.when(s.z < PARTS - 1)
            def _():
                self.take(1)
            self.b_copy(1).start()
            self.b_copy(0).start()
            self.own_copy().start()

    def pass_on(self):
        @pl.when(self.beside)
        def _():
            self.b_copy(0).wait_recv()
            self.b_copy(2).start()

    def close(self):
        self.y_copy().wait_send()
        self.send(lambda copy: copy.wait_send())

        @pl.when(self.at_home)
        def _():
            self.b_copy(0).wait_send()
            self.b_copy(1).wait_send()
            self.own_copy().wait()

        @pl.when(self.beside)
        def _():
            self.b_copy(2).wait_send()

        @pl.when(jnp.logical_not(jnp.logical_or(self.at_home, self.beside)))
        def _():
            self.b_copy(0).wait_recv()


class Total:
    def __init__(self, split, part, met, out, came, whole, sems, slot):
        self.split, self.part, self.met, self.out = split, part, met, out
        self.came, self.whole = came.at[slot], whole
        self.sent, self.got = sems
        self.chunks = part.shape[0]
        self.high = part.shape[2]

    def first_copy(self, at):
        s = self.split
        return remote(self.part.at[at, 1 - s.core], self.met.at[at], self.sent.at[at, 0],
                      self.got.at[at, 0], s.core_peer)

    def second_copy(self, at):
        return remote(self.out.at[at], self.came.at[at], self.sent.at[at, 1],
                      self.got.at[at, 1], self.split.x_peer)

    def third_copy(self, at, half):
        s = self.split
        return remote(self.whole.at[at, half], self.whole.at[at, half], self.sent.at[at, 2],
                      self.got.at[at, 2], s.core_peer)

    def start(self, at):
        self.first_copy(at).start()

    def middle(self, at):
        s = self.split
        self.first_copy(at).wait_recv()

        def body(rows):
            both = self.part[at, s.core, rows] + self.met[at, rows]
            self.out[at, rows] = both.astype(BF16)
        each(self.high, 32, body)
        self.second_copy(at).start()

    def third(self, at):
        s = self.split
        self.second_copy(at).wait_recv()

        def body(rows):
            self.whole[at, s.core, rows] = self.out[at, rows].astype(
                F32) + self.came[at, rows].astype(F32)
        each(self.high, 32, body)
        self.third_copy(at, s.core).start()

    def fourth(self, at):
        s = self.split
        self.third_copy(at, 1 - s.core).wait_recv()
        self.first_copy(at).wait_send()
        self.second_copy(at).wait_send()
        self.third_copy(at, s.core).wait_send()

    def begin(self, produce):
        @pl.loop(0, self.chunks + 1)
        def _(at):
            @pl.when(at < self.chunks)
            def _():
                produce(at)
                self.start(at)

            @pl.when(at > 0)
            def _():
                self.middle(at - 1)

    def finish(self, consume):
        self.third(0)

        @pl.loop(0, self.chunks)
        def _(at):
            @pl.when(at + 1 < self.chunks)
            def _():
                self.third(at + 1)
            self.fourth(at)
            consume(at)


def head_mask(width, size, head):
    lanes = lax.broadcasted_iota(jnp.int32, (1, width), 1)
    return lax.div(lanes, size) == head


def keep(mask, values):
    return jnp.where(mask, values, jnp.zeros_like(values))


class Block:
    def __init__(self, rows, width, heads, size, names, refs, vectors):
        self.rows, self.width, self.heads, self.size = rows, width, heads, size
        self.share = heads * size
        self.scaling = 1.0 / math.sqrt(size)
        self.refs = refs
        self.vectors = vectors
        self.name = names
        self.tile = 32 * 1024 // width
        self.chunk = 2 * refs[names + "part"].shape[2]

    def ref(self, name):
        return self.refs[self.name + name]

    def row(self, at):
        return self.refs["gains"][self.vectors + at:self.vectors + at + 1, 0:self.width]

    def norm(self, first, base=0, count=None):
        unit, scale = self.ref("unit_a" if first else "unit_b"), self.ref(
            "scale_a" if first else "scale_b")
        out = self.ref("normed" if first else "lifted")
        gain, bias = self.row(0 if first else 2), self.row(1 if first else 3)
        residual = self.ref("residual")

        def body(rows):
            one, size = norm_parts(residual[rows])
            unit[rows] = one
            scale[rows] = size
            out[rows] = (one * gain + bias).astype(BF16)
        each(count or self.rows, self.tile, body, base)

    def project(self):
        normed, mixed, weight = self.ref("normed"), self.ref("qkv"), self.ref("w_qkv")

        def body(rows):
            mixed[rows] = dot(normed[rows], weight[...]).astype(BF16)
        each(self.rows, 128, body)

    def parts(self, rows):
        share, qkv = self.share, self.ref("qkv")
        return (qkv[rows, 0:share], qkv[rows, share:2 * share], qkv[rows, 2 * share:3 * share])

    def attend(self, ids_column, ids_row):
        probs, mixture = self.ref("probs"), self.ref("mixture")
        everything = pl.ds(0, self.rows)

        def body(queries):
            query = self.parts(queries)[0]
            unused, key_rows, values = self.parts(everything)
            allowed = ids_column[...] == ids_row[:, queries]

            def one(head, mixed):
                mask = head_mask(self.share, self.size, head)
                scores = jnp.where(
                    allowed, dot_b(keep(mask, key_rows), query) * self.scaling, MASKED_SCORE
                )
                exponent = jnp.exp(scores - jnp.max(scores, axis=0, keepdims=True))
                softmaxed = exponent * (1.0 / jnp.sum(exponent, axis=0, keepdims=True))
                probs[head, :, queries] = softmaxed
                return mixed + dot_t(keep(mask, values), softmaxed.astype(BF16))

            mixed = lax.fori_loop(0, self.heads, one, jnp.zeros((self.share, 128), F32))
            mixture[queries] = mixed.T.astype(BF16)
        each(self.rows, 128, body)

    def product(self, left, weight, back=False):
        target, deep = self.ref("part"), self.chunk

        def produce(at):
            rows = pl.ds(pl.multiple_of(at * deep, deep), deep)
            made = (dot_b if back else dot)(left[rows], weight[...])
            target[at, 0] = made[:deep // 2]
            target[at, 1] = made[deep // 2:]
        return produce

    def halves(self, rows):
        half = self.chunk // 2
        at = lax.div(rows.start, half)
        place = pl.ds(pl.multiple_of(lax.rem(rows.start, half), rows.size), rows.size)
        return self.ref("whole")[lax.div(at, 2), lax.rem(at, 2), place]

    def add_total(self, at):
        residual = self.ref("residual")

        def body(rows):
            residual[rows] = residual[rows] + self.halves(rows)
        each(self.chunk, self.tile, body, at * self.chunk)

    def expand(self, base=0, count=None):
        lifted, weight = self.ref("lifted"), self.ref("w_up")
        hidden, slope = self.ref("hidden"), self.ref("slope")

        def body(rows):
            def inner(columns):
                made, gradient = gelu_both(dot(lifted[rows], weight[:, columns]))
                hidden[rows, columns] = made.astype(BF16)
                slope[rows, columns] = gradient
            each(weight.shape[1], 256, inner)
        each(count or self.rows, 128, body, base)

    def back_hidden(self, branch, base=0, count=None):
        weight, slope, grad = self.ref("w_down"), self.ref("slope"), self.ref("grad_upper")

        def body(rows):
            def inner(columns):
                made = dot_b(branch[rows], weight[columns])
                grad[rows, columns] = (made * slope[rows, columns]).astype(BF16)
            each(weight.shape[0], 256, inner)
        each(count or self.rows, 128, body, base)

    def clear_sums(self):
        sums = self.ref("sums")
        sums[...] = jnp.zeros(sums.shape, F32)

    def norm_back(self, at, first, out):
        unit, scale = self.ref("unit_a" if first else "unit_b"), self.ref(
            "scale_a" if first else "scale_b")
        gain, grad, sums = self.row(0 if first else 2), self.ref("grad"), self.ref("sums")

        def body(rows):
            moved, gains, biases = norm_back(self.halves(rows), unit[rows], scale[rows], gain)
            new = grad[rows] + moved
            grad[rows] = new
            out[rows] = new.astype(BF16)
            sums[0:1] += gains
            sums[1:2] += biases
        each(self.chunk, self.tile, body, at * self.chunk)

    def back_mixture(self, branch, base=0, count=None):
        weight, grad = self.ref("w_out"), self.ref("grad_mixture")

        def body(rows):
            grad[rows] = dot_b(branch[rows], weight[...]).astype(BF16)
        each(count or self.rows, self.chunk, body, base)

    def attend_back(self):
        probs, grad_mixture, grads = self.ref("probs"), self.ref("grad_mixture"), self.ref(
            "grad_qkv")
        key_sum, value_sum = self.ref("key_sum"), self.ref("value_sum")
        share, everything = self.share, pl.ds(0, self.rows)
        key_sum[...] = jnp.zeros(key_sum.shape, F32)
        value_sum[...] = jnp.zeros(value_sum.shape, F32)

        def body(queries):
            query = self.parts(queries)[0]
            unused, key_rows, values = self.parts(everything)
            grad_rows = grad_mixture[queries]

            def one(head, total):
                mask = head_mask(share, self.size, head)
                softmaxed = probs[head, :, queries]
                grad_probs = dot_b(keep(mask, values), grad_rows)
                value_sum[...] += dot(softmaxed.astype(BF16), keep(mask, grad_rows))
                delta = jnp.sum(softmaxed * grad_probs, axis=0, keepdims=True)
                grad_scores = (softmaxed * (grad_probs - delta)).astype(BF16)
                key_sum[...] += dot(grad_scores, keep(mask, query))
                return total + dot_t(keep(mask, key_rows), grad_scores)

            total = lax.fori_loop(0, self.heads, one, jnp.zeros((share, 128), F32))
            grads[queries, 0:share] = (total.T * self.scaling).astype(BF16)
        each(self.rows, 128, body)

        def close(rows):
            grads[rows, share:2 * share] = (key_sum[rows] * self.scaling).astype(BF16)
            grads[rows, 2 * share:3 * share] = value_sum[rows].astype(BF16)
        each(self.rows, 128, close)


def weight_grad(left, right, target):
    if len(target.shape) == 4:
        parts, sides, rows, width = target.shape
        if rows >= 128:
            @pl.loop(0, parts * sides)
            def _(at):
                block = dot_t(left[:, span(at * rows, rows)], right[...])
                target[lax.div(at, sides), lax.rem(at, sides)] = block.astype(BF16)
        else:
            @pl.loop(0, parts)
            def _(at):
                block = dot_t(left[:, span(at * sides * rows, sides * rows)], right[...])
                target[at] = block.reshape(sides, rows, width).astype(BF16)
    else:
        sides, rows, width = target.shape
        if rows >= 128:
            @pl.loop(0, sides)
            def _(at):
                block = dot_t(left[:, span(at * rows, rows)], right[...])
                target[at] = block.astype(BF16)
        else:
            block = dot_t(left[...], right[...])
            target[...] = block.reshape(sides, rows, width).astype(BF16)


def vector_store(target, at, row, whole):
    for owner in range(8):
        block = owner if whole else owner // 2
        target[owner // 2, owner % 2, at:at + 1, :] = row[:, 128 * block:128 * block + 128]


COLUMN_UNITS = ("e_qkv", "e_up", "e_down", "embed", "d_qkv", "d_up")
ROW_UNITS = ("e_out", "d_out", "d_down")
MESSAGES = COLUMN_UNITS + ROW_UNITS
TRADED = ("e_qkv", "e_up", "e_down")
EARLY = ("e_down",)


def unit_shapes(width, dec_width, hidden, dec_hidden):
    return {
        "e_qkv": (width // 8, 3 * width // 4),
        "e_up": (width // 8, hidden // 4),
        "e_down": (hidden // 32, width),
        "embed": (width // 8, dec_width // 4),
        "d_qkv": (dec_width // 8, 3 * dec_width // 4),
        "d_up": (dec_width // 8, dec_hidden // 4),
        "e_out": (width // 8, width),
        "d_out": (dec_width // 8, dec_width),
        "d_down": (dec_hidden // 8, dec_width),
    }


def scratch_table(width, dec_width, hidden, dec_hidden, rows, shown):
    units = unit_shapes(width, dec_width, hidden, dec_hidden)
    table = {}
    for name in COLUMN_UNITS:
        height, columns = units[name]
        if name != "embed":
            table["w_" + name] = ((8 * height, columns), BF16)
        table["g_" + name] = ((PARTS, SIDES, height, columns), BF16)
        table["m_" + name] = ((PARTS, height, columns), BF16)
        table["c_" + name] = ((PARTS, height, columns), BF16)
        if name in TRADED:
            del table["g_" + name]
            table["l_" + name] = ((PARTS, shown, 128), BF16)
            table["r_" + name] = ((shown, columns), BF16)
    table["w_embed"] = ((width, dec_width), BF16)
    for name in ROW_UNITS:
        height, columns = units[name]
        table["w_" + name] = ((2 * height, columns), BF16)
        table["g_" + name] = ((SIDES, height, columns), BF16)
        table["m_" + name] = ((height, columns), BF16)
        table["c_" + name] = ((2, height, columns), BF16)
    table["w_vector"] = ((8 * VECTORS, 128), BF16)
    table["g_vector"] = ((PARTS, SIDES, VECTORS, 128), F32)
    table["m_vector"] = ((PARTS, VECTORS, 128), F32)
    table["c_vector"] = ((PARTS, VECTORS, 128), F32)
    table["gains"] = ((VECTORS, width), F32)
    table["group"] = ((rows, width), BF16)
    table["cotangents"] = ((rows, dec_width), BF16)
    for key, count, wide, deep, heads, size, chunks in (
        ("e_", shown, width, hidden // 4, 4, 64, 2),
        ("d_", rows, dec_width, dec_hidden // 4, 4, 32, 4),
    ):
        share = heads * size
        for name, shape, kind in (
            ("residual", (count, wide), F32), ("unit_a", (count, wide), F32),
            ("unit_b", (count, wide), F32), ("scale_a", (count, 1), F32),
            ("scale_b", (count, 1), F32), ("normed", (count, wide), BF16),
            ("lifted", (count, wide), BF16), ("qkv", (count, 3 * share), BF16),
            ("probs", (heads, count, count), F32), ("mixture", (count, share), BF16),
            ("hidden", (count, deep), BF16), ("slope", (count, deep), F32),
            ("grad_upper", (count, deep), BF16), ("grad", (count, wide), F32),
            ("grad_mixture", (count, share), BF16), ("grad_qkv", (count, 3 * share), BF16),
            ("key_sum", (count, share), F32), ("value_sum", (count, share), F32),
            ("branch", (count, wide), BF16), ("branch_b", (count, wide), BF16),
            ("part", (chunks, 2, count // chunks // 2, wide), F32),
            ("met", (chunks, count // chunks // 2, wide), F32),
            ("out", (chunks, count // chunks // 2, wide), BF16),
            ("came", (2, chunks, count // chunks // 2, wide), BF16),
            ("whole", (chunks, 2, count // chunks // 2, wide), F32),
            ("sums", (8, wide), F32),
        ):
            table[key + name] = (shape, kind)
    table["last_part"] = ((2, 2, rows // 4, dec_width), F32)
    table["last_met"] = ((2, rows // 4, dec_width), F32)
    table["last_out"] = ((rows // 4, dec_width), BF16)
    table["last_came"] = ((rows // 4, dec_width), BF16)
    for name, shape, kind in (
        ("rank_row", (1, rows), jnp.int32), ("rank_column", (rows, 1), jnp.int32),
        ("ids_row", (1, rows), jnp.int32), ("ids_column", (rows, 1), jnp.int32),
        ("packed_row", (1, shown), jnp.int32), ("packed_column", (shown, 1), jnp.int32),
        ("code", (shown, width), F32), ("dec_code", (rows, dec_width), F32),
        ("staged", (VECTORS, 128), F32),
    ):
        table[name] = (shape, kind)
    table["lowered"] = ((shown, width), BF16)
    table["picked"] = ((shown, dec_width), BF16)
    return table


VECTOR_NAMES = (
    "v_gain_a", "v_bias_a", "v_gain_b", "v_bias_b", "v_mask",
    "v_dec_gain_a", "v_dec_bias_a", "v_dec_gain_b", "v_dec_bias_b",
)
INPUTS = ("lengths", "gsd", "visible") + VECTOR_NAMES + (
    "patches", "cotangent", "query", "key", "value", "out", "up", "down", "embed",
    "dec_query", "dec_key", "dec_value", "dec_out", "dec_up", "dec_down",
)
RESULTS = ("decoded", "grad_patches", "grad_vector") + MESSAGES
SEMAPHORES = {
    "local": (40,),
    "z_sent": (10, 2, 4), "z_got": (10, 2, 4), "y_sent": (10, 4), "y_got": (10, 4),
    "gy_sent": (10,), "gy_got": (10,), "gz_sent": (10, 3), "gz_got": (10, 4),
    "f_sent": (3, 5), "f_got": (3, 5),
    "gb_sent": (10, 4), "gb_got": (10, 3),
    "p_sent": (3,), "p_got": (3,), "c_sent": (3,), "c_got": (3,),
    "e_sent": (3,), "e_got": (3,), "t_sent": (8, 4, 3), "t_got": (8, 4, 3),
}


def place_of(ref, positions):
    ids = jnp.zeros(positions.shape, jnp.int32)
    first = jnp.zeros(positions.shape, jnp.int32)
    ratio = jnp.zeros(positions.shape, F32) + ref["gsd"][0, 0]
    end = jnp.int32(0)
    count = ref["lengths"].shape[1]
    for at in range(count - 1):
        end = end + ref["lengths"][0, at]
        later = positions >= end
        ids = ids + later.astype(jnp.int32)
        first = jnp.where(later, end, first)
        ratio = jnp.where(later, ref["gsd"][0, at + 1], ratio)
    return ids, (positions - first).astype(F32) * ratio


def lay_out(ref, rows, shown, width, dec_width):
    ids_row, scaled_row = place_of(ref, lax.broadcasted_iota(jnp.int32, (1, rows), 1))
    ids_column, scaled_column = place_of(ref, lax.broadcasted_iota(jnp.int32, (rows, 1), 0))
    ref["ids_row"][...] = ids_row
    ref["ids_column"][...] = ids_column
    visible = ref["visible"][...] > 0
    marks = jnp.broadcast_to(visible.astype(F32), (16, rows)).astype(BF16)
    down = lax.broadcasted_iota(jnp.int32, (rows, rows), 0)
    along = lax.broadcasted_iota(jnp.int32, (rows, rows), 1)
    until = (along <= down).astype(BF16)
    before = (along < down).astype(BF16)
    count_row = dot_b(marks, until)[0:1]
    rank_row = jnp.where(visible, count_row.astype(jnp.int32) - 1, -1)
    count_column = dot_b(until, marks)[:, 0:1].astype(jnp.int32)
    others = dot_b(before, marks)[:, 0:1].astype(jnp.int32)
    rank_column = jnp.where(count_column > others, others, -1)
    ref["rank_row"][...] = rank_row
    ref["rank_column"][...] = rank_column
    here = lax.broadcasted_iota(jnp.int32, (shown, rows), 0) == rank_row
    packed = jnp.sum(jnp.where(here, ids_row.astype(F32), 0.0), axis=1, keepdims=True)
    ref["packed_column"][...] = packed.astype(jnp.int32)
    packed_scaled = jnp.sum(jnp.where(here, scaled_row, 0.0), axis=1, keepdims=True)
    there = lax.broadcasted_iota(jnp.int32, (rows, shown), 1) == rank_column
    packed = jnp.sum(jnp.where(there, ids_column.astype(F32), 0.0), axis=0, keepdims=True)
    ref["packed_row"][...] = packed.astype(jnp.int32)
    for target, scaled, wide in (
        (ref["code"], packed_scaled, width), (ref["dec_code"], scaled_column, dec_width)
    ):
        half = wide // 2
        steps = lax.broadcasted_iota(jnp.int32, (1, half), 1).astype(F32)
        frequency = jnp.exp(steps * (-math.log(10000.0) / half))
        target[:, 0:1] = scaled
        tall = 16 * 1024 // half

        def body(part):
            angles = target[part, 0:1] * frequency
            made = jnp.concatenate([jnp.sin(angles), jnp.cos(angles)], axis=1)
            target[part] = made
        each(target.shape[0], tall, body)


def main_kernel(names, *refs):
    ref = dict(zip(names, refs))
    s = Split()
    shown, width = ref["code"].shape
    rows, dec_width = ref["dec_code"].shape
    own = ref["patches"].shape[0]
    sem = {name: ref["s_" + name] for name in SEMAPHORES}
    counter = [0]

    def local(source, target):
        at = counter[0]
        counter[0] = at + 1
        return pltpu.make_async_copy(source, target, sem["local"].at[at])

    barrier = pltpu.get_barrier_semaphore()
    peers = [s.z_peer(step) for step in (1, 2, 3)] + [s.y_peer] + list(s.blk_peers)
    for peer in peers:
        pl.semaphore_signal(barrier, inc=1, device_id=peer, device_id_type=pl.DeviceIdType.MESH)

    order = ("vector", "e_qkv", "e_out", "e_up", "embed", "e_down", "d_qkv", "d_out", "d_up",
             "d_down")
    units = {}
    for at, name in enumerate(order):
        sems = tuple(sem[kind].at[at] for kind in ("z_sent", "z_got", "y_sent", "y_got"))
        whole = ref["w_" + name]
        if name == "vector":
            units[name] = Columns(s, whole, VECTORS, [], sems)
        elif name in ROW_UNITS:
            source = ref[{"e_out": "out", "d_out": "dec_out", "d_down": "dec_down"}[name]]
            height = source.shape[0]
            copy = local(source, whole.at[span(s.y * height, height)])
            units[name] = Rows(s, whole, height, copy, sems)
        else:
            height = ref["m_" + name].shape[1]
            mine = span(s.dp * height, height)
            columns = None
            if name in ("e_qkv", "d_qkv"):
                kinds = ("query", "key", "value")
                if name == "d_qkv":
                    kinds = ("dec_query", "dec_key", "dec_value")
                size = ref[kinds[0]].shape[1] // PARTS
                copies = [
                    local(ref[kind].at[:, span(s.part * size, size)],
                          whole.at[mine, pl.ds(place * size, size)])
                    for place, kind in enumerate(kinds)
                ]
            elif name == "e_up":
                size = height
                copies = [
                    local(ref["up"].at[:, span((owner * PARTS + s.blk) * size, size)],
                          whole.at[mine, pl.ds(owner * size, size)])
                    for owner in range(8)
                ]
            elif name == "e_down":
                copies = [local(ref["down"].at[span(s.blk * height, height)], whole.at[mine])]
            elif name == "embed":
                size = dec_width // PARTS
                columns = span(s.part * size, size)
                copies = [local(ref["embed"].at[:, columns], whole.at[mine, columns])]
            else:
                size = ref["dec_up"].shape[1] // PARTS
                copies = [local(ref["dec_up"].at[:, span(s.part * size, size)], whole.at[mine])]
            kind = EarlyColumns if name in EARLY else Columns
            units[name] = kind(s, whole, height, copies, sems, columns)

    sums = {}
    for at, name in enumerate(order):
        sems = tuple(
            sem[kind].at[at]
            for kind in ("gy_sent", "gy_got", "gz_sent", "gz_got", "gb_sent", "gb_got")
        )
        kind = RowSum if name in ROW_UNITS else ProductSum if name in TRADED else ColumnSum
        done = None if name == "vector" else ref["o_" + name]
        wide = ref["m_" + name].shape[-1]
        sums[name] = kind(s, ref.get("g_" + name), ref["m_" + name], ref["c_" + name], done, sems,
                          16 if wide > 512 else 32 if name != "vector" else 8)
    for at, (name, left, right) in enumerate((
        ("e_qkv", "e_normed", "e_grad_qkv"), ("e_up", "e_lifted", "e_grad_upper"),
        ("e_down", "e_hidden", "e_branch"),
    )):
        sums[name].trade(ref[left], ref[right], ref["l_" + name], ref["r_" + name],
                         (sem["f_sent"].at[at], sem["f_got"].at[at]))

    totals = []
    for at in range(7):
        key, slot = ("e_", at % 2) if at in (0, 1, 5, 6) else ("d_", at % 2)
        totals.append(Total(
            s, *(ref[key + name] for name in ("part", "met", "out", "came", "whole")),
            (sem["t_sent"].at[at], sem["t_got"].at[at]), slot,
        ))

    encoder = Block(shown, width, 4, 64, "e_", ref, 0)
    decoder = Block(rows, dec_width, 4, 32, "d_", ref, 5)
    for block, key in ((encoder, "e_"), (decoder, "d_")):
        for short, long in (("w_qkv", "qkv"), ("w_out", "out"), ("w_up", "up"),
                            ("w_down", "down")):
            ref[key + short] = ref["w_" + key + long]

    for name in order:
        units[name].fetch()
    mine = span(s.blk * own, own)
    own_patches = local(ref["patches"], ref["group"].at[mine])
    own_cotangents = local(ref["cotangent"], ref["cotangents"].at[mine])
    own_patches.start()
    own_cotangents.start()
    staged = ref["staged"]
    staged[...] = jnp.zeros(staged.shape, F32)
    for at, name in enumerate(VECTOR_NAMES):
        row = ref[name][...].astype(F32)[None, :]
        staged[at:at + 1, 0:row.shape[1]] = row
    ref["w_vector"][span(s.dp * VECTORS, VECTORS)] = staged[...].astype(BF16)

    pl.semaphore_wait(barrier, len(peers))

    def shares(source, target, kind, which):
        return remote(source, target.at[mine], sem[kind + "_sent"].at[which],
                      sem[kind + "_got"].at[which], s.blk_peers[which])

    def shares_arrival(source, target, kind, which):
        place = span(s.blk_peers[which][1] * own, own)
        return remote(source, target.at[place], sem[kind + "_sent"].at[which],
                      sem[kind + "_got"].at[which], s.blk_peers[which])

    for name in ("vector", "e_qkv", "e_out"):
        units[name].send()
    for which in range(3):
        shares(ref["patches"], ref["group"], "p", which).start()
    for which in range(3):
        shares(ref["cotangent"], ref["cotangents"], "c", which).start()
    units["e_up"].send()

    lay_out(ref, rows, shown, width, dec_width)
    own_patches.wait()
    for which in range(3):
        shares_arrival(ref["patches"], ref["group"], "p", which).wait_recv()

    places = (
        lax.broadcasted_iota(jnp.int32, (shown, rows), 0) == ref["rank_row"][...]
    ).astype(BF16)
    residual = ref["e_residual"]

    def place_patches(columns):
        residual[:, columns] = dot(places, ref["group"][:, columns]) + ref["code"][:, columns]
    each(width, 256, place_patches)

    units["vector"].forward()
    units["vector"].finish()
    vectors = ref["w_vector"][...].astype(F32)
    gains = ref["gains"]
    for at in range(9):
        for owner in range(8):
            row = vectors[VECTORS * owner + at:VECTORS * owner + at + 1, :]
            if at < 4:
                gains[at:at + 1, 128 * owner:128 * owner + 128] = row
            elif owner % 2 == 0:
                pair = VECTORS * (owner + 1) + at
                other = pltpu.roll(vectors[pair:pair + 1, :], 64, 1)
                gains[at:at + 1, 64 * owner:64 * owner + 128] = row + other
    encoder.norm(True)
    units["e_qkv"].forward()
    units["embed"].send()
    units["e_out"].forward()
    units["e_qkv"].finish()
    encoder.project()
    encoder.attend(ref["packed_column"], ref["packed_row"])
    units["e_down"].send()
    units["e_out"].finish()
    totals[0].begin(encoder.product(ref["e_mixture"], ref["w_e_out"]))

    def after_attention(at):
        encoder.add_total(at)
        encoder.norm(False, at * encoder.chunk, encoder.chunk)
    totals[0].finish(after_attention)
    columns = span(s.part * (dec_width // PARTS), dec_width // PARTS)

    def embed_copy(which):
        block = ref["w_embed"].at[:, columns]
        return remote(block, block, sem["e_sent"].at[which], sem["e_got"].at[which],
                      s.blk_peers[which])

    def embed_arrival(which):
        size = dec_width // PARTS
        place = span(lax.rem(3 * s.blk_peers[which][1], PARTS) * size, size)
        block = ref["w_embed"].at[:, place]
        return remote(block, block, sem["e_sent"].at[which], sem["e_got"].at[which],
                      s.blk_peers[which])

    units["e_up"].forward()
    units["e_down"].cross()
    units["embed"].forward()
    units["d_qkv"].send()
    units["e_up"].finish()
    encoder.expand()
    units["embed"].finish()
    for which in range(3):
        embed_copy(which).start()
    for name in ("d_out", "d_up"):
        units[name].send()
    units["e_down"].forward()
    units["d_qkv"].forward()
    units["d_down"].send()
    units["e_down"].finish()
    totals[1].begin(encoder.product(ref["e_hidden"], ref["w_e_down"]))
    units["d_out"].forward()
    for which in range(3):
        embed_arrival(which).wait_recv()
    lowered = ref["lowered"]

    def after_hidden(at):
        encoder.add_total(at)
        part = pl.ds(pl.multiple_of(at * encoder.chunk, encoder.chunk), encoder.chunk)
        lowered[part] = residual[part].astype(BF16)
    totals[1].finish(after_hidden)

    embedded = dot(lowered[...], ref["w_embed"][...])
    high = embedded.astype(BF16)
    low = (embedded - high.astype(F32)).astype(BF16)
    token = gains[4:5, 0:dec_width]
    start = ref["d_residual"]

    def place_rows(part):
        rank = ref["rank_column"][part]
        here = (lax.broadcasted_iota(jnp.int32, (128, shown), 1) == rank).astype(BF16)
        made = jnp.where(rank >= 0, dot(here, high) + dot(here, low), token)
        start[part] = made + ref["dec_code"][part]
    each(rows, 128, place_rows)
    decoder.norm(True)
    units["d_up"].forward()
    units["d_qkv"].finish()
    decoder.project()
    decoder.attend(ref["ids_column"], ref["ids_row"])
    units["d_down"].forward()
    units["d_out"].finish()
    totals[2].begin(decoder.product(ref["d_mixture"], ref["w_d_out"]))
    units["d_up"].finish()
    units["d_down"].finish()
    last_part, last_met = ref["last_part"], ref["last_met"]
    quarter = rows // 4

    def decoder_rest(at):
        decoder.add_total(at)
        decoder.norm(False, at * decoder.chunk, decoder.chunk)
        decoder.expand(at * decoder.chunk, decoder.chunk)
        part = pl.ds(pl.multiple_of(at * quarter, quarter), quarter)
        made = dot(ref["d_hidden"][part], ref["w_d_down"][...])
        last_part[lax.div(at, 2), lax.rem(at, 2)] = made
    totals[2].finish(decoder_rest)
    last_sent, last_got = sem["t_sent"].at[7, 0], sem["t_got"].at[7, 0]
    last_first = remote(last_part.at[:, 1 - s.core], last_met, last_sent.at[0], last_got.at[0],
                        s.core_peer)
    last_second = remote(ref["last_out"], ref["last_came"], last_sent.at[1], last_got.at[1],
                         s.x_peer)
    last_first.start()

    own_cotangents.wait()
    for which in range(3):
        shares_arrival(ref["cotangent"], ref["cotangents"], "c", which).wait_recv()
    cotangents, grad = ref["cotangents"], ref["d_grad"]
    multiply = decoder.product(ref["d_grad_upper"], ref["w_d_up"], back=True)

    def decoder_hidden(at):
        decoder.back_hidden(cotangents, at * decoder.chunk, decoder.chunk)
        multiply(at)
    totals[3].begin(decoder_hidden)
    last_first.wait_recv()

    def last_add(part):
        made = last_part[1 - s.x, s.core, part] + last_met[1 - s.x, part]
        ref["last_out"][part] = made.astype(BF16)
    each(quarter, 64, last_add)
    last_second.start()

    def copy_grad(part):
        grad[part] = cotangents[part].astype(F32)
    each(rows, 64, copy_grad)
    vector_grad = ref["g_vector"]
    vector_grad[...] = jnp.zeros(vector_grad.shape, F32)
    decoder.clear_sums()
    weight_grad(ref["d_hidden"], cotangents, ref["g_d_down"])
    sums["d_down"].start()
    weight_grad(ref["d_lifted"], ref["d_grad_upper"], ref["g_d_up"])
    sums["d_up"].start()

    def decoder_middle(at):
        decoder.norm_back(at, False, ref["d_branch"])
        decoder.back_mixture(ref["d_branch"], at * decoder.chunk, decoder.chunk)
    totals[3].finish(decoder_middle)
    vector_store(vector_grad, 7, ref["d_sums"][0:1], False)
    vector_store(vector_grad, 8, ref["d_sums"][1:2], False)
    decoder.attend_back()
    sums["d_down"].middle()
    totals[4].begin(decoder.product(ref["d_grad_qkv"], ref["w_d_qkv"], back=True))
    sums["d_up"].middle()
    last_second.wait_recv()

    def last_close(part):
        made = last_part[s.x, s.core, part] + last_met[s.x, part]
        before = ref["d_residual"][pl.ds(pl.multiple_of(s.blk * own + part.start, 64), 64)]
        whole = made + ref["last_came"][part].astype(F32) + before
        ref["decoded"][part] = whole.astype(BF16)
    each(quarter, 64, last_close)
    decoder.clear_sums()
    weight_grad(ref["d_normed"], ref["d_grad_qkv"], ref["g_d_qkv"])
    sums["d_qkv"].start()
    weight_grad(ref["d_mixture"], ref["d_branch"], ref["g_d_out"])
    sums["d_out"].start()

    def decoder_first(at):
        decoder.norm_back(at, True, ref["d_branch_b"])
    totals[4].finish(decoder_first)
    picked = ref["picked"]
    picked[...] = dot(places, ref["d_branch_b"][...]).astype(BF16)
    encoder_grad = ref["e_grad"]

    def back_embed(part):
        made = dot_b(picked[...], ref["w_embed"][part])
        encoder_grad[:, part] = made
        ref["e_branch"][:, part] = made.astype(BF16)
    each(width, 256, back_embed)

    sums["e_down"].start()
    encoder.back_hidden(ref["e_branch"])
    sums["e_up"].start()
    totals[5].begin(encoder.product(ref["e_grad_upper"], ref["w_e_up"], back=True))
    sums["d_down"].join()
    sums["e_down"].middle()
    encoder.clear_sums()

    def encoder_middle(at):
        encoder.norm_back(at, False, ref["e_branch_b"])
        encoder.back_mixture(ref["e_branch_b"], at * encoder.chunk, encoder.chunk)
    totals[5].finish(encoder_middle)
    vector_store(vector_grad, 2, ref["e_sums"][0:1], True)
    vector_store(vector_grad, 3, ref["e_sums"][1:2], True)
    sums["e_up"].middle()
    encoder.attend_back()
    sums["e_qkv"].start()
    totals[6].begin(encoder.product(ref["e_grad_qkv"], ref["w_e_qkv"], back=True))
    weight_grad(ref["e_mixture"], ref["e_branch_b"], ref["g_e_out"])
    sums["e_out"].start()
    sums["e_down"].join()
    encoder.clear_sums()
    sums["e_qkv"].middle()

    def encoder_first(at):
        encoder.norm_back(at, True, ref["e_branch_b"])
    totals[6].finish(encoder_first)
    vector_store(vector_grad, 0, ref["e_sums"][0:1], True)
    vector_store(vector_grad, 1, ref["e_sums"][1:2], True)
    vector_store(vector_grad, 5, ref["d_sums"][0:1], False)
    vector_store(vector_grad, 6, ref["d_sums"][1:2], False)

    def mask_sum(at, total):
        part = pl.ds(pl.multiple_of(at * 64, 64), 64)
        hidden_row = ref["rank_column"][part] < 0
        return total + jnp.sum(jnp.where(hidden_row, grad[part], 0.0), axis=0, keepdims=True)
    token_grad = lax.fori_loop(0, rows // 64, mask_sum, jnp.zeros((1, dec_width), F32))
    vector_store(vector_grad, 4, token_grad, False)
    sums["vector"].start()
    embed_columns = picked.at[:, columns]
    weight_grad(lowered, embed_columns, ref["g_embed"])
    sums["embed"].start()
    sums["e_out"].middle()
    for name in ("d_qkv", "d_out"):
        sums[name].middle()
    sums["d_up"].join()
    sums["e_up"].join()
    sums["d_down"].last()
    sums["d_up"].last()
    sums["embed"].middle()
    sums["vector"].middle()
    sums["e_down"].last()

    rank = ref["rank_column"][mine]
    here = (lax.broadcasted_iota(jnp.int32, (own, shown), 1) == rank).astype(BF16)

    def place_grad(part):
        values = encoder_grad[:, part]
        top = values.astype(BF16)
        rest = (values - top.astype(F32)).astype(BF16)
        ref["grad_patches"][:, part] = dot(here, top) + dot(here, rest)
    each(width, 256, place_grad)
    sums["e_qkv"].join()
    sums["d_down"].pass_on()
    sums["d_up"].pass_on()
    sums["e_up"].last()
    sums["e_down"].pass_on()
    for name in ("e_out", "d_qkv", "d_out", "embed", "vector"):
        sums[name].join()
    sums["e_qkv"].last()
    sums["e_up"].pass_on()
    for name in ("e_out", "d_qkv", "d_out", "embed"):
        sums[name].last()

    def vector_out(part, whole):
        ref["grad_vector"][part] = whole
    sums["vector"].total(vector_out)
    sums["vector"].drain()
    for name in ("e_qkv", "e_out", "d_qkv", "d_out", "embed"):
        sums[name].pass_on()
    for name in MESSAGES:
        sums[name].close()
    last_first.wait_send()
    last_second.wait_send()
    for name in order:
        units[name].drain()
    for which in range(3):
        shares(ref["patches"], ref["group"], "p", which).wait_send()
        shares(ref["cotangent"], ref["cotangents"], "c", which).wait_send()
        embed_copy(which).wait_send()


def unpack_kernel(names, *refs):
    ref = dict(zip(names, refs))
    side = lax.rem(lax.axis_index("dp"), 2)
    ref["decoded"][...] = ref["i_decoded"][...]
    ref["grad_patches"][...] = ref["i_grad_patches"][...]
    vectors = ref["i_grad_vector"][...]
    for at, name in enumerate(("e_gain_a", "e_bias_a", "e_gain_b", "e_bias_b")):
        ref[name][...] = vectors[at:at + 1, :]
    for at, name in enumerate(("mask", "d_gain_a", "d_bias_a", "d_gain_b", "d_bias_b")):
        row = vectors[at + 4:at + 5, :]
        ref[name][...] = jnp.where(side == 0, row[:, 0:64], row[:, 64:128])
    for blk in range(PARTS):
        part = 3 * blk % PARTS
        for key in ("e_", "d_"):
            size = ref[key + "query"].shape[1] // PARTS
            for place, kind in enumerate(("query", "key", "value")):
                ref[key + kind][:, part * size:(part + 1) * size] = ref["i_" + key + "qkv"][
                    blk, :, place * size:(place + 1) * size].astype(F32)
        size = ref["i_e_up"].shape[1]
        for owner in range(8):
            column = (owner * PARTS + blk) * size
            ref["e_up"][:, column:column + size] = ref["i_e_up"][
                blk, :, owner * size:(owner + 1) * size].astype(F32)
        size = ref["i_e_down"].shape[1]
        ref["e_down"][blk * size:(blk + 1) * size, :] = ref["i_e_down"][blk].astype(F32)
        for name in ("embed", "d_up"):
            size = ref["i_" + name].shape[2]
            ref[name][:, part * size:(part + 1) * size] = ref["i_" + name][blk].astype(F32)
    for name in ROW_UNITS:
        ref[name][...] = ref["i_" + name][...].astype(F32)


def local_kernel(*arguments):
    (patches, lengths, gsd_scale, visible,
     e_gain_a, e_bias_a, e_query, e_key, e_value, e_out, e_gain_b, e_bias_b, e_up, e_down,
     embed, mask,
     d_gain_a, d_bias_a, d_query, d_key, d_value, d_out, d_gain_b, d_bias_b, d_up, d_down,
     cotangent) = arguments
    width, dec_width = patches.shape[1], cotangent.shape[1]
    hidden, dec_hidden = e_up.shape[1], d_up.shape[1]
    rows = visible.shape[1]
    inputs = {
        "lengths": lengths, "gsd": gsd_scale, "visible": visible,
        "patches": patches, "cotangent": cotangent,
        "query": e_query, "key": e_key, "value": e_value, "out": e_out, "up": e_up,
        "down": e_down, "embed": embed, "dec_query": d_query, "dec_key": d_key,
        "dec_value": d_value, "dec_out": d_out, "dec_up": d_up, "dec_down": d_down,
    }
    inputs.update(zip(VECTOR_NAMES, (
        e_gain_a, e_bias_a, e_gain_b, e_bias_b, mask, d_gain_a, d_bias_a, d_gain_b, d_bias_b)))
    units = unit_shapes(width, dec_width, hidden, dec_hidden)
    shapes = {
        "decoded": (cotangent.shape, BF16), "grad_patches": (patches.shape, F32),
        "grad_vector": ((VECTORS, 128), F32),
    }
    for name in COLUMN_UNITS:
        shapes[name] = ((PARTS,) + units[name], BF16)
    for name in ROW_UNITS:
        shapes[name] = (units[name], BF16)
    table = scratch_table(width, dec_width, hidden, dec_hidden, rows, SHOWN)
    names = INPUTS + tuple("o_" + name if name in MESSAGES else name for name in RESULTS)
    names = names + tuple(table) + tuple("s_" + name for name in SEMAPHORES)
    spaces = {"lengths": pltpu.SMEM, "gsd": pltpu.SMEM, "visible": pltpu.VMEM}
    spaces.update({name: pltpu.VMEM for name in VECTOR_NAMES})
    results = pl.pallas_call(
        functools.partial(main_kernel, names),
        out_shape=[jax.ShapeDtypeStruct(*shapes[name]) for name in RESULTS],
        in_specs=[pl.BlockSpec(memory_space=spaces.get(name, pl.ANY)) for name in INPUTS],
        out_specs=[
            pl.BlockSpec(memory_space=pl.ANY if name in MESSAGES else pltpu.VMEM)
            for name in RESULTS
        ],
        scratch_shapes=[pltpu.VMEM(*entry) for entry in table.values()]
        + [pltpu.SemaphoreType.DMA(shape) for shape in SEMAPHORES.values()],
        compiler_params=pltpu.CompilerParams(
            collective_id=0, has_side_effects=True, vmem_limit_bytes=62 * MIB
        ),
    )(*(inputs[name] for name in INPUTS))
    made = {"i_" + name: result for name, result in zip(RESULTS, results)}
    finals = {
        "decoded": (cotangent.shape, BF16), "grad_patches": (patches.shape, F32),
    }
    for key, wide, deep in (("e_", width, hidden), ("d_", dec_width, dec_hidden)):
        small, tall = wide // 8, deep // 8
        if key == "d_":
            finals["embed"] = ((width // 8, dec_width), F32)
            finals["mask"] = ((1, small), F32)
        for name, shape in (
            ("gain_a", (1, small)), ("bias_a", (1, small)), ("query", (small, wide)),
            ("key", (small, wide)), ("value", (small, wide)), ("out", (small, wide)),
            ("gain_b", (1, small)), ("bias_b", (1, small)), ("up", (small, deep)),
            ("down", (tall, wide)),
        ):
            finals[key + name] = (shape, F32)
    outputs = pl.pallas_call(
        functools.partial(unpack_kernel, tuple(made) + tuple(finals)),
        out_shape=[jax.ShapeDtypeStruct(*entry) for entry in finals.values()],
        in_specs=[pl.BlockSpec(memory_space=pltpu.VMEM)] * len(made),
        out_specs=[pl.BlockSpec(memory_space=pltpu.VMEM)] * len(finals),
        compiler_params=pltpu.CompilerParams(vmem_limit_bytes=62 * MIB),
    )(*made.values())
    return tuple(
        output.reshape(-1) if output.shape[0] == 1 else output for output in outputs
    )


def solution(mesh):
    both, vec, mat = P(("dp", "blk"), None), P("dp"), P("dp", None)
    block = (vec, vec, mat, mat, mat, mat, vec, vec, mat, mat)
    in_specs = (both, mat, mat, mat) + block + (mat, vec) + block + (both,)
    out_specs = (both, both) + block + (mat, vec) + block
    body = local_kernel if mesh.shape["dp"] == 8 and mesh.shape["blk"] == 4 else local
    return jax.shard_map(body, mesh=mesh, in_specs=in_specs, out_specs=out_specs, check_vma=False)
```

```python
import functools
import math

import jax
import jax.numpy as jnp
from jax import lax
from jax.experimental import pallas as pl
from jax.experimental.pallas import tpu as pltpu
from jax.sharding import PartitionSpec as P

HEADS = 16
EPSILON = 1e-06
MASKED_SCORE = -1e30
F32 = jnp.float32
BF16 = jnp.bfloat16


def dot(left, right):
    return lax.dot_general(left, right, (((1,), (0,)), ((), ())), preferred_element_type=F32)


def dot_t(left, right):
    return lax.dot_general(left, right, (((0,), (0,)), ((), ())), preferred_element_type=F32)


def dot_b(left, right):
    return lax.dot_general(left, right, (((1,), (1,)), ((), ())), preferred_element_type=F32)


def sincos(scaled, width):
    half_width = width // 2
    frequency = jnp.exp(
        jnp.arange(half_width, dtype=F32) * (-math.log(10000.0) / half_width)
    )
    angles = scaled[:, None] * frequency[None, :]
    return jnp.concatenate([jnp.sin(angles), jnp.cos(angles)], axis=1)


def norm_parts(values):
    center = values - jnp.mean(values, axis=-1, keepdims=True)
    spread = jnp.mean(center * center, axis=-1, keepdims=True)
    scale = lax.rsqrt(spread + EPSILON)
    return center * scale, scale


def norm_back(grad, unit, scale, gain):
    grad_gain = jnp.sum(grad * unit, axis=0, keepdims=True)
    grad_bias = jnp.sum(grad, axis=0, keepdims=True)
    inner = grad * gain
    mean_inner = jnp.mean(inner, axis=-1, keepdims=True)
    mean_cross = jnp.mean(inner * unit, axis=-1, keepdims=True)
    return scale * (inner - mean_inner - unit * mean_cross), grad_gain, grad_bias


def gelu_both(upper):
    phi = 0.5 * (1.0 + lax.erf(upper * math.sqrt(0.5)))
    density = jnp.exp(-0.5 * upper * upper) * (1.0 / math.sqrt(2.0 * math.pi))
    return upper * phi, phi + upper * density


def head_forward(queries, key_rows, values, allowed, scaling):
    scores = jnp.where(allowed, dot_b(queries, key_rows) * scaling, MASKED_SCORE)
    largest = jnp.max(scores, axis=-1, keepdims=True)
    exponent = jnp.exp(scores - largest)
    softmaxed = exponent / jnp.sum(exponent, axis=-1, keepdims=True)
    return softmaxed, dot(softmaxed.astype(BF16), values).astype(BF16)


def head_backward(queries, key_rows, values, softmaxed, grad_mixture, scaling):
    grad_values = dot_t(softmaxed.astype(BF16), grad_mixture).astype(BF16)
    grad_probs = dot_b(grad_mixture, values)
    delta = jnp.sum(softmaxed * grad_probs, axis=-1, keepdims=True)
    grad_scores = (softmaxed * (grad_probs - delta)).astype(BF16)
    grad_queries = (dot(grad_scores, key_rows) * scaling).astype(BF16)
    grad_keys = (dot_t(grad_scores, queries) * scaling).astype(BF16)
    return grad_queries, grad_keys, grad_values


def block_forward(residual, params, heads, allowed, total):
    gain_a, bias_a, w_query, w_key, w_value, w_out, gain_b, bias_b, w_up, w_down = params
    unit_a, scale_a = norm_parts(residual)
    normed = (unit_a * gain_a + bias_a).astype(BF16)
    queries = dot(normed, w_query).astype(BF16)
    key_rows = dot(normed, w_key).astype(BF16)
    values = dot(normed, w_value).astype(BF16)
    size = queries.shape[1] // heads
    scaling = 1.0 / math.sqrt(size)
    probs, mixed = [], []
    for head in range(heads):
        part = slice(head * size, (head + 1) * size)
        softmaxed, mixture = head_forward(
            queries[:, part], key_rows[:, part], values[:, part], allowed, scaling
        )
        probs.append(softmaxed)
        mixed.append(mixture)
    mixture = jnp.concatenate(mixed, axis=1)
    middle = residual + total(dot(mixture, w_out))
    unit_b, scale_b = norm_parts(middle)
    lifted = (unit_b * gain_b + bias_b).astype(BF16)
    hidden, slope = gelu_both(dot(lifted, w_up))
    hidden = hidden.astype(BF16)
    result = middle + total(dot(hidden, w_down))
    return result, (
        unit_a, scale_a, normed, queries, key_rows, values, probs, mixture,
        unit_b, scale_b, lifted, slope, hidden,
    )


def block_backward(grad_result, params, heads, saved, total):
    gain_a, bias_a, w_query, w_key, w_value, w_out, gain_b, bias_b, w_up, w_down = params
    (unit_a, scale_a, normed, queries, key_rows, values, probs, mixture,
     unit_b, scale_b, lifted, slope, hidden) = saved
    size = queries.shape[1] // heads
    scaling = 1.0 / math.sqrt(size)
    grad_branch = grad_result.astype(BF16)
    grad_down = dot_t(hidden, grad_branch)
    grad_upper = (dot_b(grad_branch, w_down) * slope).astype(BF16)
    grad_up = dot_t(lifted, grad_upper)
    grad_lifted = total(dot_b(grad_upper, w_up))
    grad_in, grad_gain_b, grad_bias_b = norm_back(grad_lifted, unit_b, scale_b, gain_b)
    grad_middle = grad_result + grad_in
    grad_attention = grad_middle.astype(BF16)
    grad_out = dot_t(mixture, grad_attention)
    grad_mixture = dot_b(grad_attention, w_out).astype(BF16)
    pieces = []
    for head in range(heads):
        part = slice(head * size, (head + 1) * size)
        pieces.append(
            head_backward(
                queries[:, part], key_rows[:, part], values[:, part], probs[head],
                grad_mixture[:, part], scaling,
            )
        )
    grad_queries, grad_keys, grad_values = (
        jnp.concatenate([piece[at] for piece in pieces], axis=1) for at in range(3)
    )
    grad_normed = total(
        dot_b(grad_queries, w_query) + dot_b(grad_keys, w_key) + dot_b(grad_values, w_value)
    )
    grad_in, grad_gain_a, grad_bias_a = norm_back(grad_normed, unit_a, scale_a, gain_a)
    return grad_middle + grad_in, (
        grad_gain_a, grad_bias_a, dot_t(normed, grad_queries), dot_t(normed, grad_keys),
        dot_t(normed, grad_values), grad_out, grad_gain_b, grad_bias_b, grad_up, grad_down,
    )


def layout(lengths_row, gsd_row, visible_row):
    count = visible_row.shape[0]
    positions = jnp.arange(count, dtype=jnp.int32)
    image_ends = jnp.cumsum(lengths_row)
    image_starts = image_ends - lengths_row
    image_ids = jnp.sum((positions[:, None] >= image_ends[None, :]).astype(jnp.int32), axis=1)
    onehot = image_ids[:, None] == jnp.arange(lengths_row.shape[0], dtype=jnp.int32)[None, :]
    first_row = jnp.sum(jnp.where(onehot, image_starts[None, :], 0), axis=1)
    ratio = jnp.sum(jnp.where(onehot, gsd_row[None, :], 0.0), axis=1)
    scaled = (positions - first_row).astype(F32) * ratio
    shown = visible_row > 0
    earlier = (positions[None, :] <= positions[:, None]) & shown[None, :]
    rank = jnp.where(shown, jnp.sum(earlier.astype(jnp.int32), axis=1) - 1, -1)
    return image_ids, scaled, rank


def spread_rows(grad, rank, offset, rows):
    own = lax.dynamic_slice_in_dim(rank, offset, rows)
    place = (own[:, None] == jnp.arange(grad.shape[0], dtype=jnp.int32)[None, :]).astype(BF16)
    high = grad.astype(BF16)
    low = (grad - high.astype(F32)).astype(BF16)
    return dot(place, high) + dot(place, low)


SHOWN = 128


def local(*arguments):
    patches, lengths, gsd_scale, visible = arguments[:4]
    encoder_shards = arguments[4:14]
    embed_shard, mask_shard = arguments[14:16]
    decoder_shards = arguments[16:26]
    cotangent = arguments[26]
    dp_count = lax.axis_size("dp")
    blk_count = lax.axis_size("blk")
    blk = lax.axis_index("blk")
    dp = lax.axis_index("dp")
    rows = patches.shape[0]
    offset = blk * rows
    heads = HEADS // blk_count
    image_ids, scaled, rank = layout(lengths[0], gsd_scale[0], visible[0])
    shown = rank >= 0
    places = rank[None, :] == jnp.arange(SHOWN, dtype=jnp.int32)[:, None]
    packed_ids = jnp.sum(jnp.where(places, image_ids[None, :], 0), axis=1)
    packed_scaled = jnp.sum(jnp.where(places, scaled[None, :], 0.0), axis=1)

    def gather(shard):
        return lax.all_gather(shard, "dp", axis=0, tiled=True)

    def by_columns(shard):
        width = shard.shape[1] // blk_count
        return gather(lax.dynamic_slice_in_dim(shard, blk * width, width, axis=1))

    def by_rows(shard):
        whole = gather(shard)
        height = whole.shape[0] // blk_count
        return lax.dynamic_slice_in_dim(whole, blk * height, height, axis=0)

    def vector(shard):
        return gather(shard).astype(F32)[None, :]

    def load(shards):
        kinds = (vector, vector, by_columns, by_columns, by_columns, by_rows,
                 vector, vector, by_columns, by_rows)
        return tuple(kind(shard) for kind, shard in zip(kinds, shards))

    def total(partial):
        return lax.psum(partial, "blk")

    def sum_columns(grad):
        summed = lax.psum_scatter(grad.astype(BF16), "dp", scatter_dimension=0, tiled=True)
        return lax.all_gather(summed, "blk", axis=1, tiled=True).astype(F32)

    def sum_rows(grad):
        whole = lax.all_gather(grad.astype(BF16), "blk", axis=0, tiled=True)
        return lax.psum_scatter(whole, "dp", scatter_dimension=0, tiled=True).astype(F32)

    def sum_vector(grad):
        return lax.psum_scatter(grad[0], "dp", scatter_dimension=0, tiled=True)

    def reduce(grads):
        kinds = (sum_vector, sum_vector, sum_columns, sum_columns, sum_columns, sum_rows,
                 sum_vector, sum_vector, sum_columns, sum_rows)
        return tuple(kind(grad) for kind, grad in zip(kinds, grads))

    group = lax.all_gather(patches, "blk", axis=0, tiled=True)
    picked = dot(places.astype(BF16), group)
    encoder = load(encoder_shards)
    residual = picked + sincos(packed_scaled, patches.shape[1])
    encoded, encoder_saved = block_forward(
        residual, encoder, heads, packed_ids[:, None] == packed_ids[None, :], total
    )
    embed = gather(embed_shard)
    lowered = encoded.astype(BF16)
    embedded = dot(lowered, embed)
    high = embedded.astype(BF16)
    low = (embedded - high.astype(F32)).astype(BF16)
    places_b = places.astype(BF16)
    start = jnp.where(
        shown[:, None], dot_t(places_b, high) + dot_t(places_b, low), vector(mask_shard)
    ) + sincos(scaled, embed.shape[1])
    decoder = load(decoder_shards)
    decoded, decoder_saved = block_forward(
        start, decoder, heads, image_ids[:, None] == image_ids[None, :], total
    )
    decoded_rows = lax.dynamic_slice_in_dim(decoded, offset, rows).astype(BF16)
    grad_out = lax.all_gather(cotangent, "blk", axis=0, tiled=True).astype(F32)
    grad_start, decoder_grads = block_backward(grad_out, decoder, heads, decoder_saved, total)
    grad_mask = jnp.sum(jnp.where(shown[:, None], 0.0, grad_start), axis=0, keepdims=True)
    grad_embedded = dot(places_b, grad_start.astype(BF16)).astype(BF16)
    width = embed.shape[1] // blk_count
    grad_embed = dot_t(
        lowered, lax.dynamic_slice_in_dim(grad_embedded, blk * width, width, axis=1)
    )
    grad_encoded = dot_b(grad_embedded, embed)
    grad_residual, encoder_grads = block_backward(
        grad_encoded, encoder, heads, encoder_saved, total
    )
    grad_patches = spread_rows(grad_residual, rank, offset, rows)
    return (
        (decoded_rows, grad_patches) + reduce(encoder_grads)
        + (sum_columns(grad_embed), sum_vector(grad_mask)) + reduce(decoder_grads)
    )


MIB = 2**20
DECODER_ROWS = 512
PARTS = 4
SIDES = 2
VECTORS = 16


class Split:
    def __init__(self):
        self.dp = lax.axis_index("dp")
        self.blk = lax.axis_index("blk")
        self.z = lax.div(self.dp, 2)
        self.y = lax.rem(self.dp, 2)
        self.x = lax.div(self.blk, 2)
        self.core = lax.rem(self.blk, 2)
        self.part = lax.rem(3 * self.blk, PARTS)
        self.y_peer = (self.z * 2 + 1 - self.y, self.blk)
        self.core_peer = (self.dp, self.x * 2 + 1 - self.core)
        self.x_peer = (self.dp, (1 - self.x) * 2 + self.core)
        self.far_peer = (self.dp, (1 - self.x) * 2 + 1 - self.core)
        self.blk_peers = (self.core_peer, self.x_peer, self.far_peer)

    def ahead(self, step):
        return lax.rem(self.z + step, PARTS)

    def behind(self, step):
        return lax.rem(self.z + PARTS - step, PARTS)

    def z_peer(self, step):
        return (self.ahead(step) * 2 + self.y, self.blk)

    def at_z(self, z):
        return (z * 2 + self.y, self.blk)

    def inward(self, step):
        high = lax.div(self.z, 2)
        return lax.rem(self.z + high * (PARTS - step) + (1 - high) * step, PARTS)

    @property
    def inner(self):
        return jnp.logical_or(self.z == 1, self.z == 2)

    @property
    def near_end(self):
        return jnp.where(self.inner, 3 * self.z - 3, lax.div(self.z, 3) + 1)

    @property
    def far_end(self):
        return 6 - 3 * self.z


def remote(source, target, sent, received, device):
    return pltpu.make_async_remote_copy(
        src_ref=source, dst_ref=target, send_sem=sent, recv_sem=received,
        device_id=device, device_id_type=pl.DeviceIdType.MESH,
    )


def span(at, size):
    return pl.ds(pl.multiple_of(at, size), size)


class Columns:
    def __init__(self, split, whole, rows, local, sems, columns=None):
        self.split, self.whole, self.rows, self.local = split, whole, rows, local
        self.columns = columns
        self.z_sent, self.z_got, self.y_sent, self.y_got = sems[:4]
        self.cross_sent, self.cross_got = sems[4:]

    def view(self, rows):
        if self.columns is None:
            return self.whole.at[rows]
        return self.whole.at[rows, self.columns]

    def block(self, z, y):
        return self.view(span((z * 2 + y) * self.rows, self.rows))

    def lane(self, crossed):
        s = self.split
        if crossed:
            return 1 - s.y, self.cross_sent, self.cross_got
        return s.y, self.z_sent, self.z_got

    def z_copy(self, step, crossed=False):
        s = self.split
        y, sent, got = self.lane(crossed)
        block = self.block(s.z, y)
        return remote(block, block, sent, got.at[s.z], s.at_z(s.inward(step)))

    def z_arrival(self, z, crossed=False):
        y, sent, got = self.lane(crossed)
        block = self.block(z, y)
        return remote(block, block, sent, got.at[z], self.split.y_peer)

    def relay(self, crossed=False):
        s = self.split
        y, sent, got = self.lane(crossed)
        block = self.block(s.far_end, y)
        return remote(block, block, sent, got.at[s.far_end], s.at_z(s.near_end))

    def y_copy(self, z, at):
        s = self.split
        block = self.block(z, s.y)
        return remote(block, block, self.y_sent, self.y_got.at[at], s.y_peer)

    def y_arrival(self, z, at):
        s = self.split
        block = self.block(z, 1 - s.y)
        return remote(block, block, self.y_sent, self.y_got.at[at], s.y_peer)

    def sent(self, sem, count):
        blocks = self.view(pl.ds(0, count * self.rows))
        remote(blocks, blocks, sem, self.y_got.at[0], self.split.y_peer).wait_send()

    def fetch(self):
        for copy in self.local:
            copy.start()

    def spread(self, crossed=False):
        self.z_copy(1, crossed).start()
        self.z_copy(2, crossed).start()

        @pl.when(self.split.inner)
        def _():
            self.z_copy(3, crossed).start()

    def collect(self, step, crossed=False):
        s = self.split
        z = s.inward(step)
        self.z_arrival(z, crossed).wait_recv()
        if step == 2:
            @pl.when(s.inner)
            def _():
                self.relay(crossed).start()
        return z

    def send(self, y_too=True):
        for copy in self.local:
            copy.wait()
        self.spread()
        if y_too:
            self.send_y()

    def send_y(self):
        self.y_copy(self.split.z, 0).start()

    def forward(self, steps=(1, 2, 3)):
        for step in steps:
            self.y_copy(self.collect(step), step).start()

    def finish(self):
        for step in range(PARTS):
            self.y_arrival(self.split.inward(step), step).wait_recv()

    def drain_z(self, sem):
        @pl.when(self.split.inner)
        def _():
            self.sent(sem, 4)

        @pl.when(jnp.logical_not(self.split.inner))
        def _():
            self.sent(sem, 2)

    def drain(self):
        self.drain_z(self.z_sent)
        self.sent(self.y_sent, PARTS)


class EarlyColumns(Columns):
    def cross(self):
        s = self.split
        self.y_arrival(s.z, 0).wait_recv()
        self.spread(True)

    def forward(self, steps=(1, 2, 3)):
        for step in steps:
            self.collect(step)

    def finish(self, steps=(1, 2, 3)):
        for step in steps:
            self.collect(step, True)

    def drain(self):
        self.drain_z(self.z_sent)
        self.drain_z(self.cross_sent)
        self.sent(self.y_sent, 1)


class Shared:
    def __init__(self, split, source, block, sems):
        self.split, self.source, self.block = split, source, block
        self.sents, self.gots = sems

    def copy(self, which):
        s = self.split
        if which == 2:
            block = self.block(s.x_peer[1])
            return remote(block, block, self.sents.at[2], self.gots.at[2], s.core_peer)
        return remote(self.source, self.block(s.blk), self.sents.at[which],
                      self.gots.at[which], s.blk_peers[which])

    def arrival(self, which):
        s = self.split
        block = self.block(s.blk_peers[which][1])
        return remote(block, block, self.sents.at[which], self.gots.at[which], s.core_peer)

    def start(self):
        self.copy(1).start()
        self.copy(0).start()

    def pass_on(self):
        self.arrival(1).wait_recv()
        self.copy(2).start()

    def finish(self):
        self.arrival(0).wait_recv()
        self.arrival(2).wait_recv()

    def drain(self):
        for which in range(3):
            self.copy(which).wait_send()


class Rows:
    def __init__(self, split, whole, rows, local, sems):
        self.split, self.whole, self.rows, self.local = split, whole, rows, local
        self.z_sent, self.z_got, self.y_sent, self.y_got = sems[:4]

    def block(self, y):
        return self.whole.at[span(y * self.rows, self.rows)]

    def z_copy(self, way):
        s = self.split
        return remote(self.block(s.y), self.block(s.y), self.z_got.at[1 + way],
                      self.z_got.at[0], s.at_z(s.z + 1 - 2 * way))

    def pass_on(self, act):
        s = self.split

        @pl.when(jnp.logical_and(s.z >= s.part, s.z < PARTS - 1))
        def _():
            act(self.z_copy(0))

        @pl.when(jnp.logical_and(s.z <= s.part, s.z > 0))
        def _():
            act(self.z_copy(1))

    def y_copy(self):
        s = self.split
        return remote(self.block(s.y), self.block(s.y), self.y_sent,
                      self.y_got.at[0], s.y_peer)

    def fetch(self):
        @pl.when(self.split.z == self.split.part)
        def _():
            self.local.start()

    def send(self):
        @pl.when(self.split.z == self.split.part)
        def _():
            self.local.wait()
            self.pass_on(lambda copy: copy.start())
            self.y_copy().start()

    def forward(self):
        s = self.split

        @pl.when(s.z != s.part)
        def _():
            remote(self.block(s.y), self.block(s.y), self.z_sent,
                   self.z_got.at[0], s.y_peer).wait_recv()
            self.pass_on(lambda copy: copy.start())
            self.y_copy().start()

    def finish(self):
        s = self.split
        block = self.block(1 - s.y)
        remote(block, block, self.y_sent, self.y_got.at[0], s.y_peer).wait_recv()

    def drain(self):
        self.pass_on(lambda copy: copy.wait_send())
        self.y_copy().wait_send()


def each(count, step, body, base=0):
    @pl.loop(0, count // step)
    def _(at):
        body(pl.ds(pl.multiple_of(base + at * step, step), step))


class ColumnSum:
    def __init__(self, split, grad, met, came, done, sems, step):
        self.split, self.grad, self.met, self.came, self.done = split, grad, met, came, done
        self.y_sent, self.y_got, self.z_sent, self.z_got, self.b_sent, self.b_got = sems
        self.step = step

    def y_copy(self):
        s = self.split
        return remote(self.grad.at[:, 1 - s.y], self.met, self.y_sent, self.y_got, s.y_peer)

    def z_copy(self, step):
        s = self.split
        target = s.inward(step)
        return remote(self.met.at[target], self.came.at[s.z], self.z_sent.at[step - 1],
                      self.z_got.at[s.z], s.at_z(target))

    def z_arrival(self, z):
        s = self.split
        return remote(self.met.at[z], self.came.at[z], self.z_sent.at[0], self.z_got.at[z],
                      s.y_peer)

    def relay(self):
        s = self.split
        return remote(self.met.at[3 - s.z], self.came.at[s.near_end], self.z_sent.at[2],
                      self.z_got.at[s.near_end], s.at_z(s.near_end))

    def b_copy(self, which):
        s = self.split
        if which == 2:
            block = self.done.at[s.x_peer[1]]
            return remote(block, block, self.b_sent.at[2], self.b_got.at[2], s.core_peer)
        return remote(self.met.at[s.z], self.done.at[s.blk], self.b_sent.at[which],
                      self.b_got.at[which], s.blk_peers[which])

    def b_arrival(self, which):
        s = self.split
        block = self.done.at[s.blk_peers[which][1]]
        return remote(block, block, self.b_sent.at[which], self.b_got.at[which],
                      s.blk_peers[which])

    def own_copy(self):
        s = self.split
        return pltpu.make_async_copy(self.met.at[s.z], self.done.at[s.blk], self.b_sent.at[3])

    def start(self):
        self.y_copy().start()

    def add(self, z):
        def body(rows):
            both = self.grad[z, self.split.y, rows].astype(F32) + self.met[z, rows].astype(F32)
            self.met[z, rows] = both.astype(self.met.dtype)
        each(self.met.shape[1], self.step, body)

    def arrive(self):
        self.y_copy().wait_recv()

    def middle(self):
        s = self.split
        self.arrive()

        @pl.when(s.inner)
        def _():
            self.add(s.inward(1))
            self.z_copy(1).start()
            self.add(s.inward(3))
            self.z_copy(3).start()
            self.add(s.inward(2))

        @pl.when(jnp.logical_not(s.inner))
        def _():
            self.add(3 - s.z)
            self.relay().start()
            self.add(s.inward(2))
            self.z_copy(2).start()
            self.add(s.inward(1))
            self.z_copy(1).start()
        self.add(s.z)

    def join(self):
        s = self.split

        @pl.when(s.inner)
        def _():
            target = s.inward(2)
            self.z_arrival(s.z).wait_recv()

            def body(rows):
                both = self.met[target, rows].astype(F32) + self.came[s.z, rows].astype(F32)
                self.met[target, rows] = both.astype(self.met.dtype)
            each(self.met.shape[1], self.step, body)
            self.z_copy(2).start()

    def total(self, store):
        s = self.split

        @pl.when(s.inner)
        def _():
            sources = (0, 3, 3 - s.z)
            for z in sources:
                self.z_arrival(z).wait_recv()

            def body(rows):
                whole = self.met[s.z, rows].astype(F32)
                for z in sources:
                    whole = whole + self.came[z, rows].astype(F32)
                store(rows, whole)
            each(self.met.shape[1], self.step, body)

        @pl.when(jnp.logical_not(s.inner))
        def _():
            for z in (1, 2):
                self.z_arrival(z).wait_recv()

            def body(rows):
                whole = self.met[s.z, rows].astype(F32)
                for z in (1, 2):
                    whole = whole + self.came[z, rows].astype(F32)
                store(rows, whole)
            each(self.met.shape[1], self.step, body)

    def last(self):
        s = self.split

        def store(rows, whole):
            self.met[s.z, rows] = whole.astype(self.met.dtype)
        self.total(store)
        self.b_copy(1).start()
        self.b_copy(0).start()
        self.own_copy().start()

    def pass_on(self):
        self.b_arrival(1).wait_recv()
        self.b_copy(2).start()

    def close(self):
        self.b_arrival(0).wait_recv()
        self.b_arrival(2).wait_recv()
        for which in range(3):
            self.b_copy(which).wait_send()
        self.own_copy().wait()
        self.drain()

    def drain_y(self):
        self.y_copy().wait_send()

    def drain(self):
        self.drain_y()
        for step in (1, 2, 3):
            self.z_copy(step).wait_send()


class ProductSum(ColumnSum):
    def trade(self, left, right, their_left, their_right, sems, told=None, heard=None, after=None):
        self.left, self.right = left, right
        self.their_left, self.their_right = their_left, their_right
        self.told = right if told is None else told
        self.heard = their_right if heard is None else heard
        self.tells = told is not False
        self.after = after
        self.t_sent, self.t_got = sems
        self.width = their_left.shape[2]

    def columns(self, z, y):
        return self.left.at[:, span((z * 2 + y) * self.width, self.width)]

    def left_copy(self, z):
        s = self.split
        return remote(self.columns(z, 1 - s.y), self.their_left.at[z], self.t_sent.at[0],
                      self.t_got.at[0], s.y_peer)

    def left_copies(self):
        return remote(self.their_left, self.their_left, self.t_sent.at[0], self.t_got.at[0],
                      self.split.y_peer)

    def right_copy(self):
        return remote(self.told, self.heard, self.t_sent.at[1], self.t_got.at[1],
                      self.split.y_peer)

    def start_left(self):
        for z in range(PARTS):
            self.left_copy(z).start()

    def start(self):
        self.right_copy().start()

    def add(self, z):
        both = dot_t(self.columns(z, self.split.y)[...], self.right[...]) + dot_t(
            self.their_left[z], self.their_right[...])
        self.met[z] = both.astype(self.met.dtype)

    def arrive(self):
        self.left_copies().wait_recv()
        if self.tells:
            self.right_copy().wait_recv()
        if self.after is not None:
            self.after()

    def drain_y(self):
        self.left_copies().wait_send()
        if self.tells:
            self.right_copy().wait_send()


class RowSum:
    def __init__(self, split, grad, met, came, done, sems, step):
        self.split, self.grad, self.met, self.came, self.done = split, grad, met, came, done
        self.y_sent, self.y_got, self.z_sent, self.z_got, self.b_sent, self.b_got = sems
        self.step = step
        s = split
        self.home = lax.rem(3 * s.z, PARTS)
        self.at_home = s.z == s.part
        self.below = s.z < s.part
        self.above = s.z > s.part
        self.beside = s.x_peer[1] == self.home

    def y_copy(self):
        s = self.split
        return remote(self.grad.at[1 - s.y], self.met, self.y_sent, self.y_got, s.y_peer)

    def z_copy(self, way):
        s = self.split
        return remote(self.met, self.came.at[way], self.z_sent.at[way], self.z_got.at[way],
                      s.at_z(s.z + 1 - 2 * way))

    def z_arrival(self, way):
        return remote(self.met, self.came.at[way], self.z_sent.at[way], self.z_got.at[way],
                      self.split.y_peer)

    def b_copy(self, which):
        s = self.split
        source = self.done if which == 2 else self.met
        device = s.core_peer if which == 2 else s.blk_peers[which]
        return remote(source, self.done, self.b_sent.at[which], self.b_got.at[0], device)

    def own_copy(self):
        return pltpu.make_async_copy(self.met, self.done, self.b_sent.at[3])

    def start(self):
        self.y_copy().start()

    def send(self, act):
        @pl.when(self.below)
        def _():
            act(self.z_copy(0))

        @pl.when(self.above)
        def _():
            act(self.z_copy(1))

    def take(self, way):
        self.z_arrival(way).wait_recv()

        def body(rows):
            both = self.met[rows].astype(F32) + self.came[way, rows].astype(F32)
            self.met[rows] = both.astype(self.met.dtype)
        each(self.met.shape[0], self.step, body)

    def middle(self):
        s = self.split
        self.y_copy().wait_recv()

        def body(rows):
            both = self.grad[s.y, rows].astype(F32) + self.met[rows].astype(F32)
            self.met[rows] = both.astype(self.met.dtype)
        each(self.met.shape[0], self.step, body)

        @pl.when(jnp.logical_not(s.inner))
        def _():
            self.send(lambda copy: copy.start())

    def join(self):
        s = self.split

        @pl.when(s.inner)
        def _():
            @pl.when(self.below)
            def _():
                self.take(0)

            @pl.when(self.above)
            def _():
                self.take(1)
            self.send(lambda copy: copy.start())

    def last(self):
        s = self.split

        @pl.when(self.at_home)
        def _():
            @pl.when(s.z > 0)
            def _():
                self.take(0)

            @pl.when(s.z < PARTS - 1)
            def _():
                self.take(1)
            self.b_copy(1).start()
            self.b_copy(0).start()
            self.own_copy().start()

    def pass_on(self):
        @pl.when(self.beside)
        def _():
            self.b_copy(0).wait_recv()
            self.b_copy(2).start()

    def close(self):
        self.y_copy().wait_send()
        self.send(lambda copy: copy.wait_send())

        @pl.when(self.at_home)
        def _():
            self.b_copy(0).wait_send()
            self.b_copy(1).wait_send()
            self.own_copy().wait()

        @pl.when(self.beside)
        def _():
            self.b_copy(2).wait_send()

        @pl.when(jnp.logical_not(jnp.logical_or(self.at_home, self.beside)))
        def _():
            self.b_copy(0).wait_recv()


class Total:
    def __init__(self, split, part, met, out, came, whole, sems, slot):
        self.split, self.part, self.met, self.out = split, part, met, out
        self.came, self.whole = came.at[slot], whole
        self.sent, self.got = sems
        self.chunks = part.shape[0]
        self.high = part.shape[2]

    def first_copy(self, at):
        s = self.split
        return remote(self.part.at[at, 1 - s.core], self.met.at[at], self.sent.at[at, 0],
                      self.got.at[at, 0], s.core_peer)

    def second_copy(self, at):
        return remote(self.out.at[at], self.came.at[at], self.sent.at[at, 1],
                      self.got.at[at, 1], self.split.x_peer)

    def third_copy(self, at, half):
        s = self.split
        return remote(self.whole.at[at, half], self.whole.at[at, half], self.sent.at[at, 2],
                      self.got.at[at, 2], s.core_peer)

    def start(self, at):
        self.first_copy(at).start()

    def middle(self, at):
        s = self.split
        self.first_copy(at).wait_recv()

        def body(rows):
            both = self.part[at, s.core, rows] + self.met[at, rows]
            self.out[at, rows] = both.astype(BF16)
        each(self.high, 32, body)
        self.second_copy(at).start()

    def third(self, at):
        s = self.split
        self.second_copy(at).wait_recv()

        def body(rows):
            self.whole[at, s.core, rows] = self.out[at, rows].astype(
                F32) + self.came[at, rows].astype(F32)
        each(self.high, 32, body)
        self.third_copy(at, s.core).start()

    def fourth(self, at):
        s = self.split
        self.third_copy(at, 1 - s.core).wait_recv()
        self.first_copy(at).wait_send()
        self.second_copy(at).wait_send()
        self.third_copy(at, s.core).wait_send()

    def begin(self, produce):
        @pl.loop(0, self.chunks + 1)
        def _(at):
            @pl.when(at < self.chunks)
            def _():
                produce(at)
                self.start(at)

            @pl.when(at > 0)
            def _():
                self.middle(at - 1)

    def finish(self, consume):
        self.third(0)

        @pl.loop(0, self.chunks)
        def _(at):
            @pl.when(at + 1 < self.chunks)
            def _():
                self.third(at + 1)
            self.fourth(at)
            consume(at)


def head_mask(width, size, head):
    lanes = lax.broadcasted_iota(jnp.int32, (1, width), 1)
    return lax.div(lanes, size) == head


def keep(mask, values):
    return jnp.where(mask, values, jnp.zeros_like(values))


class Block:
    def __init__(self, rows, width, heads, size, names, refs, vectors):
        self.rows, self.width, self.heads, self.size = rows, width, heads, size
        self.share = heads * size
        self.scaling = 1.0 / math.sqrt(size)
        self.refs = refs
        self.vectors = vectors
        self.name = names
        self.tile = 32 * 1024 // width
        self.chunk = 2 * refs[names + "part"].shape[2]

    def ref(self, name):
        return self.refs[self.name + name]

    def row(self, at):
        return self.refs["gains"][self.vectors + at:self.vectors + at + 1, 0:self.width]

    def norm(self, first, base=0, count=None):
        unit, scale = self.ref("unit_a" if first else "unit_b"), self.ref(
            "scale_a" if first else "scale_b")
        out = self.ref("normed" if first else "lifted")
        gain, bias = self.row(0 if first else 2), self.row(1 if first else 3)
        residual = self.ref("residual")

        def body(rows):
            one, size = norm_parts(residual[rows])
            unit[rows] = one
            scale[rows] = size
            out[rows] = (one * gain + bias).astype(BF16)
        each(count or self.rows, self.tile, body, base)

    def project(self):
        normed, mixed, weight = self.ref("normed"), self.ref("qkv"), self.ref("w_qkv")

        def body(rows):
            mixed[rows] = dot(normed[rows], weight[...]).astype(BF16)
        each(self.rows, 128, body)

    def parts(self, rows):
        share, qkv = self.share, self.ref("qkv")
        return (qkv[rows, 0:share], qkv[rows, share:2 * share], qkv[rows, 2 * share:3 * share])

    def attend(self, ids_column, ids_row):
        probs, mixture = self.ref("probs"), self.ref("mixture")
        everything = pl.ds(0, self.rows)

        def body(queries):
            query = self.parts(queries)[0]
            unused, key_rows, values = self.parts(everything)
            allowed = ids_column[...] == ids_row[:, queries]

            def one(head, mixed):
                mask = head_mask(self.share, self.size, head)
                scores = jnp.where(
                    allowed, dot_b(keep(mask, key_rows), query) * self.scaling, MASKED_SCORE
                )
                exponent = jnp.exp(scores - jnp.max(scores, axis=0, keepdims=True))
                softmaxed = exponent * (1.0 / jnp.sum(exponent, axis=0, keepdims=True))
                probs[head, :, queries] = softmaxed
                return mixed + dot_t(keep(mask, values), softmaxed.astype(BF16))

            mixed = lax.fori_loop(0, self.heads, one, jnp.zeros((self.share, 128), F32))
            mixture[queries] = mixed.T.astype(BF16)
        each(self.rows, 128, body)

    def product(self, left, weight, back=False):
        target, deep = self.ref("part"), self.chunk

        def produce(at):
            rows = pl.ds(pl.multiple_of(at * deep, deep), deep)
            made = (dot_b if back else dot)(left[rows], weight[...])
            target[at, 0] = made[:deep // 2]
            target[at, 1] = made[deep // 2:]
        return produce

    def halves(self, rows):
        half = self.chunk // 2
        at = lax.div(rows.start, half)
        place = pl.ds(pl.multiple_of(lax.rem(rows.start, half), rows.size), rows.size)
        return self.ref("whole")[lax.div(at, 2), lax.rem(at, 2), place]

    def add_total(self, at):
        residual = self.ref("residual")

        def body(rows):
            residual[rows] = residual[rows] + self.halves(rows)
        each(self.chunk, self.tile, body, at * self.chunk)

    def expand(self, base=0, count=None):
        lifted, weight = self.ref("lifted"), self.ref("w_up")
        hidden, slope = self.ref("hidden"), self.ref("slope")

        def body(rows):
            def inner(columns):
                made, gradient = gelu_both(dot(lifted[rows], weight[:, columns]))
                hidden[rows, columns] = made.astype(BF16)
                slope[rows, columns] = gradient
            each(weight.shape[1], 256, inner)
        each(count or self.rows, 128, body, base)

    def back_hidden(self, branch, base=0, count=None):
        weight, slope, grad = self.ref("w_down"), self.ref("slope"), self.ref("grad_upper")

        def body(rows):
            def inner(columns):
                made = dot_b(branch[rows], weight[columns])
                grad[rows, columns] = (made * slope[rows, columns]).astype(BF16)
            each(weight.shape[0], 256, inner)
        each(count or self.rows, 128, body, base)

    def clear_sums(self):
        sums = self.ref("sums")
        sums[...] = jnp.zeros(sums.shape, F32)

    def norm_back(self, at, first, out):
        unit, scale = self.ref("unit_a" if first else "unit_b"), self.ref(
            "scale_a" if first else "scale_b")
        gain, grad, sums = self.row(0 if first else 2), self.ref("grad"), self.ref("sums")

        def body(rows):
            moved, gains, biases = norm_back(self.halves(rows), unit[rows], scale[rows], gain)
            new = grad[rows] + moved
            grad[rows] = new
            if out is not None:
                out[rows] = new.astype(BF16)
            sums[0:1] += gains
            sums[1:2] += biases
        each(self.chunk, self.tile, body, at * self.chunk)

    def back_mixture(self, branch, base=0, count=None):
        weight, grad = self.ref("w_out"), self.ref("grad_mixture")

        def body(rows):
            grad[rows] = dot_b(branch[rows], weight[...]).astype(BF16)
        each(count or self.rows, self.chunk, body, base)

    def attend_back(self):
        probs, grad_mixture, grads = self.ref("probs"), self.ref("grad_mixture"), self.ref(
            "grad_qkv")
        key_sum, value_sum = self.ref("key_sum"), self.ref("value_sum")
        share, everything = self.share, pl.ds(0, self.rows)
        key_sum[...] = jnp.zeros(key_sum.shape, F32)
        value_sum[...] = jnp.zeros(value_sum.shape, F32)

        def body(queries):
            query = self.parts(queries)[0]
            unused, key_rows, values = self.parts(everything)
            grad_rows = grad_mixture[queries]

            def one(head, total):
                mask = head_mask(share, self.size, head)
                softmaxed = probs[head, :, queries]
                grad_probs = dot_b(keep(mask, values), grad_rows)
                value_sum[...] += dot(softmaxed.astype(BF16), keep(mask, grad_rows))
                delta = jnp.sum(softmaxed * grad_probs, axis=0, keepdims=True)
                grad_scores = (softmaxed * (grad_probs - delta)).astype(BF16)
                key_sum[...] += dot(grad_scores, keep(mask, query))
                return total + dot_t(keep(mask, key_rows), grad_scores)

            total = lax.fori_loop(0, self.heads, one, jnp.zeros((share, 128), F32))
            grads[queries, 0:share] = (total.T * self.scaling).astype(BF16)
        each(self.rows, 128, body)

        def close(rows):
            grads[rows, share:2 * share] = (key_sum[rows] * self.scaling).astype(BF16)
            grads[rows, 2 * share:3 * share] = value_sum[rows].astype(BF16)
        each(self.rows, 128, close)


def weight_grad(left, right, target):
    if len(target.shape) == 4:
        parts, sides, rows, width = target.shape
        if rows >= 128:
            @pl.loop(0, parts * sides)
            def _(at):
                block = dot_t(left[:, span(at * rows, rows)], right[...])
                target[lax.div(at, sides), lax.rem(at, sides)] = block.astype(BF16)
        else:
            @pl.loop(0, parts)
            def _(at):
                block = dot_t(left[:, span(at * sides * rows, sides * rows)], right[...])
                target[at] = block.reshape(sides, rows, width).astype(BF16)
    else:
        sides, rows, width = target.shape
        if rows >= 128:
            @pl.loop(0, sides)
            def _(at):
                block = dot_t(left[:, span(at * rows, rows)], right[...])
                target[at] = block.astype(BF16)
        else:
            block = dot_t(left[...], right[...])
            target[...] = block.reshape(sides, rows, width).astype(BF16)


def vector_store(target, at, row, whole):
    for owner in range(8):
        block = owner if whole else owner // 2
        target[owner // 2, owner % 2, at:at + 1, :] = row[:, 128 * block:128 * block + 128]


COLUMN_UNITS = ("e_qkv", "e_up", "e_down", "embed", "d_qkv", "d_up")
ROW_UNITS = ("e_out", "d_out", "d_down")
ROW_SUMS = ("d_out", "d_down")
MESSAGES = COLUMN_UNITS + ROW_UNITS
TRADED = ("e_qkv", "e_up", "e_down", "e_out", "embed")
EARLY = ()


def unit_shapes(width, dec_width, hidden, dec_hidden):
    return {
        "e_qkv": (width // 8, 3 * width // 4),
        "e_up": (width // 8, hidden // 4),
        "e_down": (hidden // 32, width),
        "embed": (width // 8, dec_width // 4),
        "d_qkv": (dec_width // 8, 3 * dec_width // 4),
        "d_up": (dec_width // 8, dec_hidden // 4),
        "e_out": (width // 8, width),
        "d_out": (dec_width // 8, dec_width),
        "d_down": (dec_hidden // 8, dec_width),
    }


def scratch_table(width, dec_width, hidden, dec_hidden, rows, shown):
    units = unit_shapes(width, dec_width, hidden, dec_hidden)
    table = {}
    for name in COLUMN_UNITS:
        height, columns = units[name]
        if name != "embed":
            table["w_" + name] = ((8 * height, columns), BF16)
        table["g_" + name] = ((PARTS, SIDES, height, columns), BF16)
        table["m_" + name] = ((PARTS, height, columns), BF16)
        table["c_" + name] = ((PARTS, height, columns), BF16)
        if name in TRADED:
            del table["g_" + name]
            table["l_" + name] = ((PARTS, shown, 128), BF16)
            if name != "embed":
                table["r_" + name] = ((shown, columns), BF16)
    table["w_embed"] = ((width, dec_width), BF16)
    for name in ROW_UNITS:
        height, columns = units[name]
        table["w_" + name] = ((2 * height, columns), BF16)
        if name == "e_out":
            narrow = columns // PARTS
            table["m_e_out"] = ((PARTS, height, narrow), BF16)
            table["c_e_out"] = ((PARTS, height, narrow), BF16)
            table["l_e_out"] = ((PARTS, shown, 128), BF16)
            table["r_e_out"] = ((shown, narrow), BF16)
            table["mixture_all"] = ((shown, width), BF16)
            continue
        table["g_" + name] = ((SIDES, height, columns), BF16)
        table["m_" + name] = ((height, columns), BF16)
        table["c_" + name] = ((2, height, columns), BF16)
    table["w_vector"] = ((8 * VECTORS, 128), BF16)
    table["g_vector"] = ((PARTS, SIDES, VECTORS, 128), F32)
    table["m_vector"] = ((PARTS, VECTORS, 128), F32)
    table["c_vector"] = ((PARTS, VECTORS, 128), F32)
    table["gains"] = ((VECTORS, width), F32)
    table["group"] = ((rows, width), BF16)
    table["cotangents"] = ((rows, dec_width), BF16)
    for key, count, wide, deep, heads, size, chunks in (
        ("e_", shown, width, hidden // 4, 4, 64, 2),
        ("d_", rows, dec_width, dec_hidden // 4, 4, 32, 4),
    ):
        share = heads * size
        for name, shape, kind in (
            ("residual", (count, wide), F32), ("unit_a", (count, wide), F32),
            ("unit_b", (count, wide), F32), ("scale_a", (count, 1), F32),
            ("scale_b", (count, 1), F32), ("normed", (count, wide), BF16),
            ("lifted", (count, wide), BF16), ("qkv", (count, 3 * share), BF16),
            ("probs", (heads, count, count), F32), ("mixture", (count, share), BF16),
            ("hidden", (count, deep), BF16), ("slope", (count, deep), F32),
            ("grad_upper", (count, deep), BF16), ("grad", (count, wide), F32),
            ("grad_mixture", (count, share), BF16), ("grad_qkv", (count, 3 * share), BF16),
            ("key_sum", (count, share), F32), ("value_sum", (count, share), F32),
            ("branch", (count, wide), BF16), ("branch_b", (count, wide), BF16),
            ("part", (chunks, 2, count // chunks // 2, wide), F32),
            ("met", (chunks, count // chunks // 2, wide), F32),
            ("out", (chunks, count // chunks // 2, wide), BF16),
            ("came", (2, chunks, count // chunks // 2, wide), BF16),
            ("whole", (chunks, 2, count // chunks // 2, wide), F32),
            ("sums", (8, wide), F32),
        ):
            table[key + name] = (shape, kind)
    table["last_part"] = ((2, 2, rows // 4, dec_width), F32)
    table["last_met"] = ((2, rows // 4, dec_width), F32)
    table["last_out"] = ((rows // 4, dec_width), BF16)
    table["last_came"] = ((rows // 4, dec_width), BF16)
    for name, shape, kind in (
        ("rank_row", (1, rows), jnp.int32), ("rank_column", (rows, 1), jnp.int32),
        ("ids_row", (1, rows), jnp.int32), ("ids_column", (rows, 1), jnp.int32),
        ("packed_row", (1, shown), jnp.int32), ("packed_column", (shown, 1), jnp.int32),
        ("code", (shown, width), F32), ("dec_code", (rows, dec_width), F32),
        ("staged", (VECTORS, 128), F32),
    ):
        table[name] = (shape, kind)
    table["lowered"] = ((shown, width), BF16)
    table["their_picked"] = ((shown, dec_width), BF16)
    table["picked"] = ((shown, dec_width), BF16)
    return table


VECTOR_NAMES = (
    "v_gain_a", "v_bias_a", "v_gain_b", "v_bias_b", "v_mask",
    "v_dec_gain_a", "v_dec_bias_a", "v_dec_gain_b", "v_dec_bias_b",
)
INPUTS = ("lengths", "gsd", "visible") + VECTOR_NAMES + (
    "patches", "cotangent", "query", "key", "value", "out", "up", "down", "embed",
    "dec_query", "dec_key", "dec_value", "dec_out", "dec_up", "dec_down",
)
RESULTS = ("decoded", "grad_patches", "grad_vector") + MESSAGES
SEMAPHORES = {
    "local": (24,),
    "z_sent": (11,), "z_got": (11, 4), "y_sent": (11,), "y_got": (11, 4),
    "cross_sent": (1,), "cross_got": (1, 4),
    "gy_sent": (11,), "gy_got": (11,), "gz_sent": (11, 3), "gz_got": (11, 4),
    "f_sent": (5, 2), "f_got": (5, 2), "m_sent": (3,), "m_got": (3,), "gb_sent": (11, 4), "gb_got": (11, 3),
    "p_sent": (3,), "p_got": (3,), "c_sent": (3,), "c_got": (3,),
    "e_sent": (3,), "e_got": (3,), "l_sent": (2,), "l_got": (2,),
    "e_t_sent": (2, 2, 3), "e_t_got": (2, 2, 3), "d_t_sent": (2, 4, 3), "d_t_got": (2, 4, 3),
}


def place_of(ref, positions):
    ids = jnp.zeros(positions.shape, jnp.int32)
    first = jnp.zeros(positions.shape, jnp.int32)
    ratio = jnp.zeros(positions.shape, F32) + ref["gsd"][0, 0]
    end = jnp.int32(0)
    count = ref["lengths"].shape[1]
    for at in range(count - 1):
        end = end + ref["lengths"][0, at]
        later = positions >= end
        ids = ids + later.astype(jnp.int32)
        first = jnp.where(later, end, first)
        ratio = jnp.where(later, ref["gsd"][0, at + 1], ratio)
    return ids, (positions - first).astype(F32) * ratio


def lay_out(ref, rows, shown, width, dec_width):
    ids_row, scaled_row = place_of(ref, lax.broadcasted_iota(jnp.int32, (1, rows), 1))
    ids_column, scaled_column = place_of(ref, lax.broadcasted_iota(jnp.int32, (rows, 1), 0))
    ref["ids_row"][...] = ids_row
    ref["ids_column"][...] = ids_column
    visible = ref["visible"][...] > 0
    marks = jnp.broadcast_to(visible.astype(F32), (16, rows)).astype(BF16)
    down = lax.broadcasted_iota(jnp.int32, (rows, rows), 0)
    along = lax.broadcasted_iota(jnp.int32, (rows, rows), 1)
    until = (along <= down).astype(BF16)
    before = (along < down).astype(BF16)
    count_row = dot_b(marks, until)[0:1]
    rank_row = jnp.where(visible, count_row.astype(jnp.int32) - 1, -1)
    count_column = dot_b(until, marks)[:, 0:1].astype(jnp.int32)
    others = dot_b(before, marks)[:, 0:1].astype(jnp.int32)
    rank_column = jnp.where(count_column > others, others, -1)
    ref["rank_row"][...] = rank_row
    ref["rank_column"][...] = rank_column
    here = lax.broadcasted_iota(jnp.int32, (shown, rows), 0) == rank_row
    packed = jnp.sum(jnp.where(here, ids_row.astype(F32), 0.0), axis=1, keepdims=True)
    ref["packed_column"][...] = packed.astype(jnp.int32)
    packed_scaled = jnp.sum(jnp.where(here, scaled_row, 0.0), axis=1, keepdims=True)
    there = lax.broadcasted_iota(jnp.int32, (rows, shown), 1) == rank_column
    packed = jnp.sum(jnp.where(there, ids_column.astype(F32), 0.0), axis=0, keepdims=True)
    ref["packed_row"][...] = packed.astype(jnp.int32)
    for target, scaled, wide in (
        (ref["code"], packed_scaled, width), (ref["dec_code"], scaled_column, dec_width)
    ):
        half = wide // 2
        steps = lax.broadcasted_iota(jnp.int32, (1, half), 1).astype(F32)
        frequency = jnp.exp(steps * (-math.log(10000.0) / half))
        target[:, 0:1] = scaled
        tall = 16 * 1024 // half

        def body(part):
            angles = target[part, 0:1] * frequency
            made = jnp.concatenate([jnp.sin(angles), jnp.cos(angles)], axis=1)
            target[part] = made
        each(target.shape[0], tall, body)


def main_kernel(names, *refs):
    ref = dict(zip(names, refs))
    s = Split()
    shown, width = ref["code"].shape
    rows, dec_width = ref["dec_code"].shape
    own = ref["patches"].shape[0]
    sem = {name: ref["s_" + name] for name in SEMAPHORES}
    counter = [0]

    def local(source, target):
        at = counter[0]
        counter[0] = at + 1
        return pltpu.make_async_copy(source, target, sem["local"].at[at])

    barrier = pltpu.get_barrier_semaphore()
    peers = [s.z_peer(step) for step in (1, 2, 3)] + [s.y_peer] + list(s.blk_peers)
    for peer in peers:
        pl.semaphore_signal(barrier, inc=1, device_id=peer, device_id_type=pl.DeviceIdType.MESH)

    order = ("vector", "e_qkv", "e_out", "e_up", "embed", "e_down", "e_down_b", "d_qkv", "d_out",
             "d_up", "d_down")
    units = {}
    for at, name in enumerate(order):
        sems = tuple(sem[kind].at[at] for kind in ("z_sent", "z_got", "y_sent", "y_got"))
        sems = sems + (sem["cross_sent"].at[0], sem["cross_got"].at[0])
        whole = ref["w_e_down" if name == "e_down_b" else "w_" + name]
        if name == "vector":
            units[name] = Columns(s, whole, VECTORS, [], sems)
        elif name in ROW_UNITS:
            source = ref[{"e_out": "out", "d_out": "dec_out", "d_down": "dec_down"}[name]]
            height = source.shape[0]
            copy = local(source, whole.at[span(s.y * height, height)])
            units[name] = Rows(s, whole, height, copy, sems)
        else:
            height = ref["m_e_down" if name == "e_down_b" else "m_" + name].shape[1]
            mine = span(s.dp * height, height)
            columns = None
            if name in ("e_qkv", "d_qkv"):
                kinds = ("query", "key", "value")
                if name == "d_qkv":
                    kinds = ("dec_query", "dec_key", "dec_value")
                size = ref[kinds[0]].shape[1] // PARTS
                copies = [
                    local(ref[kind].at[:, span(s.part * size, size)],
                          whole.at[mine, pl.ds(place * size, size)])
                    for place, kind in enumerate(kinds)
                ]
            elif name == "e_up":
                size = height
                copies = [
                    local(ref["up"].at[:, span((owner * PARTS + s.blk) * size, size)],
                          whole.at[mine, pl.ds(owner * size, size)])
                    for owner in range(8)
                ]
            elif name in ("e_down", "e_down_b"):
                size = width // 2
                columns = pl.ds(size if name == "e_down_b" else 0, size)
                copies = [local(ref["down"].at[span(s.blk * height, height), columns],
                                whole.at[mine, columns])]
            elif name == "embed":
                size = dec_width // PARTS
                columns = span(s.part * size, size)
                copies = [local(ref["embed"].at[:, columns], whole.at[mine, columns])]
            else:
                size = ref["dec_up"].shape[1] // PARTS
                copies = [local(ref["dec_up"].at[:, span(s.part * size, size)], whole.at[mine])]
            kind = EarlyColumns if name in EARLY else Columns
            units[name] = kind(s, whole, height, copies, sems, columns)

    sums = {}
    for at, name in enumerate(order):
        if name == "e_down_b":
            continue
        sems = tuple(
            sem[kind].at[at]
            for kind in ("gy_sent", "gy_got", "gz_sent", "gz_got", "gb_sent", "gb_got")
        )
        kind = RowSum if name in ROW_SUMS else ProductSum if name in TRADED else ColumnSum
        done = None if name == "vector" else ref["o_" + name]
        wide = ref["m_" + name].shape[-1]
        sums[name] = kind(s, ref.get("g_" + name), ref["m_" + name], ref["c_" + name], done, sems,
                          16 if wide > 512 else 32 if name != "vector" else 8)
    def their_embed():
        def body(part):
            made = dot_b(ref["their_picked"][...], ref["w_embed"][part])
            ref["r_e_down"][:, part] = made.astype(BF16)
        each(width, 256, body)

    picked, their_picked = ref["picked"], ref["their_picked"]
    embed_columns = span(s.part * (dec_width // PARTS), dec_width // PARTS)
    out_columns = span(s.part * (width // PARTS), width // PARTS)
    for at, (name, left, right, their_right, more) in enumerate((
        ("e_qkv", "e_normed", ref["e_grad_qkv"], ref["r_e_qkv"], ()),
        ("e_up", "e_lifted", ref["e_grad_upper"], ref["r_e_up"], ()),
        ("e_down", "e_hidden", ref["e_branch"], ref["r_e_down"],
         (picked, their_picked, their_embed)),
        ("e_out", "mixture_all", ref["e_branch_b"].at[:, out_columns], ref["r_e_out"], ()),
        ("embed", "lowered", picked.at[:, embed_columns], their_picked.at[:, embed_columns],
         (False,)),
    )):
        sums[name].trade(ref[left], right, ref["l_" + name], their_right,
                         (sem["f_sent"].at[at], sem["f_got"].at[at]), *more)

    totals = []
    for at in range(7):
        key, slot = ("e_", at % 2) if at in (0, 1, 5, 6) else ("d_", at % 2)
        totals.append(Total(
            s, *(ref[key + name] for name in ("part", "met", "out", "came", "whole")),
            (sem[key + "t_sent"].at[slot], sem[key + "t_got"].at[slot]), slot,
        ))

    encoder = Block(shown, width, 4, 64, "e_", ref, 0)
    decoder = Block(rows, dec_width, 4, 32, "d_", ref, 5)
    for block, key in ((encoder, "e_"), (decoder, "d_")):
        for short, long in (("w_qkv", "qkv"), ("w_out", "out"), ("w_up", "up"),
                            ("w_down", "down")):
            ref[key + short] = ref["w_" + key + long]

    for name in order:
        units[name].fetch()
    mine = span(s.blk * own, own)
    own_patches = local(ref["patches"], ref["group"].at[mine])
    own_cotangents = local(ref["cotangent"], ref["cotangents"].at[mine])
    own_patches.start()
    own_cotangents.start()
    staged = ref["staged"]
    staged[...] = jnp.zeros(staged.shape, F32)
    for at, name in enumerate(VECTOR_NAMES):
        row = ref[name][...].astype(F32)[None, :]
        staged[at:at + 1, 0:row.shape[1]] = row
    ref["w_vector"][span(s.dp * VECTORS, VECTORS)] = staged[...].astype(BF16)

    pl.semaphore_wait(barrier, len(peers))

    def place_in(name):
        return lambda blk: ref[name].at[span(blk * own, own)]

    def embed_block(blk):
        size = dec_width // PARTS
        return ref["w_embed"].at[:, span(lax.rem(3 * blk, PARTS) * size, size)]

    def mixture_block(blk):
        size = width // PARTS
        return ref["mixture_all"].at[:, span(lax.rem(3 * blk, PARTS) * size, size)]

    shared = {
        "p": Shared(s, ref["patches"], place_in("group"), (sem["p_sent"], sem["p_got"])),
        "c": Shared(s, ref["cotangent"], place_in("cotangents"), (sem["c_sent"], sem["c_got"])),
        "e": Shared(s, embed_block(s.blk), embed_block, (sem["e_sent"], sem["e_got"])),
        "m": Shared(s, ref["e_mixture"], mixture_block, (sem["m_sent"], sem["m_got"])),
    }
    for name in ("vector", "e_qkv", "e_out"):
        units[name].send()
    shared["p"].start()
    units["e_up"].send()

    lay_out(ref, rows, shown, width, dec_width)
    units["vector"].forward()
    units["e_qkv"].forward()
    shared["p"].pass_on()
    own_patches.wait()
    units["e_out"].forward()
    shared["p"].finish()

    places = (
        lax.broadcasted_iota(jnp.int32, (shown, rows), 0) == ref["rank_row"][...]
    ).astype(BF16)
    residual = ref["e_residual"]

    def place_patches(columns):
        residual[:, columns] = dot(places, ref["group"][:, columns]) + ref["code"][:, columns]
    each(width, 256, place_patches)

    units["e_up"].forward((1,))
    units["vector"].finish()
    vectors = ref["w_vector"][...].astype(F32)
    gains = ref["gains"]
    for at in range(9):
        for owner in range(8):
            row = vectors[VECTORS * owner + at:VECTORS * owner + at + 1, :]
            if at < 4:
                gains[at:at + 1, 128 * owner:128 * owner + 128] = row
            elif owner % 2 == 0:
                pair = VECTORS * (owner + 1) + at
                other = pltpu.roll(vectors[pair:pair + 1, :], 64, 1)
                gains[at:at + 1, 64 * owner:64 * owner + 128] = row + other
    encoder.norm(True)
    units["e_up"].forward((2,))
    units["embed"].send()
    units["e_down"].send()
    units["e_qkv"].finish()
    encoder.project()
    units["e_up"].forward((3,))
    encoder.attend(ref["packed_column"], ref["packed_row"])
    ref["mixture_all"][:, out_columns] = ref["e_mixture"][...]
    units["e_out"].finish()
    totals[0].begin(encoder.product(ref["e_mixture"], ref["w_e_out"]))
    units["embed"].forward()

    def after_attention(at):
        encoder.add_total(at)
        encoder.norm(False, at * encoder.chunk, encoder.chunk)
    totals[0].finish(after_attention)
    shared["c"].start()
    shared["m"].start()
    units["e_down"].forward()
    units["e_down_b"].send()
    units["e_up"].finish()
    encoder.expand()
    units["d_qkv"].send()
    units["d_out"].send()
    units["embed"].finish()
    shared["e"].start()
    shared["c"].pass_on()
    shared["m"].pass_on()
    units["e_down_b"].forward()
    units["d_up"].send()
    units["d_down"].send()
    units["d_qkv"].forward()
    shared["e"].pass_on()
    units["e_down"].finish()
    units["e_down_b"].finish()
    totals[1].begin(encoder.product(ref["e_hidden"], ref["w_e_down"]))
    units["d_out"].forward()
    units["d_up"].forward()
    shared["e"].finish()
    lowered = ref["lowered"]

    def after_hidden(at):
        encoder.add_total(at)
        part = pl.ds(pl.multiple_of(at * encoder.chunk, encoder.chunk), encoder.chunk)
        lowered[part] = residual[part].astype(BF16)
    totals[1].finish(after_hidden)

    embedded = dot(lowered[...], ref["w_embed"][...])
    high = embedded.astype(BF16)
    low = (embedded - high.astype(F32)).astype(BF16)
    token = gains[4:5, 0:dec_width]
    start = ref["d_residual"]

    def place_rows(part):
        rank = ref["rank_column"][part]
        here = (lax.broadcasted_iota(jnp.int32, (128, shown), 1) == rank).astype(BF16)
        made = jnp.where(rank >= 0, dot(here, high) + dot(here, low), token)
        start[part] = made + ref["dec_code"][part]
    each(rows, 128, place_rows)
    decoder.norm(True)
    units["d_down"].forward()
    units["d_qkv"].finish()
    decoder.project()
    decoder.attend(ref["ids_column"], ref["ids_row"])
    units["d_out"].finish()
    totals[2].begin(decoder.product(ref["d_mixture"], ref["w_d_out"]))
    units["d_up"].finish()
    units["d_down"].finish()
    last_part, last_met = ref["last_part"], ref["last_met"]
    quarter = rows // 4

    def decoder_rest(at):
        decoder.add_total(at)
        decoder.norm(False, at * decoder.chunk, decoder.chunk)
        decoder.expand(at * decoder.chunk, decoder.chunk)
        part = pl.ds(pl.multiple_of(at * quarter, quarter), quarter)
        made = dot(ref["d_hidden"][part], ref["w_d_down"][...])
        last_part[lax.div(at, 2), lax.rem(at, 2)] = made
    totals[2].finish(decoder_rest)
    last_sent, last_got = sem["l_sent"], sem["l_got"]
    last_first = remote(last_part.at[:, 1 - s.core], last_met, last_sent.at[0], last_got.at[0],
                        s.core_peer)
    last_second = remote(ref["last_out"], ref["last_came"], last_sent.at[1], last_got.at[1],
                         s.x_peer)
    last_first.start()

    own_cotangents.wait()
    shared["c"].finish()
    shared["m"].finish()
    for name in ("e_down", "embed", "e_up", "e_out", "e_qkv"):
        sums[name].start_left()
    cotangents, grad = ref["cotangents"], ref["d_grad"]
    multiply = decoder.product(ref["d_grad_upper"], ref["w_d_up"], back=True)

    def decoder_hidden(at):
        decoder.back_hidden(cotangents, at * decoder.chunk, decoder.chunk)
        multiply(at)
    totals[3].begin(decoder_hidden)
    last_first.wait_recv()

    def last_add(part):
        made = last_part[1 - s.x, s.core, part] + last_met[1 - s.x, part]
        ref["last_out"][part] = made.astype(BF16)
    each(quarter, 64, last_add)
    last_second.start()

    def copy_grad(part):
        grad[part] = cotangents[part].astype(F32)
    each(rows, 64, copy_grad)
    vector_grad = ref["g_vector"]
    vector_grad[...] = jnp.zeros(vector_grad.shape, F32)
    decoder.clear_sums()
    weight_grad(ref["d_hidden"], cotangents, ref["g_d_down"])
    sums["d_down"].start()
    weight_grad(ref["d_lifted"], ref["d_grad_upper"], ref["g_d_up"])
    sums["d_up"].start()

    def decoder_middle(at):
        decoder.norm_back(at, False, ref["d_branch"])
        decoder.back_mixture(ref["d_branch"], at * decoder.chunk, decoder.chunk)
    totals[3].finish(decoder_middle)
    vector_store(vector_grad, 7, ref["d_sums"][0:1], False)
    vector_store(vector_grad, 8, ref["d_sums"][1:2], False)
    decoder.attend_back()
    sums["d_down"].middle()
    totals[4].begin(decoder.product(ref["d_grad_qkv"], ref["w_d_qkv"], back=True))
    sums["d_up"].middle()
    last_second.wait_recv()

    def last_close(part):
        made = last_part[s.x, s.core, part] + last_met[s.x, part]
        before = ref["d_residual"][pl.ds(pl.multiple_of(s.blk * own + part.start, 64), 64)]
        whole = made + ref["last_came"][part].astype(F32) + before
        ref["decoded"][part] = whole.astype(BF16)
    each(quarter, 64, last_close)
    decoder.clear_sums()
    weight_grad(ref["d_normed"], ref["d_grad_qkv"], ref["g_d_qkv"])
    sums["d_qkv"].start()
    weight_grad(ref["d_mixture"], ref["d_branch"], ref["g_d_out"])
    sums["d_out"].start()

    def decoder_first(at):
        decoder.norm_back(at, True, ref["d_branch_b"])
    totals[4].finish(decoder_first)
    picked[...] = dot(places, ref["d_branch_b"][...]).astype(BF16)
    sums["e_down"].start()
    encoder_grad = ref["e_grad"]

    def back_embed(part):
        made = dot_b(picked[...], ref["w_embed"][part])
        encoder_grad[:, part] = made
        ref["e_branch"][:, part] = made.astype(BF16)
    each(width, 256, back_embed)
    sums["d_down"].join()

    encoder.back_hidden(ref["e_branch"])
    sums["e_up"].start()
    totals[5].begin(encoder.product(ref["e_grad_upper"], ref["w_e_up"], back=True))
    sums["d_qkv"].middle()
    sums["d_out"].middle()
    sums["e_down"].middle()
    encoder.clear_sums()

    def encoder_middle(at):
        encoder.norm_back(at, False, ref["e_branch_b"])
        encoder.back_mixture(ref["e_branch_b"], at * encoder.chunk, encoder.chunk)
    totals[5].finish(encoder_middle)
    sums["e_out"].start()
    sums["d_up"].join()
    sums["e_up"].middle()
    encoder.attend_back()
    sums["e_qkv"].start()
    totals[6].begin(encoder.product(ref["e_grad_qkv"], ref["w_e_qkv"], back=True))
    sums["d_down"].last()
    sums["d_qkv"].join()
    sums["d_out"].join()
    sums["d_up"].last()
    sums["e_out"].middle()
    sums["embed"].middle()
    vector_store(vector_grad, 2, ref["e_sums"][0:1], True)
    vector_store(vector_grad, 3, ref["e_sums"][1:2], True)
    encoder.clear_sums()
    sums["e_down"].join()
    sums["e_qkv"].middle()

    def encoder_first(at):
        encoder.norm_back(at, True, None)
    totals[6].finish(encoder_first)
    sums["e_up"].join()
    sums["d_down"].pass_on()
    sums["d_up"].pass_on()
    sums["d_qkv"].last()
    sums["d_out"].last()
    vector_store(vector_grad, 0, ref["e_sums"][0:1], True)
    vector_store(vector_grad, 1, ref["e_sums"][1:2], True)
    vector_store(vector_grad, 5, ref["d_sums"][0:1], False)
    vector_store(vector_grad, 6, ref["d_sums"][1:2], False)

    def mask_sum(at, total):
        part = pl.ds(pl.multiple_of(at * 64, 64), 64)
        hidden_row = ref["rank_column"][part] < 0
        return total + jnp.sum(jnp.where(hidden_row, grad[part], 0.0), axis=0, keepdims=True)
    token_grad = lax.fori_loop(0, rows // 64, mask_sum, jnp.zeros((1, dec_width), F32))
    vector_store(vector_grad, 4, token_grad, False)
    sums["vector"].start()
    rank = ref["rank_column"][mine]
    here = (lax.broadcasted_iota(jnp.int32, (own, shown), 1) == rank).astype(BF16)

    def place_grad(part):
        values = encoder_grad[:, part]
        top = values.astype(BF16)
        rest = (values - top.astype(F32)).astype(BF16)
        ref["grad_patches"][:, part] = dot(here, top) + dot(here, rest)
    each(width, 256, place_grad)
    sums["e_out"].join()
    sums["embed"].join()
    sums["d_qkv"].pass_on()
    sums["d_out"].pass_on()
    sums["vector"].middle()
    sums["e_down"].last()
    sums["e_qkv"].join()
    sums["vector"].join()
    sums["e_down"].pass_on()
    sums["e_up"].last()
    sums["e_out"].last()
    sums["embed"].last()
    sums["e_up"].pass_on()
    sums["e_qkv"].last()
    sums["e_out"].pass_on()
    sums["embed"].pass_on()

    def vector_out(part, whole):
        ref["grad_vector"][part] = whole
    sums["vector"].total(vector_out)
    sums["vector"].drain()
    sums["e_qkv"].pass_on()
    for name in MESSAGES:
        sums[name].close()
    last_first.wait_send()
    last_second.wait_send()
    for name in order:
        units[name].drain()
    for gathered in shared.values():
        gathered.drain()


def unpack_kernel(names, *refs):
    ref = dict(zip(names, refs))
    side = lax.rem(lax.axis_index("dp"), 2)
    ref["decoded"][...] = ref["i_decoded"][...]
    ref["grad_patches"][...] = ref["i_grad_patches"][...]
    vectors = ref["i_grad_vector"][...]
    for at, name in enumerate(("e_gain_a", "e_bias_a", "e_gain_b", "e_bias_b")):
        ref[name][...] = vectors[at:at + 1, :]
    for at, name in enumerate(("mask", "d_gain_a", "d_bias_a", "d_gain_b", "d_bias_b")):
        row = vectors[at + 4:at + 5, :]
        ref[name][...] = jnp.where(side == 0, row[:, 0:64], row[:, 64:128])
    for blk in range(PARTS):
        part = 3 * blk % PARTS
        for key in ("e_", "d_"):
            size = ref[key + "query"].shape[1] // PARTS
            for place, kind in enumerate(("query", "key", "value")):
                ref[key + kind][:, part * size:(part + 1) * size] = ref["i_" + key + "qkv"][
                    blk, :, place * size:(place + 1) * size].astype(F32)
        size = ref["i_e_up"].shape[1]
        for owner in range(8):
            column = (owner * PARTS + blk) * size
            ref["e_up"][:, column:column + size] = ref["i_e_up"][
                blk, :, owner * size:(owner + 1) * size].astype(F32)
        size = ref["i_e_down"].shape[1]
        ref["e_down"][blk * size:(blk + 1) * size, :] = ref["i_e_down"][blk].astype(F32)
        for name in ("embed", "d_up", "e_out"):
            size = ref["i_" + name].shape[2]
            ref[name][:, part * size:(part + 1) * size] = ref["i_" + name][blk].astype(F32)
    for name in ROW_SUMS:
        ref[name][...] = ref["i_" + name][...].astype(F32)


def local_kernel(*arguments):
    (patches, lengths, gsd_scale, visible,
     e_gain_a, e_bias_a, e_query, e_key, e_value, e_out, e_gain_b, e_bias_b, e_up, e_down,
     embed, mask,
     d_gain_a, d_bias_a, d_query, d_key, d_value, d_out, d_gain_b, d_bias_b, d_up, d_down,
     cotangent) = arguments
    width, dec_width = patches.shape[1], cotangent.shape[1]
    hidden, dec_hidden = e_up.shape[1], d_up.shape[1]
    rows = visible.shape[1]
    inputs = {
        "lengths": lengths, "gsd": gsd_scale, "visible": visible,
        "patches": patches, "cotangent": cotangent,
        "query": e_query, "key": e_key, "value": e_value, "out": e_out, "up": e_up,
        "down": e_down, "embed": embed, "dec_query": d_query, "dec_key": d_key,
        "dec_value": d_value, "dec_out": d_out, "dec_up": d_up, "dec_down": d_down,
    }
    inputs.update(zip(VECTOR_NAMES, (
        e_gain_a, e_bias_a, e_gain_b, e_bias_b, mask, d_gain_a, d_bias_a, d_gain_b, d_bias_b)))
    units = unit_shapes(width, dec_width, hidden, dec_hidden)
    shapes = {
        "decoded": (cotangent.shape, BF16), "grad_patches": (patches.shape, F32),
        "grad_vector": ((VECTORS, 128), F32),
    }
    for name in COLUMN_UNITS:
        shapes[name] = ((PARTS,) + units[name], BF16)
    for name in ROW_SUMS:
        shapes[name] = (units[name], BF16)
    shapes["e_out"] = ((PARTS, width // 8, width // PARTS), BF16)
    table = scratch_table(width, dec_width, hidden, dec_hidden, rows, SHOWN)
    names = INPUTS + tuple("o_" + name if name in MESSAGES else name for name in RESULTS)
    names = names + tuple(table) + tuple("s_" + name for name in SEMAPHORES)
    spaces = {"lengths": pltpu.SMEM, "gsd": pltpu.SMEM, "visible": pltpu.VMEM}
    spaces.update({name: pltpu.VMEM for name in VECTOR_NAMES})
    results = pl.pallas_call(
        functools.partial(main_kernel, names),
        out_shape=[jax.ShapeDtypeStruct(*shapes[name]) for name in RESULTS],
        in_specs=[pl.BlockSpec(memory_space=spaces.get(name, pl.ANY)) for name in INPUTS],
        out_specs=[
            pl.BlockSpec(memory_space=pl.ANY if name in MESSAGES else pltpu.VMEM)
            for name in RESULTS
        ],
        scratch_shapes=[pltpu.VMEM(*entry) for entry in table.values()]
        + [pltpu.SemaphoreType.DMA(shape) for shape in SEMAPHORES.values()],
        compiler_params=pltpu.CompilerParams(
            collective_id=0, has_side_effects=True, vmem_limit_bytes=62 * MIB
        ),
    )(*(inputs[name] for name in INPUTS))
    made = {"i_" + name: result for name, result in zip(RESULTS, results)}
    finals = {
        "decoded": (cotangent.shape, BF16), "grad_patches": (patches.shape, F32),
    }
    for key, wide, deep in (("e_", width, hidden), ("d_", dec_width, dec_hidden)):
        small, tall = wide // 8, deep // 8
        if key == "d_":
            finals["embed"] = ((width // 8, dec_width), F32)
            finals["mask"] = ((1, small), F32)
        for name, shape in (
            ("gain_a", (1, small)), ("bias_a", (1, small)), ("query", (small, wide)),
            ("key", (small, wide)), ("value", (small, wide)), ("out", (small, wide)),
            ("gain_b", (1, small)), ("bias_b", (1, small)), ("up", (small, deep)),
            ("down", (tall, wide)),
        ):
            finals[key + name] = (shape, F32)
    outputs = pl.pallas_call(
        functools.partial(unpack_kernel, tuple(made) + tuple(finals)),
        out_shape=[jax.ShapeDtypeStruct(*entry) for entry in finals.values()],
        in_specs=[pl.BlockSpec(memory_space=pltpu.VMEM)] * len(made),
        out_specs=[pl.BlockSpec(memory_space=pltpu.VMEM)] * len(finals),
        compiler_params=pltpu.CompilerParams(vmem_limit_bytes=62 * MIB),
    )(*made.values())
    return tuple(
        output.reshape(-1) if output.shape[0] == 1 else output for output in outputs
    )


def solution(mesh):
    both, vec, mat = P(("dp", "blk"), None), P("dp"), P("dp", None)
    block = (vec, vec, mat, mat, mat, mat, vec, vec, mat, mat)
    in_specs = (both, mat, mat, mat) + block + (mat, vec) + block + (both,)
    out_specs = (both, both) + block + (mat, vec) + block
    body = local_kernel if mesh.shape["dp"] == 8 and mesh.shape["blk"] == 4 else local
    return jax.shard_map(body, mesh=mesh, in_specs=in_specs, out_specs=out_specs, check_vma=False)
```

```python
import functools
import math

import jax
import jax.numpy as jnp
from jax import lax
from jax.experimental import pallas as pl
from jax.experimental.pallas import tpu as pltpu
from jax.sharding import PartitionSpec as P

HEADS = 16
EPSILON = 1e-06
MASKED_SCORE = -1e30
F32 = jnp.float32
BF16 = jnp.bfloat16


def dot(left, right):
    return lax.dot_general(left, right, (((1,), (0,)), ((), ())), preferred_element_type=F32)


def dot_t(left, right):
    return lax.dot_general(left, right, (((0,), (0,)), ((), ())), preferred_element_type=F32)


def dot_b(left, right):
    return lax.dot_general(left, right, (((1,), (1,)), ((), ())), preferred_element_type=F32)


def sincos(scaled, width):
    half_width = width // 2
    frequency = jnp.exp(
        jnp.arange(half_width, dtype=F32) * (-math.log(10000.0) / half_width)
    )
    angles = scaled[:, None] * frequency[None, :]
    return jnp.concatenate([jnp.sin(angles), jnp.cos(angles)], axis=1)


def norm_parts(values):
    center = values - jnp.mean(values, axis=-1, keepdims=True)
    spread = jnp.mean(center * center, axis=-1, keepdims=True)
    scale = lax.rsqrt(spread + EPSILON)
    return center * scale, scale


def norm_back(grad, unit, scale, gain):
    grad_gain = jnp.sum(grad * unit, axis=0, keepdims=True)
    grad_bias = jnp.sum(grad, axis=0, keepdims=True)
    inner = grad * gain
    mean_inner = jnp.mean(inner, axis=-1, keepdims=True)
    mean_cross = jnp.mean(inner * unit, axis=-1, keepdims=True)
    return scale * (inner - mean_inner - unit * mean_cross), grad_gain, grad_bias


def gelu_both(upper):
    phi = 0.5 * (1.0 + lax.erf(upper * math.sqrt(0.5)))
    density = jnp.exp(-0.5 * upper * upper) * (1.0 / math.sqrt(2.0 * math.pi))
    return upper * phi, phi + upper * density


def head_forward(queries, key_rows, values, allowed, scaling):
    scores = jnp.where(allowed, dot_b(queries, key_rows) * scaling, MASKED_SCORE)
    largest = jnp.max(scores, axis=-1, keepdims=True)
    exponent = jnp.exp(scores - largest)
    softmaxed = exponent / jnp.sum(exponent, axis=-1, keepdims=True)
    return softmaxed, dot(softmaxed.astype(BF16), values).astype(BF16)


def head_backward(queries, key_rows, values, softmaxed, grad_mixture, scaling):
    grad_values = dot_t(softmaxed.astype(BF16), grad_mixture).astype(BF16)
    grad_probs = dot_b(grad_mixture, values)
    delta = jnp.sum(softmaxed * grad_probs, axis=-1, keepdims=True)
    grad_scores = (softmaxed * (grad_probs - delta)).astype(BF16)
    grad_queries = (dot(grad_scores, key_rows) * scaling).astype(BF16)
    grad_keys = (dot_t(grad_scores, queries) * scaling).astype(BF16)
    return grad_queries, grad_keys, grad_values


def block_forward(residual, params, heads, allowed, total):
    gain_a, bias_a, w_query, w_key, w_value, w_out, gain_b, bias_b, w_up, w_down = params
    unit_a, scale_a = norm_parts(residual)
    normed = (unit_a * gain_a + bias_a).astype(BF16)
    queries = dot(normed, w_query).astype(BF16)
    key_rows = dot(normed, w_key).astype(BF16)
    values = dot(normed, w_value).astype(BF16)
    size = queries.shape[1] // heads
    scaling = 1.0 / math.sqrt(size)
    probs, mixed = [], []
    for head in range(heads):
        part = slice(head * size, (head + 1) * size)
        softmaxed, mixture = head_forward(
            queries[:, part], key_rows[:, part], values[:, part], allowed, scaling
        )
        probs.append(softmaxed)
        mixed.append(mixture)
    mixture = jnp.concatenate(mixed, axis=1)
    middle = residual + total(dot(mixture, w_out))
    unit_b, scale_b = norm_parts(middle)
    lifted = (unit_b * gain_b + bias_b).astype(BF16)
    hidden, slope = gelu_both(dot(lifted, w_up))
    hidden = hidden.astype(BF16)
    result = middle + total(dot(hidden, w_down))
    return result, (
        unit_a, scale_a, normed, queries, key_rows, values, probs, mixture,
        unit_b, scale_b, lifted, slope, hidden,
    )


def block_backward(grad_result, params, heads, saved, total):
    gain_a, bias_a, w_query, w_key, w_value, w_out, gain_b, bias_b, w_up, w_down = params
    (unit_a, scale_a, normed, queries, key_rows, values, probs, mixture,
     unit_b, scale_b, lifted, slope, hidden) = saved
    size = queries.shape[1] // heads
    scaling = 1.0 / math.sqrt(size)
    grad_branch = grad_result.astype(BF16)
    grad_down = dot_t(hidden, grad_branch)
    grad_upper = (dot_b(grad_branch, w_down) * slope).astype(BF16)
    grad_up = dot_t(lifted, grad_upper)
    grad_lifted = total(dot_b(grad_upper, w_up))
    grad_in, grad_gain_b, grad_bias_b = norm_back(grad_lifted, unit_b, scale_b, gain_b)
    grad_middle = grad_result + grad_in
    grad_attention = grad_middle.astype(BF16)
    grad_out = dot_t(mixture, grad_attention)
    grad_mixture = dot_b(grad_attention, w_out).astype(BF16)
    pieces = []
    for head in range(heads):
        part = slice(head * size, (head + 1) * size)
        pieces.append(
            head_backward(
                queries[:, part], key_rows[:, part], values[:, part], probs[head],
                grad_mixture[:, part], scaling,
            )
        )
    grad_queries, grad_keys, grad_values = (
        jnp.concatenate([piece[at] for piece in pieces], axis=1) for at in range(3)
    )
    grad_normed = total(
        dot_b(grad_queries, w_query) + dot_b(grad_keys, w_key) + dot_b(grad_values, w_value)
    )
    grad_in, grad_gain_a, grad_bias_a = norm_back(grad_normed, unit_a, scale_a, gain_a)
    return grad_middle + grad_in, (
        grad_gain_a, grad_bias_a, dot_t(normed, grad_queries), dot_t(normed, grad_keys),
        dot_t(normed, grad_values), grad_out, grad_gain_b, grad_bias_b, grad_up, grad_down,
    )


def layout(lengths_row, gsd_row, visible_row):
    count = visible_row.shape[0]
    positions = jnp.arange(count, dtype=jnp.int32)
    image_ends = jnp.cumsum(lengths_row)
    image_starts = image_ends - lengths_row
    image_ids = jnp.sum((positions[:, None] >= image_ends[None, :]).astype(jnp.int32), axis=1)
    onehot = image_ids[:, None] == jnp.arange(lengths_row.shape[0], dtype=jnp.int32)[None, :]
    first_row = jnp.sum(jnp.where(onehot, image_starts[None, :], 0), axis=1)
    ratio = jnp.sum(jnp.where(onehot, gsd_row[None, :], 0.0), axis=1)
    scaled = (positions - first_row).astype(F32) * ratio
    shown = visible_row > 0
    earlier = (positions[None, :] <= positions[:, None]) & shown[None, :]
    rank = jnp.where(shown, jnp.sum(earlier.astype(jnp.int32), axis=1) - 1, -1)
    return image_ids, scaled, rank


def spread_rows(grad, rank, offset, rows):
    own = lax.dynamic_slice_in_dim(rank, offset, rows)
    place = (own[:, None] == jnp.arange(grad.shape[0], dtype=jnp.int32)[None, :]).astype(BF16)
    high = grad.astype(BF16)
    low = (grad - high.astype(F32)).astype(BF16)
    return dot(place, high) + dot(place, low)


SHOWN = 128


def local(*arguments):
    patches, lengths, gsd_scale, visible = arguments[:4]
    encoder_shards = arguments[4:14]
    embed_shard, mask_shard = arguments[14:16]
    decoder_shards = arguments[16:26]
    cotangent = arguments[26]
    dp_count = lax.axis_size("dp")
    blk_count = lax.axis_size("blk")
    blk = lax.axis_index("blk")
    dp = lax.axis_index("dp")
    rows = patches.shape[0]
    offset = blk * rows
    heads = HEADS // blk_count
    image_ids, scaled, rank = layout(lengths[0], gsd_scale[0], visible[0])
    shown = rank >= 0
    places = rank[None, :] == jnp.arange(SHOWN, dtype=jnp.int32)[:, None]
    packed_ids = jnp.sum(jnp.where(places, image_ids[None, :], 0), axis=1)
    packed_scaled = jnp.sum(jnp.where(places, scaled[None, :], 0.0), axis=1)

    def gather(shard):
        return lax.all_gather(shard, "dp", axis=0, tiled=True)

    def by_columns(shard):
        width = shard.shape[1] // blk_count
        return gather(lax.dynamic_slice_in_dim(shard, blk * width, width, axis=1))

    def by_rows(shard):
        whole = gather(shard)
        height = whole.shape[0] // blk_count
        return lax.dynamic_slice_in_dim(whole, blk * height, height, axis=0)

    def vector(shard):
        return gather(shard).astype(F32)[None, :]

    def load(shards):
        kinds = (vector, vector, by_columns, by_columns, by_columns, by_rows,
                 vector, vector, by_columns, by_rows)
        return tuple(kind(shard) for kind, shard in zip(kinds, shards))

    def total(partial):
        return lax.psum(partial, "blk")

    def sum_columns(grad):
        summed = lax.psum_scatter(grad.astype(BF16), "dp", scatter_dimension=0, tiled=True)
        return lax.all_gather(summed, "blk", axis=1, tiled=True).astype(F32)

    def sum_rows(grad):
        whole = lax.all_gather(grad.astype(BF16), "blk", axis=0, tiled=True)
        return lax.psum_scatter(whole, "dp", scatter_dimension=0, tiled=True).astype(F32)

    def sum_vector(grad):
        return lax.psum_scatter(grad[0], "dp", scatter_dimension=0, tiled=True)

    def reduce(grads):
        kinds = (sum_vector, sum_vector, sum_columns, sum_columns, sum_columns, sum_rows,
                 sum_vector, sum_vector, sum_columns, sum_rows)
        return tuple(kind(grad) for kind, grad in zip(kinds, grads))

    group = lax.all_gather(patches, "blk", axis=0, tiled=True)
    picked = dot(places.astype(BF16), group)
    encoder = load(encoder_shards)
    residual = picked + sincos(packed_scaled, patches.shape[1])
    encoded, encoder_saved = block_forward(
        residual, encoder, heads, packed_ids[:, None] == packed_ids[None, :], total
    )
    embed = gather(embed_shard)
    lowered = encoded.astype(BF16)
    embedded = dot(lowered, embed)
    high = embedded.astype(BF16)
    low = (embedded - high.astype(F32)).astype(BF16)
    places_b = places.astype(BF16)
    start = jnp.where(
        shown[:, None], dot_t(places_b, high) + dot_t(places_b, low), vector(mask_shard)
    ) + sincos(scaled, embed.shape[1])
    decoder = load(decoder_shards)
    decoded, decoder_saved = block_forward(
        start, decoder, heads, image_ids[:, None] == image_ids[None, :], total
    )
    decoded_rows = lax.dynamic_slice_in_dim(decoded, offset, rows).astype(BF16)
    grad_out = lax.all_gather(cotangent, "blk", axis=0, tiled=True).astype(F32)
    grad_start, decoder_grads = block_backward(grad_out, decoder, heads, decoder_saved, total)
    grad_mask = jnp.sum(jnp.where(shown[:, None], 0.0, grad_start), axis=0, keepdims=True)
    grad_embedded = dot(places_b, grad_start.astype(BF16)).astype(BF16)
    width = embed.shape[1] // blk_count
    grad_embed = dot_t(
        lowered, lax.dynamic_slice_in_dim(grad_embedded, blk * width, width, axis=1)
    )
    grad_encoded = dot_b(grad_embedded, embed)
    grad_residual, encoder_grads = block_backward(
        grad_encoded, encoder, heads, encoder_saved, total
    )
    grad_patches = spread_rows(grad_residual, rank, offset, rows)
    return (
        (decoded_rows, grad_patches) + reduce(encoder_grads)
        + (sum_columns(grad_embed), sum_vector(grad_mask)) + reduce(decoder_grads)
    )


MIB = 2**20
DECODER_ROWS = 512
PARTS = 4
SIDES = 2
VECTORS = 16


class Split:
    def __init__(self):
        self.dp = lax.axis_index("dp")
        self.blk = lax.axis_index("blk")
        self.z = lax.div(self.dp, 2)
        self.y = lax.rem(self.dp, 2)
        self.x = lax.div(self.blk, 2)
        self.core = lax.rem(self.blk, 2)
        self.part = lax.rem(3 * self.blk, PARTS)
        self.y_peer = (self.z * 2 + 1 - self.y, self.blk)
        self.core_peer = (self.dp, self.x * 2 + 1 - self.core)
        self.x_peer = (self.dp, (1 - self.x) * 2 + self.core)
        self.far_peer = (self.dp, (1 - self.x) * 2 + 1 - self.core)
        self.blk_peers = (self.core_peer, self.x_peer, self.far_peer)

    def ahead(self, step):
        return lax.rem(self.z + step, PARTS)

    def behind(self, step):
        return lax.rem(self.z + PARTS - step, PARTS)

    def z_peer(self, step):
        return (self.ahead(step) * 2 + self.y, self.blk)

    def at_z(self, z):
        return (z * 2 + self.y, self.blk)

    def inward(self, step):
        high = lax.div(self.z, 2)
        return lax.rem(self.z + high * (PARTS - step) + (1 - high) * step, PARTS)

    @property
    def inner(self):
        return jnp.logical_or(self.z == 1, self.z == 2)

    @property
    def near_end(self):
        return jnp.where(self.inner, 3 * self.z - 3, lax.div(self.z, 3) + 1)

    @property
    def far_end(self):
        return 6 - 3 * self.z


def remote(source, target, sent, received, device):
    return pltpu.make_async_remote_copy(
        src_ref=source, dst_ref=target, send_sem=sent, recv_sem=received,
        device_id=device, device_id_type=pl.DeviceIdType.MESH,
    )


def span(at, size):
    return pl.ds(pl.multiple_of(at, size), size)


class Columns:
    def __init__(self, split, whole, rows, local, sems, columns=None):
        self.split, self.whole, self.rows, self.local = split, whole, rows, local
        self.columns = columns
        self.z_sent, self.z_got, self.y_sent, self.y_got = sems[:4]
        self.cross_sent, self.cross_got = sems[4:]

    def view(self, rows):
        if self.columns is None:
            return self.whole.at[rows]
        return self.whole.at[rows, self.columns]

    def block(self, z, y):
        return self.view(span((z * 2 + y) * self.rows, self.rows))

    def lane(self, crossed):
        s = self.split
        if crossed:
            return 1 - s.y, self.cross_sent, self.cross_got
        return s.y, self.z_sent, self.z_got

    def z_copy(self, step, crossed=False):
        s = self.split
        y, sent, got = self.lane(crossed)
        block = self.block(s.z, y)
        return remote(block, block, sent, got.at[s.z], s.at_z(s.inward(step)))

    def z_arrival(self, z, crossed=False):
        y, sent, got = self.lane(crossed)
        block = self.block(z, y)
        return remote(block, block, sent, got.at[z], self.split.y_peer)

    def relay(self, crossed=False):
        s = self.split
        y, sent, got = self.lane(crossed)
        block = self.block(s.far_end, y)
        return remote(block, block, sent, got.at[s.far_end], s.at_z(s.near_end))

    def y_copy(self, z, at):
        s = self.split
        block = self.block(z, s.y)
        return remote(block, block, self.y_sent, self.y_got.at[at], s.y_peer)

    def y_arrival(self, z, at):
        s = self.split
        block = self.block(z, 1 - s.y)
        return remote(block, block, self.y_sent, self.y_got.at[at], s.y_peer)

    def sent(self, sem, count):
        blocks = self.view(pl.ds(0, count * self.rows))
        remote(blocks, blocks, sem, self.y_got.at[0], self.split.y_peer).wait_send()

    def fetch(self):
        for copy in self.local:
            copy.start()

    def spread(self, crossed=False):
        self.z_copy(1, crossed).start()
        self.z_copy(2, crossed).start()

        @pl.when(self.split.inner)
        def _():
            self.z_copy(3, crossed).start()

    def collect(self, step, crossed=False):
        s = self.split
        z = s.inward(step)
        self.z_arrival(z, crossed).wait_recv()
        if step == 2:
            @pl.when(s.inner)
            def _():
                self.relay(crossed).start()
        return z

    def send(self, y_too=True):
        for copy in self.local:
            copy.wait()
        self.spread()
        if y_too:
            self.send_y()

    def send_y(self):
        self.y_copy(self.split.z, 0).start()

    def forward(self, steps=(1, 2, 3)):
        for step in steps:
            self.y_copy(self.collect(step), step).start()

    def finish(self):
        for step in range(PARTS):
            self.y_arrival(self.split.inward(step), step).wait_recv()

    def drain_z(self, sem):
        @pl.when(self.split.inner)
        def _():
            self.sent(sem, 4)

        @pl.when(jnp.logical_not(self.split.inner))
        def _():
            self.sent(sem, 2)

    def drain(self):
        self.drain_z(self.z_sent)
        self.sent(self.y_sent, PARTS)


class EarlyColumns(Columns):
    def cross(self):
        s = self.split
        self.y_arrival(s.z, 0).wait_recv()
        self.spread(True)

    def forward(self, steps=(1, 2, 3)):
        for step in steps:
            self.collect(step)

    def finish(self, steps=(1, 2, 3)):
        for step in steps:
            self.collect(step, True)

    def drain(self):
        self.drain_z(self.z_sent)
        self.drain_z(self.cross_sent)
        self.sent(self.y_sent, 1)


class Shared:
    def __init__(self, split, source, block, sems):
        self.split, self.source, self.block = split, source, block
        self.sents, self.gots = sems

    def copy(self, which):
        s = self.split
        if which == 2:
            block = self.block(s.x_peer[1])
            return remote(block, block, self.sents.at[2], self.gots.at[2], s.core_peer)
        return remote(self.source, self.block(s.blk), self.sents.at[which],
                      self.gots.at[which], s.blk_peers[which])

    def arrival(self, which):
        s = self.split
        block = self.block(s.blk_peers[which][1])
        return remote(block, block, self.sents.at[which], self.gots.at[which], s.core_peer)

    def start(self):
        self.copy(1).start()
        self.copy(0).start()

    def pass_on(self):
        self.arrival(1).wait_recv()
        self.copy(2).start()

    def finish(self):
        self.arrival(0).wait_recv()
        self.arrival(2).wait_recv()

    def drain(self):
        for which in range(3):
            self.copy(which).wait_send()


class Rows:
    def __init__(self, split, whole, rows, local, sems):
        self.split, self.whole, self.rows, self.local = split, whole, rows, local
        self.z_sent, self.z_got, self.y_sent, self.y_got = sems[:4]

    def block(self, y):
        return self.whole.at[span(y * self.rows, self.rows)]

    def z_copy(self, way):
        s = self.split
        return remote(self.block(s.y), self.block(s.y), self.z_got.at[1 + way],
                      self.z_got.at[0], s.at_z(s.z + 1 - 2 * way))

    def pass_on(self, act):
        s = self.split

        @pl.when(jnp.logical_and(s.z >= s.part, s.z < PARTS - 1))
        def _():
            act(self.z_copy(0))

        @pl.when(jnp.logical_and(s.z <= s.part, s.z > 0))
        def _():
            act(self.z_copy(1))

    def y_copy(self):
        s = self.split
        return remote(self.block(s.y), self.block(s.y), self.y_sent,
                      self.y_got.at[0], s.y_peer)

    def fetch(self):
        @pl.when(self.split.z == self.split.part)
        def _():
            self.local.start()

    def send(self):
        @pl.when(self.split.z == self.split.part)
        def _():
            self.local.wait()
            self.pass_on(lambda copy: copy.start())
            self.y_copy().start()

    def forward(self):
        s = self.split

        @pl.when(s.z != s.part)
        def _():
            remote(self.block(s.y), self.block(s.y), self.z_sent,
                   self.z_got.at[0], s.y_peer).wait_recv()
            self.pass_on(lambda copy: copy.start())
            self.y_copy().start()

    def finish(self):
        s = self.split
        block = self.block(1 - s.y)
        remote(block, block, self.y_sent, self.y_got.at[0], s.y_peer).wait_recv()

    def drain(self):
        self.pass_on(lambda copy: copy.wait_send())
        self.y_copy().wait_send()


def each(count, step, body, base=0):
    @pl.loop(0, count // step)
    def _(at):
        body(pl.ds(pl.multiple_of(base + at * step, step), step))


class ColumnSum:
    def __init__(self, split, grad, met, came, done, sems, step):
        self.split, self.grad, self.met, self.came, self.done = split, grad, met, came, done
        self.y_sent, self.y_got, self.z_sent, self.z_got, self.b_sent, self.b_got = sems
        self.step = step

    def y_copy(self):
        s = self.split
        return remote(self.grad.at[:, 1 - s.y], self.met, self.y_sent, self.y_got, s.y_peer)

    def z_copy(self, step):
        s = self.split
        target = s.inward(step)
        return remote(self.met.at[target], self.came.at[s.z], self.z_sent.at[step - 1],
                      self.z_got.at[s.z], s.at_z(target))

    def z_arrival(self, z):
        s = self.split
        return remote(self.met.at[z], self.came.at[z], self.z_sent.at[0], self.z_got.at[z],
                      s.y_peer)

    def relay(self):
        s = self.split
        return remote(self.met.at[3 - s.z], self.came.at[s.near_end], self.z_sent.at[2],
                      self.z_got.at[s.near_end], s.at_z(s.near_end))

    def b_copy(self, which):
        s = self.split
        if which == 2:
            block = self.done.at[s.x_peer[1]]
            return remote(block, block, self.b_sent.at[2], self.b_got.at[2], s.core_peer)
        return remote(self.met.at[s.z], self.done.at[s.blk], self.b_sent.at[which],
                      self.b_got.at[which], s.blk_peers[which])

    def b_arrival(self, which):
        s = self.split
        block = self.done.at[s.blk_peers[which][1]]
        return remote(block, block, self.b_sent.at[which], self.b_got.at[which],
                      s.blk_peers[which])

    def own_copy(self):
        s = self.split
        return pltpu.make_async_copy(self.met.at[s.z], self.done.at[s.blk], self.b_sent.at[3])

    def start(self):
        self.y_copy().start()

    def add(self, z):
        def body(rows):
            both = self.grad[z, self.split.y, rows].astype(F32) + self.met[z, rows].astype(F32)
            self.met[z, rows] = both.astype(self.met.dtype)
        each(self.met.shape[1], self.step, body)

    def arrive(self):
        self.y_copy().wait_recv()

    def middle(self):
        s = self.split
        self.arrive()

        @pl.when(s.inner)
        def _():
            self.add(s.inward(1))
            self.z_copy(1).start()
            self.add(s.inward(3))
            self.z_copy(3).start()
            self.add(s.inward(2))

        @pl.when(jnp.logical_not(s.inner))
        def _():
            self.add(3 - s.z)
            self.relay().start()
            self.add(s.inward(2))
            self.z_copy(2).start()
            self.add(s.inward(1))
            self.z_copy(1).start()
        self.add(s.z)

    def join(self):
        s = self.split

        @pl.when(s.inner)
        def _():
            target = s.inward(2)
            self.z_arrival(s.z).wait_recv()

            def body(rows):
                both = self.met[target, rows].astype(F32) + self.came[s.z, rows].astype(F32)
                self.met[target, rows] = both.astype(self.met.dtype)
            each(self.met.shape[1], self.step, body)
            self.z_copy(2).start()

    def total(self, store):
        s = self.split

        @pl.when(s.inner)
        def _():
            sources = (0, 3, 3 - s.z)
            for z in sources:
                self.z_arrival(z).wait_recv()

            def body(rows):
                whole = self.met[s.z, rows].astype(F32)
                for z in sources:
                    whole = whole + self.came[z, rows].astype(F32)
                store(rows, whole)
            each(self.met.shape[1], self.step, body)

        @pl.when(jnp.logical_not(s.inner))
        def _():
            for z in (1, 2):
                self.z_arrival(z).wait_recv()

            def body(rows):
                whole = self.met[s.z, rows].astype(F32)
                for z in (1, 2):
                    whole = whole + self.came[z, rows].astype(F32)
                store(rows, whole)
            each(self.met.shape[1], self.step, body)

    def last(self):
        s = self.split

        def store(rows, whole):
            self.met[s.z, rows] = whole.astype(self.met.dtype)
        self.total(store)
        self.b_copy(1).start()
        self.b_copy(0).start()
        self.own_copy().start()

    def pass_on(self):
        self.b_arrival(1).wait_recv()
        self.b_copy(2).start()

    def close(self):
        self.b_arrival(0).wait_recv()
        self.b_arrival(2).wait_recv()
        for which in range(3):
            self.b_copy(which).wait_send()
        self.own_copy().wait()
        self.drain()

    def drain_y(self):
        self.y_copy().wait_send()

    def drain(self):
        self.drain_y()
        for step in (1, 2, 3):
            self.z_copy(step).wait_send()


class ProductSum(ColumnSum):
    def trade(self, left, right, their_left, their_right, sems, told=None, heard=None, after=None):
        self.left, self.right = left, right
        self.their_left, self.their_right = their_left, their_right
        self.told = right if told is None else told
        self.heard = their_right if heard is None else heard
        self.tells = told is not False
        self.after = after
        self.t_sent, self.t_got = sems
        self.width = their_left.shape[2]

    def columns(self, z, y):
        return self.left.at[:, span((z * 2 + y) * self.width, self.width)]

    def left_copy(self, z):
        s = self.split
        return remote(self.columns(z, 1 - s.y), self.their_left.at[z], self.t_sent.at[0],
                      self.t_got.at[0], s.y_peer)

    def left_copies(self):
        return remote(self.their_left, self.their_left, self.t_sent.at[0], self.t_got.at[0],
                      self.split.y_peer)

    def right_copy(self):
        return remote(self.told, self.heard, self.t_sent.at[1], self.t_got.at[1],
                      self.split.y_peer)

    def start_left(self):
        for z in range(PARTS):
            self.left_copy(z).start()

    def start(self):
        self.right_copy().start()

    def add(self, z):
        both = dot_t(self.columns(z, self.split.y)[...], self.right[...]) + dot_t(
            self.their_left[z], self.their_right[...])
        self.met[z] = both.astype(self.met.dtype)

    def arrive(self):
        self.left_copies().wait_recv()
        if self.tells:
            self.right_copy().wait_recv()
        if self.after is not None:
            self.after()

    def drain_y(self):
        self.left_copies().wait_send()
        if self.tells:
            self.right_copy().wait_send()


class GatheredSum(ColumnSum):
    def gather(self, left, lefts, sems, right):
        self.left, self.lefts, self.right = left, lefts, right
        self.l_sent, self.l_got = sems
        self.count, self.width = lefts.shape[0], lefts.shape[2]

    def columns(self, owner):
        return self.left.at[:, span(owner * self.width, self.width)]

    def left_copy(self, step):
        s = self.split
        owner = lax.rem(s.dp + step, self.count)
        return remote(self.columns(owner), self.lefts.at[s.dp], self.l_sent, self.l_got,
                      (owner, s.blk))

    def left_copies(self):
        blocks = self.lefts.at[pl.ds(0, self.count - 1)]
        return remote(blocks, blocks, self.l_sent, self.l_got, self.split.y_peer)

    def start_left(self):
        for step in range(1, self.count):
            self.left_copy(step).start()
        self.lefts[self.split.dp] = self.columns(self.split.dp)[...]

    def last(self):
        s = self.split
        self.left_copies().wait_recv()
        zero = jnp.zeros(self.met.shape[1:], F32)

        def one(group, whole):
            return whole + dot_t(self.lefts[group], self.right(group))
        whole = lax.fori_loop(0, self.count, one, zero)
        self.met[s.z] = whole.astype(self.met.dtype)
        self.b_copy(1).start()
        self.b_copy(0).start()
        self.own_copy().start()

    def drain(self):
        self.left_copies().wait_send()


class RowSum:
    def __init__(self, split, grad, met, came, done, sems, step):
        self.split, self.grad, self.met, self.came, self.done = split, grad, met, came, done
        self.y_sent, self.y_got, self.z_sent, self.z_got, self.b_sent, self.b_got = sems
        self.step = step
        s = split
        self.home = lax.rem(3 * s.z, PARTS)
        self.at_home = s.z == s.part
        self.below = s.z < s.part
        self.above = s.z > s.part
        self.beside = s.x_peer[1] == self.home

    def y_copy(self):
        s = self.split
        return remote(self.grad.at[1 - s.y], self.met, self.y_sent, self.y_got, s.y_peer)

    def z_copy(self, way):
        s = self.split
        return remote(self.met, self.came.at[way], self.z_sent.at[way], self.z_got.at[way],
                      s.at_z(s.z + 1 - 2 * way))

    def z_arrival(self, way):
        return remote(self.met, self.came.at[way], self.z_sent.at[way], self.z_got.at[way],
                      self.split.y_peer)

    def b_copy(self, which):
        s = self.split
        source = self.done if which == 2 else self.met
        device = s.core_peer if which == 2 else s.blk_peers[which]
        return remote(source, self.done, self.b_sent.at[which], self.b_got.at[0], device)

    def own_copy(self):
        return pltpu.make_async_copy(self.met, self.done, self.b_sent.at[3])

    def start(self):
        self.y_copy().start()

    def send(self, act):
        @pl.when(self.below)
        def _():
            act(self.z_copy(0))

        @pl.when(self.above)
        def _():
            act(self.z_copy(1))

    def take(self, way):
        self.z_arrival(way).wait_recv()

        def body(rows):
            both = self.met[rows].astype(F32) + self.came[way, rows].astype(F32)
            self.met[rows] = both.astype(self.met.dtype)
        each(self.met.shape[0], self.step, body)

    def middle(self):
        s = self.split
        self.y_copy().wait_recv()

        def body(rows):
            both = self.grad[s.y, rows].astype(F32) + self.met[rows].astype(F32)
            self.met[rows] = both.astype(self.met.dtype)
        each(self.met.shape[0], self.step, body)

        @pl.when(jnp.logical_not(s.inner))
        def _():
            self.send(lambda copy: copy.start())

    def join(self):
        s = self.split

        @pl.when(s.inner)
        def _():
            @pl.when(self.below)
            def _():
                self.take(0)

            @pl.when(self.above)
            def _():
                self.take(1)
            self.send(lambda copy: copy.start())

    def last(self):
        s = self.split

        @pl.when(self.at_home)
        def _():
            @pl.when(s.z > 0)
            def _():
                self.take(0)

            @pl.when(s.z < PARTS - 1)
            def _():
                self.take(1)
            self.b_copy(1).start()
            self.b_copy(0).start()
            self.own_copy().start()

    def pass_on(self):
        @pl.when(self.beside)
        def _():
            self.b_copy(0).wait_recv()
            self.b_copy(2).start()

    def close(self):
        self.y_copy().wait_send()
        self.send(lambda copy: copy.wait_send())

        @pl.when(self.at_home)
        def _():
            self.b_copy(0).wait_send()
            self.b_copy(1).wait_send()
            self.own_copy().wait()

        @pl.when(self.beside)
        def _():
            self.b_copy(2).wait_send()

        @pl.when(jnp.logical_not(jnp.logical_or(self.at_home, self.beside)))
        def _():
            self.b_copy(0).wait_recv()


class Total:
    def __init__(self, split, part, met, out, came, whole, sems, slot):
        self.split, self.part, self.met, self.out = split, part, met, out
        self.came, self.whole = came.at[slot], whole
        self.sent, self.got = sems
        self.chunks = part.shape[0]
        self.high = part.shape[2]

    def first_copy(self, at):
        s = self.split
        return remote(self.part.at[at, 1 - s.core], self.met.at[at], self.sent.at[at, 0],
                      self.got.at[at, 0], s.core_peer)

    def second_copy(self, at):
        return remote(self.out.at[at], self.came.at[at], self.sent.at[at, 1],
                      self.got.at[at, 1], self.split.x_peer)

    def third_copy(self, at, half):
        s = self.split
        return remote(self.whole.at[at, half], self.whole.at[at, half], self.sent.at[at, 2],
                      self.got.at[at, 2], s.core_peer)

    def start(self, at):
        self.first_copy(at).start()

    def middle(self, at):
        s = self.split
        self.first_copy(at).wait_recv()

        def body(rows):
            both = self.part[at, s.core, rows] + self.met[at, rows]
            self.out[at, rows] = both.astype(BF16)
        each(self.high, 32, body)
        self.second_copy(at).start()

    def third(self, at):
        s = self.split
        self.second_copy(at).wait_recv()

        def body(rows):
            self.whole[at, s.core, rows] = self.out[at, rows].astype(
                F32) + self.came[at, rows].astype(F32)
        each(self.high, 32, body)
        self.third_copy(at, s.core).start()

    def fourth(self, at):
        s = self.split
        self.third_copy(at, 1 - s.core).wait_recv()
        self.first_copy(at).wait_send()
        self.second_copy(at).wait_send()
        self.third_copy(at, s.core).wait_send()

    def begin(self, produce):
        @pl.loop(0, self.chunks + 1)
        def _(at):
            @pl.when(at < self.chunks)
            def _():
                produce(at)
                self.start(at)

            @pl.when(at > 0)
            def _():
                self.middle(at - 1)

    def finish(self, consume):
        self.third(0)

        @pl.loop(0, self.chunks)
        def _(at):
            @pl.when(at + 1 < self.chunks)
            def _():
                self.third(at + 1)
            self.fourth(at)
            consume(at)


def head_mask(width, size, head):
    lanes = lax.broadcasted_iota(jnp.int32, (1, width), 1)
    return lax.div(lanes, size) == head


def keep(mask, values):
    return jnp.where(mask, values, jnp.zeros_like(values))


class Block:
    def __init__(self, rows, width, heads, size, names, refs, vectors):
        self.rows, self.width, self.heads, self.size = rows, width, heads, size
        self.share = heads * size
        self.scaling = 1.0 / math.sqrt(size)
        self.refs = refs
        self.vectors = vectors
        self.name = names
        self.tile = 32 * 1024 // width
        self.chunk = 2 * refs[names + "part"].shape[2]

    def ref(self, name):
        return self.refs[self.name + name]

    def row(self, at):
        return self.refs["gains"][self.vectors + at:self.vectors + at + 1, 0:self.width]

    def norm(self, first, base=0, count=None):
        unit, scale = self.ref("unit_a" if first else "unit_b"), self.ref(
            "scale_a" if first else "scale_b")
        out = self.ref("normed" if first else "lifted")
        gain, bias = self.row(0 if first else 2), self.row(1 if first else 3)
        residual = self.ref("residual")

        def body(rows):
            one, size = norm_parts(residual[rows])
            unit[rows] = one
            scale[rows] = size
            out[rows] = (one * gain + bias).astype(BF16)
        each(count or self.rows, self.tile, body, base)

    def project(self):
        normed, mixed, weight = self.ref("normed"), self.ref("qkv"), self.ref("w_qkv")

        def body(rows):
            mixed[rows] = dot(normed[rows], weight[...]).astype(BF16)
        each(self.rows, 128, body)

    def parts(self, rows):
        share, qkv = self.share, self.ref("qkv")
        return (qkv[rows, 0:share], qkv[rows, share:2 * share], qkv[rows, 2 * share:3 * share])

    def attend(self, ids_column, ids_row):
        probs, mixture = self.ref("probs"), self.ref("mixture")
        everything = pl.ds(0, self.rows)

        def body(queries):
            query = self.parts(queries)[0]
            unused, key_rows, values = self.parts(everything)
            allowed = ids_column[...] == ids_row[:, queries]

            def one(head, mixed):
                mask = head_mask(self.share, self.size, head)
                scores = jnp.where(
                    allowed, dot_b(keep(mask, key_rows), query) * self.scaling, MASKED_SCORE
                )
                exponent = jnp.exp(scores - jnp.max(scores, axis=0, keepdims=True))
                softmaxed = exponent * (1.0 / jnp.sum(exponent, axis=0, keepdims=True))
                probs[head, :, queries] = softmaxed
                return mixed + dot_t(keep(mask, values), softmaxed.astype(BF16))

            mixed = lax.fori_loop(0, self.heads, one, jnp.zeros((self.share, 128), F32))
            mixture[queries] = mixed.T.astype(BF16)
        each(self.rows, 128, body)

    def product(self, left, weight, back=False):
        target, deep = self.ref("part"), self.chunk

        def produce(at):
            rows = pl.ds(pl.multiple_of(at * deep, deep), deep)
            made = (dot_b if back else dot)(left[rows], weight[...])
            target[at, 0] = made[:deep // 2]
            target[at, 1] = made[deep // 2:]
        return produce

    def halves(self, rows):
        half = self.chunk // 2
        at = lax.div(rows.start, half)
        place = pl.ds(pl.multiple_of(lax.rem(rows.start, half), rows.size), rows.size)
        return self.ref("whole")[lax.div(at, 2), lax.rem(at, 2), place]

    def add_total(self, at):
        residual = self.ref("residual")

        def body(rows):
            residual[rows] = residual[rows] + self.halves(rows)
        each(self.chunk, self.tile, body, at * self.chunk)

    def expand(self, base=0, count=None):
        lifted, weight = self.ref("lifted"), self.ref("w_up")
        hidden, slope = self.ref("hidden"), self.ref("slope")

        def body(rows):
            def inner(columns):
                made, gradient = gelu_both(dot(lifted[rows], weight[:, columns]))
                hidden[rows, columns] = made.astype(BF16)
                slope[rows, columns] = gradient
            each(weight.shape[1], 256, inner)
        each(count or self.rows, 128, body, base)

    def back_hidden(self, branch, base=0, count=None):
        weight, slope, grad = self.ref("w_down"), self.ref("slope"), self.ref("grad_upper")

        def body(rows):
            def inner(columns):
                made = dot_b(branch[rows], weight[columns])
                grad[rows, columns] = (made * slope[rows, columns]).astype(BF16)
            each(weight.shape[0], 256, inner)
        each(count or self.rows, 128, body, base)

    def clear_sums(self):
        sums = self.ref("sums")
        sums[...] = jnp.zeros(sums.shape, F32)

    def norm_back(self, at, first, out):
        unit, scale = self.ref("unit_a" if first else "unit_b"), self.ref(
            "scale_a" if first else "scale_b")
        gain, grad, sums = self.row(0 if first else 2), self.ref("grad"), self.ref("sums")

        def body(rows):
            moved, gains, biases = norm_back(self.halves(rows), unit[rows], scale[rows], gain)
            new = grad[rows] + moved
            grad[rows] = new
            if out is not None:
                out[rows] = new.astype(BF16)
            sums[0:1] += gains
            sums[1:2] += biases
        each(self.chunk, self.tile, body, at * self.chunk)

    def back_mixture(self, branch, base=0, count=None):
        weight, grad = self.ref("w_out"), self.ref("grad_mixture")

        def body(rows):
            grad[rows] = dot_b(branch[rows], weight[...]).astype(BF16)
        each(count or self.rows, self.chunk, body, base)

    def attend_back(self):
        probs, grad_mixture, grads = self.ref("probs"), self.ref("grad_mixture"), self.ref(
            "grad_qkv")
        key_sum, value_sum = self.ref("key_sum"), self.ref("value_sum")
        share, everything = self.share, pl.ds(0, self.rows)
        key_sum[...] = jnp.zeros(key_sum.shape, F32)
        value_sum[...] = jnp.zeros(value_sum.shape, F32)

        def body(queries):
            query = self.parts(queries)[0]
            unused, key_rows, values = self.parts(everything)
            grad_rows = grad_mixture[queries]

            def one(head, total):
                mask = head_mask(share, self.size, head)
                softmaxed = probs[head, :, queries]
                grad_probs = dot_b(keep(mask, values), grad_rows)
                value_sum[...] += dot(softmaxed.astype(BF16), keep(mask, grad_rows))
                delta = jnp.sum(softmaxed * grad_probs, axis=0, keepdims=True)
                grad_scores = (softmaxed * (grad_probs - delta)).astype(BF16)
                key_sum[...] += dot(grad_scores, keep(mask, query))
                return total + dot_t(keep(mask, key_rows), grad_scores)

            total = lax.fori_loop(0, self.heads, one, jnp.zeros((share, 128), F32))
            grads[queries, 0:share] = (total.T * self.scaling).astype(BF16)
        each(self.rows, 128, body)

        def close(rows):
            grads[rows, share:2 * share] = (key_sum[rows] * self.scaling).astype(BF16)
            grads[rows, 2 * share:3 * share] = value_sum[rows].astype(BF16)
        each(self.rows, 128, close)


def weight_grad(left, right, target):
    if len(target.shape) == 4:
        parts, sides, rows, width = target.shape
        if rows >= 128:
            @pl.loop(0, parts * sides)
            def _(at):
                block = dot_t(left[:, span(at * rows, rows)], right[...])
                target[lax.div(at, sides), lax.rem(at, sides)] = block.astype(BF16)
        else:
            @pl.loop(0, parts)
            def _(at):
                block = dot_t(left[:, span(at * sides * rows, sides * rows)], right[...])
                target[at] = block.reshape(sides, rows, width).astype(BF16)
    else:
        sides, rows, width = target.shape
        if rows >= 128:
            @pl.loop(0, sides)
            def _(at):
                block = dot_t(left[:, span(at * rows, rows)], right[...])
                target[at] = block.astype(BF16)
        else:
            block = dot_t(left[...], right[...])
            target[...] = block.reshape(sides, rows, width).astype(BF16)


def vector_store(target, at, row, whole):
    for owner in range(8):
        block = owner if whole else owner // 2
        target[owner // 2, owner % 2, at:at + 1, :] = row[:, 128 * block:128 * block + 128]


COLUMN_UNITS = ("e_qkv", "e_up", "e_down", "embed", "d_qkv", "d_up")
ROW_UNITS = ("e_out", "d_out", "d_down")
ROW_SUMS = ("d_out", "d_down")
MESSAGES = COLUMN_UNITS + ROW_UNITS
TRADED = ("e_qkv", "e_up", "e_out")
GATHERED = ("e_down", "embed")
EARLY = ()


def unit_shapes(width, dec_width, hidden, dec_hidden):
    return {
        "e_qkv": (width // 8, 3 * width // 4),
        "e_up": (width // 8, hidden // 4),
        "e_down": (hidden // 32, width),
        "embed": (width // 8, dec_width // 4),
        "d_qkv": (dec_width // 8, 3 * dec_width // 4),
        "d_up": (dec_width // 8, dec_hidden // 4),
        "e_out": (width // 8, width),
        "d_out": (dec_width // 8, dec_width),
        "d_down": (dec_hidden // 8, dec_width),
    }


def scratch_table(width, dec_width, hidden, dec_hidden, rows, shown):
    units = unit_shapes(width, dec_width, hidden, dec_hidden)
    table = {}
    for name in COLUMN_UNITS:
        height, columns = units[name]
        if name != "embed":
            table["w_" + name] = ((8 * height, columns), BF16)
        table["g_" + name] = ((PARTS, SIDES, height, columns), BF16)
        table["m_" + name] = ((PARTS, height, columns), BF16)
        table["c_" + name] = ((PARTS, height, columns), BF16)
        if name in TRADED:
            del table["g_" + name]
            table["l_" + name] = ((PARTS, shown, 128), BF16)
            table["r_" + name] = ((shown, columns), BF16)
        if name in GATHERED:
            del table["g_" + name]
            del table["c_" + name]
            table["l_" + name] = ((8, shown, 128), BF16)
    table["w_embed"] = ((width, dec_width), BF16)
    for name in ROW_UNITS:
        height, columns = units[name]
        table["w_" + name] = ((2 * height, columns), BF16)
        if name == "e_out":
            narrow = columns // PARTS
            table["m_e_out"] = ((PARTS, height, narrow), BF16)
            table["c_e_out"] = ((PARTS, height, narrow), BF16)
            table["l_e_out"] = ((PARTS, shown, 128), BF16)
            table["r_e_out"] = ((shown, narrow), BF16)
            table["mixture_all"] = ((shown, width), BF16)
            continue
        table["g_" + name] = ((SIDES, height, columns), BF16)
        table["m_" + name] = ((height, columns), BF16)
        table["c_" + name] = ((2, height, columns), BF16)
    table["w_vector"] = ((8 * VECTORS, 128), BF16)
    table["g_vector"] = ((PARTS, SIDES, VECTORS, 128), F32)
    table["m_vector"] = ((PARTS, VECTORS, 128), F32)
    table["c_vector"] = ((PARTS, VECTORS, 128), F32)
    table["gains"] = ((VECTORS, width), F32)
    table["group"] = ((rows, width), BF16)
    table["cotangents"] = ((rows, dec_width), BF16)
    for key, count, wide, deep, heads, size, chunks in (
        ("e_", shown, width, hidden // 4, 4, 64, 2),
        ("d_", rows, dec_width, dec_hidden // 4, 4, 32, 4),
    ):
        share = heads * size
        for name, shape, kind in (
            ("residual", (count, wide), F32), ("unit_a", (count, wide), F32),
            ("unit_b", (count, wide), F32), ("scale_a", (count, 1), F32),
            ("scale_b", (count, 1), F32), ("normed", (count, wide), BF16),
            ("lifted", (count, wide), BF16), ("qkv", (count, 3 * share), BF16),
            ("probs", (heads, count, count), F32), ("mixture", (count, share), BF16),
            ("hidden", (count, deep), BF16), ("slope", (count, deep), F32),
            ("grad_upper", (count, deep), BF16), ("grad", (count, wide), F32),
            ("grad_mixture", (count, share), BF16), ("grad_qkv", (count, 3 * share), BF16),
            ("key_sum", (count, share), F32), ("value_sum", (count, share), F32),
            ("branch", (count, wide), BF16), ("branch_b", (count, wide), BF16),
            ("part", (chunks, 2, count // chunks // 2, wide), F32),
            ("met", (chunks, count // chunks // 2, wide), F32),
            ("out", (chunks, count // chunks // 2, wide), BF16),
            ("came", (2, chunks, count // chunks // 2, wide), BF16),
            ("whole", (chunks, 2, count // chunks // 2, wide), F32),
            ("sums", (8, wide), F32),
        ):
            table[key + name] = (shape, kind)
    table["last_part"] = ((2, 2, rows // 4, dec_width), F32)
    table["last_met"] = ((2, rows // 4, dec_width), F32)
    table["last_out"] = ((rows // 4, dec_width), BF16)
    table["last_came"] = ((rows // 4, dec_width), BF16)
    for name, shape, kind in (
        ("rank_row", (1, rows), jnp.int32), ("rank_column", (rows, 1), jnp.int32),
        ("ids_row", (1, rows), jnp.int32), ("ids_column", (rows, 1), jnp.int32),
        ("packed_row", (1, shown), jnp.int32), ("packed_column", (shown, 1), jnp.int32),
        ("code", (shown, width), F32), ("dec_code", (rows, dec_width), F32),
        ("staged", (VECTORS, 128), F32),
    ):
        table[name] = (shape, kind)
    table["lowered"] = ((shown, width), BF16)
    table["w_picked"] = ((8 * shown, dec_width), BF16)
    table["right"] = ((shown, width), BF16)
    return table


VECTOR_NAMES = (
    "v_gain_a", "v_bias_a", "v_gain_b", "v_bias_b", "v_mask",
    "v_dec_gain_a", "v_dec_bias_a", "v_dec_gain_b", "v_dec_bias_b",
)
INPUTS = ("lengths", "gsd", "visible") + VECTOR_NAMES + (
    "patches", "cotangent", "query", "key", "value", "out", "up", "down", "embed",
    "dec_query", "dec_key", "dec_value", "dec_out", "dec_up", "dec_down",
)
RESULTS = ("decoded", "grad_patches", "grad_vector") + MESSAGES
SEMAPHORES = {
    "local": (24,),
    "z_sent": (12,), "z_got": (12, 4), "y_sent": (12,), "y_got": (12, 4),
    "cross_sent": (1,), "cross_got": (1, 4),
    "gy_sent": (11,), "gy_got": (11,), "gz_sent": (11, 3), "gz_got": (11, 4),
    "f_sent": (5, 2), "f_got": (5, 2), "m_sent": (3,), "m_got": (3,), "gb_sent": (11, 4), "gb_got": (11, 3),
    "p_sent": (3,), "p_got": (3,), "c_sent": (3,), "c_got": (3,),
    "e_sent": (3,), "e_got": (3,), "l_sent": (2,), "l_got": (2,),
    "e_t_sent": (2, 2, 3), "e_t_got": (2, 2, 3), "d_t_sent": (2, 4, 3), "d_t_got": (2, 4, 3),
}


def place_of(ref, positions):
    ids = jnp.zeros(positions.shape, jnp.int32)
    first = jnp.zeros(positions.shape, jnp.int32)
    ratio = jnp.zeros(positions.shape, F32) + ref["gsd"][0, 0]
    end = jnp.int32(0)
    count = ref["lengths"].shape[1]
    for at in range(count - 1):
        end = end + ref["lengths"][0, at]
        later = positions >= end
        ids = ids + later.astype(jnp.int32)
        first = jnp.where(later, end, first)
        ratio = jnp.where(later, ref["gsd"][0, at + 1], ratio)
    return ids, (positions - first).astype(F32) * ratio


def lay_out(ref, rows, shown, width, dec_width):
    ids_row, scaled_row = place_of(ref, lax.broadcasted_iota(jnp.int32, (1, rows), 1))
    ids_column, scaled_column = place_of(ref, lax.broadcasted_iota(jnp.int32, (rows, 1), 0))
    ref["ids_row"][...] = ids_row
    ref["ids_column"][...] = ids_column
    visible = ref["visible"][...] > 0
    marks = jnp.broadcast_to(visible.astype(F32), (16, rows)).astype(BF16)
    down = lax.broadcasted_iota(jnp.int32, (rows, rows), 0)
    along = lax.broadcasted_iota(jnp.int32, (rows, rows), 1)
    until = (along <= down).astype(BF16)
    before = (along < down).astype(BF16)
    count_row = dot_b(marks, until)[0:1]
    rank_row = jnp.where(visible, count_row.astype(jnp.int32) - 1, -1)
    count_column = dot_b(until, marks)[:, 0:1].astype(jnp.int32)
    others = dot_b(before, marks)[:, 0:1].astype(jnp.int32)
    rank_column = jnp.where(count_column > others, others, -1)
    ref["rank_row"][...] = rank_row
    ref["rank_column"][...] = rank_column
    here = lax.broadcasted_iota(jnp.int32, (shown, rows), 0) == rank_row
    packed = jnp.sum(jnp.where(here, ids_row.astype(F32), 0.0), axis=1, keepdims=True)
    ref["packed_column"][...] = packed.astype(jnp.int32)
    packed_scaled = jnp.sum(jnp.where(here, scaled_row, 0.0), axis=1, keepdims=True)
    there = lax.broadcasted_iota(jnp.int32, (rows, shown), 1) == rank_column
    packed = jnp.sum(jnp.where(there, ids_column.astype(F32), 0.0), axis=0, keepdims=True)
    ref["packed_row"][...] = packed.astype(jnp.int32)
    for target, scaled, wide in (
        (ref["code"], packed_scaled, width), (ref["dec_code"], scaled_column, dec_width)
    ):
        half = wide // 2
        steps = lax.broadcasted_iota(jnp.int32, (1, half), 1).astype(F32)
        frequency = jnp.exp(steps * (-math.log(10000.0) / half))
        target[:, 0:1] = scaled
        tall = 16 * 1024 // half

        def body(part):
            angles = target[part, 0:1] * frequency
            made = jnp.concatenate([jnp.sin(angles), jnp.cos(angles)], axis=1)
            target[part] = made
        each(target.shape[0], tall, body)


def main_kernel(names, *refs):
    ref = dict(zip(names, refs))
    s = Split()
    shown, width = ref["code"].shape
    rows, dec_width = ref["dec_code"].shape
    own = ref["patches"].shape[0]
    sem = {name: ref["s_" + name] for name in SEMAPHORES}
    counter = [0]

    def local(source, target):
        at = counter[0]
        counter[0] = at + 1
        return pltpu.make_async_copy(source, target, sem["local"].at[at])

    barrier = pltpu.get_barrier_semaphore()
    peers = [(lax.rem(s.dp + step, 8), s.blk) for step in range(1, 8)] + list(s.blk_peers)
    for peer in peers:
        pl.semaphore_signal(barrier, inc=1, device_id=peer, device_id_type=pl.DeviceIdType.MESH)

    order = ("vector", "e_qkv", "e_out", "e_up", "embed", "e_down", "e_down_b", "d_qkv", "d_out",
             "d_up", "d_down")
    units = {}
    for at, name in enumerate(order):
        sems = tuple(sem[kind].at[at] for kind in ("z_sent", "z_got", "y_sent", "y_got"))
        sems = sems + (sem["cross_sent"].at[0], sem["cross_got"].at[0])
        whole = ref["w_e_down" if name == "e_down_b" else "w_" + name]
        if name == "vector":
            units[name] = Columns(s, whole, VECTORS, [], sems)
        elif name in ROW_UNITS:
            source = ref[{"e_out": "out", "d_out": "dec_out", "d_down": "dec_down"}[name]]
            height = source.shape[0]
            copy = local(source, whole.at[span(s.y * height, height)])
            units[name] = Rows(s, whole, height, copy, sems)
        else:
            height = ref["m_e_down" if name == "e_down_b" else "m_" + name].shape[1]
            mine = span(s.dp * height, height)
            columns = None
            if name in ("e_qkv", "d_qkv"):
                kinds = ("query", "key", "value")
                if name == "d_qkv":
                    kinds = ("dec_query", "dec_key", "dec_value")
                size = ref[kinds[0]].shape[1] // PARTS
                copies = [
                    local(ref[kind].at[:, span(s.part * size, size)],
                          whole.at[mine, pl.ds(place * size, size)])
                    for place, kind in enumerate(kinds)
                ]
            elif name == "e_up":
                size = height
                copies = [
                    local(ref["up"].at[:, span((owner * PARTS + s.blk) * size, size)],
                          whole.at[mine, pl.ds(owner * size, size)])
                    for owner in range(8)
                ]
            elif name in ("e_down", "e_down_b"):
                size = width // 2
                columns = pl.ds(size if name == "e_down_b" else 0, size)
                copies = [local(ref["down"].at[span(s.blk * height, height), columns],
                                whole.at[mine, columns])]
            elif name == "embed":
                size = dec_width // PARTS
                columns = span(s.part * size, size)
                copies = [local(ref["embed"].at[:, columns], whole.at[mine, columns])]
            else:
                size = ref["dec_up"].shape[1] // PARTS
                copies = [local(ref["dec_up"].at[:, span(s.part * size, size)], whole.at[mine])]
            kind = EarlyColumns if name in EARLY else Columns
            units[name] = kind(s, whole, height, copies, sems, columns)

    sums = {}
    for at, name in enumerate(order):
        if name == "e_down_b":
            continue
        sems = tuple(
            sem[kind].at[at]
            for kind in ("gy_sent", "gy_got", "gz_sent", "gz_got", "gb_sent", "gb_got")
        )
        kind = ColumnSum
        for names, other in ((ROW_SUMS, RowSum), (TRADED, ProductSum), (GATHERED, GatheredSum)):
            if name in names:
                kind = other
        done = None if name == "vector" else ref["o_" + name]
        wide = ref["m_" + name].shape[-1]
        sums[name] = kind(s, ref.get("g_" + name), ref["m_" + name], ref.get("c_" + name), done, sems,
                          16 if wide > 512 else 32 if name != "vector" else 8)
    all_picked = ref["w_picked"]
    embed_columns = span(s.part * (dec_width // PARTS), dec_width // PARTS)
    out_columns = span(s.part * (width // PARTS), width // PARTS)
    for at, (name, left, right, their_right) in enumerate((
        ("e_qkv", "e_normed", ref["e_grad_qkv"], ref["r_e_qkv"]),
        ("e_up", "e_lifted", ref["e_grad_upper"], ref["r_e_up"]),
        ("e_out", "mixture_all", ref["e_branch_b"].at[:, out_columns], ref["r_e_out"]),
    )):
        sums[name].trade(ref[left], right, ref["l_" + name], their_right,
                         (sem["f_sent"].at[at], sem["f_got"].at[at]))

    def of_group(group):
        return pl.ds(pl.multiple_of(group * shown, shown), shown)

    def embed_right(group):
        return all_picked[of_group(group), embed_columns]

    def down_right(group):
        def body(part):
            made = dot_b(all_picked[of_group(group)], ref["w_embed"][part])
            ref["right"][:, part] = made.astype(BF16)
        each(width, 256, body)
        return ref["right"][...]

    for at, (name, left, right) in enumerate((
        ("e_down", "e_hidden", down_right), ("embed", "lowered", embed_right),
    )):
        sums[name].gather(ref[left], ref["l_" + name],
                          (sem["f_sent"].at[3 + at, 0], sem["f_got"].at[3 + at, 0]), right)
    sems = tuple(sem[kind].at[11] for kind in ("z_sent", "z_got", "y_sent", "y_got"))
    picked_unit = Columns(s, all_picked, shown, [], sems + (None, None))

    totals = []
    for at in range(7):
        key, slot = ("e_", at % 2) if at in (0, 1, 5, 6) else ("d_", at % 2)
        totals.append(Total(
            s, *(ref[key + name] for name in ("part", "met", "out", "came", "whole")),
            (sem[key + "t_sent"].at[slot], sem[key + "t_got"].at[slot]), slot,
        ))

    encoder = Block(shown, width, 4, 64, "e_", ref, 0)
    decoder = Block(rows, dec_width, 4, 32, "d_", ref, 5)
    for block, key in ((encoder, "e_"), (decoder, "d_")):
        for short, long in (("w_qkv", "qkv"), ("w_out", "out"), ("w_up", "up"),
                            ("w_down", "down")):
            ref[key + short] = ref["w_" + key + long]

    for name in order:
        units[name].fetch()
    mine = span(s.blk * own, own)
    own_patches = local(ref["patches"], ref["group"].at[mine])
    own_cotangents = local(ref["cotangent"], ref["cotangents"].at[mine])
    own_patches.start()
    own_cotangents.start()
    staged = ref["staged"]
    staged[...] = jnp.zeros(staged.shape, F32)
    for at, name in enumerate(VECTOR_NAMES):
        row = ref[name][...].astype(F32)[None, :]
        staged[at:at + 1, 0:row.shape[1]] = row
    ref["w_vector"][span(s.dp * VECTORS, VECTORS)] = staged[...].astype(BF16)

    pl.semaphore_wait(barrier, len(peers))

    def place_in(name):
        return lambda blk: ref[name].at[span(blk * own, own)]

    def embed_block(blk):
        size = dec_width // PARTS
        return ref["w_embed"].at[:, span(lax.rem(3 * blk, PARTS) * size, size)]

    def mixture_block(blk):
        size = width // PARTS
        return ref["mixture_all"].at[:, span(lax.rem(3 * blk, PARTS) * size, size)]

    shared = {
        "p": Shared(s, ref["patches"], place_in("group"), (sem["p_sent"], sem["p_got"])),
        "c": Shared(s, ref["cotangent"], place_in("cotangents"), (sem["c_sent"], sem["c_got"])),
        "e": Shared(s, embed_block(s.blk), embed_block, (sem["e_sent"], sem["e_got"])),
        "m": Shared(s, ref["e_mixture"], mixture_block, (sem["m_sent"], sem["m_got"])),
    }
    for name in ("vector", "e_qkv", "e_out"):
        units[name].send()
    shared["p"].start()
    units["e_up"].send()

    lay_out(ref, rows, shown, width, dec_width)
    units["vector"].forward()
    units["e_qkv"].forward()
    shared["p"].pass_on()
    own_patches.wait()
    units["e_out"].forward()
    shared["p"].finish()

    places = (
        lax.broadcasted_iota(jnp.int32, (shown, rows), 0) == ref["rank_row"][...]
    ).astype(BF16)
    residual = ref["e_residual"]

    def place_patches(columns):
        residual[:, columns] = dot(places, ref["group"][:, columns]) + ref["code"][:, columns]
    each(width, 256, place_patches)

    units["e_up"].forward((1,))
    units["vector"].finish()
    vectors = ref["w_vector"][...].astype(F32)
    gains = ref["gains"]
    for at in range(9):
        for owner in range(8):
            row = vectors[VECTORS * owner + at:VECTORS * owner + at + 1, :]
            if at < 4:
                gains[at:at + 1, 128 * owner:128 * owner + 128] = row
            elif owner % 2 == 0:
                pair = VECTORS * (owner + 1) + at
                other = pltpu.roll(vectors[pair:pair + 1, :], 64, 1)
                gains[at:at + 1, 64 * owner:64 * owner + 128] = row + other
    encoder.norm(True)
    units["e_up"].forward((2,))
    units["embed"].send()
    units["e_down"].send()
    units["e_qkv"].finish()
    encoder.project()
    units["e_up"].forward((3,))
    encoder.attend(ref["packed_column"], ref["packed_row"])
    ref["mixture_all"][:, out_columns] = ref["e_mixture"][...]
    units["e_out"].finish()
    totals[0].begin(encoder.product(ref["e_mixture"], ref["w_e_out"]))
    units["embed"].forward()

    def after_attention(at):
        encoder.add_total(at)
        encoder.norm(False, at * encoder.chunk, encoder.chunk)
    totals[0].finish(after_attention)
    shared["c"].start()
    shared["m"].start()
    units["e_down"].forward()
    units["e_down_b"].send()
    units["e_up"].finish()
    encoder.expand()
    units["d_qkv"].send()
    units["d_out"].send()
    units["embed"].finish()
    shared["e"].start()
    shared["c"].pass_on()
    shared["m"].pass_on()
    units["e_down_b"].forward()
    units["d_up"].send()
    units["d_down"].send()
    units["d_qkv"].forward()
    shared["e"].pass_on()
    units["e_down"].finish()
    units["e_down_b"].finish()
    totals[1].begin(encoder.product(ref["e_hidden"], ref["w_e_down"]))
    units["d_out"].forward()
    units["d_up"].forward()
    shared["e"].finish()
    lowered = ref["lowered"]

    def after_hidden(at):
        encoder.add_total(at)
        part = pl.ds(pl.multiple_of(at * encoder.chunk, encoder.chunk), encoder.chunk)
        lowered[part] = residual[part].astype(BF16)
    totals[1].finish(after_hidden)

    embedded = dot(lowered[...], ref["w_embed"][...])
    high = embedded.astype(BF16)
    low = (embedded - high.astype(F32)).astype(BF16)
    token = gains[4:5, 0:dec_width]
    start = ref["d_residual"]

    def place_rows(part):
        rank = ref["rank_column"][part]
        here = (lax.broadcasted_iota(jnp.int32, (128, shown), 1) == rank).astype(BF16)
        made = jnp.where(rank >= 0, dot(here, high) + dot(here, low), token)
        start[part] = made + ref["dec_code"][part]
    each(rows, 128, place_rows)
    decoder.norm(True)
    units["d_down"].forward()
    units["d_qkv"].finish()
    decoder.project()
    decoder.attend(ref["ids_column"], ref["ids_row"])
    units["d_out"].finish()
    totals[2].begin(decoder.product(ref["d_mixture"], ref["w_d_out"]))
    units["d_up"].finish()
    units["d_down"].finish()
    last_part, last_met = ref["last_part"], ref["last_met"]
    quarter = rows // 4

    def decoder_rest(at):
        decoder.add_total(at)
        decoder.norm(False, at * decoder.chunk, decoder.chunk)
        decoder.expand(at * decoder.chunk, decoder.chunk)
        part = pl.ds(pl.multiple_of(at * quarter, quarter), quarter)
        made = dot(ref["d_hidden"][part], ref["w_d_down"][...])
        last_part[lax.div(at, 2), lax.rem(at, 2)] = made
    totals[2].finish(decoder_rest)
    last_sent, last_got = sem["l_sent"], sem["l_got"]
    last_first = remote(last_part.at[:, 1 - s.core], last_met, last_sent.at[0], last_got.at[0],
                        s.core_peer)
    last_second = remote(ref["last_out"], ref["last_came"], last_sent.at[1], last_got.at[1],
                         s.x_peer)
    last_first.start()

    own_cotangents.wait()
    shared["c"].finish()
    shared["m"].finish()
    for name in ("e_down", "embed", "e_up", "e_out", "e_qkv"):
        sums[name].start_left()
    cotangents, grad = ref["cotangents"], ref["d_grad"]
    multiply = decoder.product(ref["d_grad_upper"], ref["w_d_up"], back=True)

    def decoder_hidden(at):
        decoder.back_hidden(cotangents, at * decoder.chunk, decoder.chunk)
        multiply(at)
    totals[3].begin(decoder_hidden)
    last_first.wait_recv()

    def last_add(part):
        made = last_part[1 - s.x, s.core, part] + last_met[1 - s.x, part]
        ref["last_out"][part] = made.astype(BF16)
    each(quarter, 64, last_add)
    last_second.start()

    def copy_grad(part):
        grad[part] = cotangents[part].astype(F32)
    each(rows, 64, copy_grad)
    vector_grad = ref["g_vector"]
    vector_grad[...] = jnp.zeros(vector_grad.shape, F32)
    decoder.clear_sums()
    weight_grad(ref["d_hidden"], cotangents, ref["g_d_down"])
    sums["d_down"].start()
    weight_grad(ref["d_lifted"], ref["d_grad_upper"], ref["g_d_up"])
    sums["d_up"].start()

    def decoder_middle(at):
        decoder.norm_back(at, False, ref["d_branch"])
        decoder.back_mixture(ref["d_branch"], at * decoder.chunk, decoder.chunk)
    totals[3].finish(decoder_middle)
    vector_store(vector_grad, 7, ref["d_sums"][0:1], False)
    vector_store(vector_grad, 8, ref["d_sums"][1:2], False)
    decoder.attend_back()
    sums["d_down"].middle()
    totals[4].begin(decoder.product(ref["d_grad_qkv"], ref["w_d_qkv"], back=True))
    sums["d_up"].middle()

    def last_close(part):
        made = last_part[s.x, s.core, part] + last_met[s.x, part]
        before = ref["d_residual"][pl.ds(pl.multiple_of(s.blk * own + part.start, 64), 64)]
        whole = made + ref["last_came"][part].astype(F32) + before
        ref["decoded"][part] = whole.astype(BF16)
    decoder.clear_sums()
    weight_grad(ref["d_normed"], ref["d_grad_qkv"], ref["g_d_qkv"])
    sums["d_qkv"].start()
    weight_grad(ref["d_mixture"], ref["d_branch"], ref["g_d_out"])
    sums["d_out"].start()

    def decoder_first(at):
        decoder.norm_back(at, True, ref["d_branch_b"])
    totals[4].finish(decoder_first)
    picked = all_picked.at[of_group(s.dp)]
    picked[...] = dot(places, ref["d_branch_b"][...]).astype(BF16)
    picked_unit.send()
    encoder_grad = ref["e_grad"]

    def back_embed(part):
        made = dot_b(picked[...], ref["w_embed"][part])
        encoder_grad[:, part] = made
        ref["e_branch"][:, part] = made.astype(BF16)
    each(width, 256, back_embed)
    sums["d_down"].join()

    encoder.back_hidden(ref["e_branch"])
    sums["e_up"].start()
    totals[5].begin(encoder.product(ref["e_grad_upper"], ref["w_e_up"], back=True))
    picked_unit.forward((1, 2))
    encoder.clear_sums()
    sums["e_up"].middle()

    def encoder_middle(at):
        encoder.norm_back(at, False, ref["e_branch_b"])
        encoder.back_mixture(ref["e_branch_b"], at * encoder.chunk, encoder.chunk)
    totals[5].finish(encoder_middle)
    sums["e_out"].start()
    picked_unit.forward((3,))
    sums["d_up"].join()
    encoder.attend_back()
    sums["e_qkv"].start()
    totals[6].begin(encoder.product(ref["e_grad_qkv"], ref["w_e_qkv"], back=True))
    sums["d_down"].last()
    sums["d_up"].last()
    sums["e_out"].middle()
    sums["d_qkv"].middle()
    sums["d_out"].middle()
    vector_store(vector_grad, 2, ref["e_sums"][0:1], True)
    vector_store(vector_grad, 3, ref["e_sums"][1:2], True)
    encoder.clear_sums()
    sums["e_qkv"].middle()

    def encoder_first(at):
        encoder.norm_back(at, True, None)
    totals[6].finish(encoder_first)
    sums["e_up"].join()
    picked_unit.finish()
    sums["embed"].last()
    sums["e_down"].last()
    sums["d_down"].pass_on()
    sums["d_up"].pass_on()
    sums["d_qkv"].join()
    sums["d_out"].join()
    vector_store(vector_grad, 0, ref["e_sums"][0:1], True)
    vector_store(vector_grad, 1, ref["e_sums"][1:2], True)
    vector_store(vector_grad, 5, ref["d_sums"][0:1], False)
    vector_store(vector_grad, 6, ref["d_sums"][1:2], False)

    def mask_sum(at, total):
        part = pl.ds(pl.multiple_of(at * 64, 64), 64)
        hidden_row = ref["rank_column"][part] < 0
        return total + jnp.sum(jnp.where(hidden_row, grad[part], 0.0), axis=0, keepdims=True)
    token_grad = lax.fori_loop(0, rows // 64, mask_sum, jnp.zeros((1, dec_width), F32))
    vector_store(vector_grad, 4, token_grad, False)
    sums["vector"].start()
    rank = ref["rank_column"][mine]
    here = (lax.broadcasted_iota(jnp.int32, (own, shown), 1) == rank).astype(BF16)

    def place_grad(part):
        values = encoder_grad[:, part]
        top = values.astype(BF16)
        rest = (values - top.astype(F32)).astype(BF16)
        ref["grad_patches"][:, part] = dot(here, top) + dot(here, rest)
    each(width, 256, place_grad)
    last_second.wait_recv()
    each(quarter, 64, last_close)
    sums["e_out"].join()
    sums["d_qkv"].last()
    sums["d_out"].last()
    sums["vector"].middle()
    sums["e_qkv"].join()
    sums["vector"].join()
    sums["e_down"].pass_on()
    sums["e_up"].last()
    sums["e_out"].last()
    sums["d_qkv"].pass_on()
    sums["d_out"].pass_on()
    sums["e_up"].pass_on()
    sums["e_qkv"].last()
    sums["e_out"].pass_on()
    sums["embed"].pass_on()

    def vector_out(part, whole):
        ref["grad_vector"][part] = whole
    sums["vector"].total(vector_out)
    sums["vector"].drain()
    sums["e_qkv"].pass_on()
    for name in MESSAGES:
        sums[name].close()
    last_first.wait_send()
    last_second.wait_send()
    for name in order:
        units[name].drain()
    picked_unit.drain()
    for gathered in shared.values():
        gathered.drain()


def unpack_kernel(names, *refs):
    ref = dict(zip(names, refs))
    side = lax.rem(lax.axis_index("dp"), 2)
    ref["decoded"][...] = ref["i_decoded"][...]
    ref["grad_patches"][...] = ref["i_grad_patches"][...]
    vectors = ref["i_grad_vector"][...]
    for at, name in enumerate(("e_gain_a", "e_bias_a", "e_gain_b", "e_bias_b")):
        ref[name][...] = vectors[at:at + 1, :]
    for at, name in enumerate(("mask", "d_gain_a", "d_bias_a", "d_gain_b", "d_bias_b")):
        row = vectors[at + 4:at + 5, :]
        ref[name][...] = jnp.where(side == 0, row[:, 0:64], row[:, 64:128])
    for blk in range(PARTS):
        part = 3 * blk % PARTS
        for key in ("e_", "d_"):
            size = ref[key + "query"].shape[1] // PARTS
            for place, kind in enumerate(("query", "key", "value")):
                ref[key + kind][:, part * size:(part + 1) * size] = ref["i_" + key + "qkv"][
                    blk, :, place * size:(place + 1) * size].astype(F32)
        size = ref["i_e_up"].shape[1]
        for owner in range(8):
            column = (owner * PARTS + blk) * size
            ref["e_up"][:, column:column + size] = ref["i_e_up"][
                blk, :, owner * size:(owner + 1) * size].astype(F32)
        size = ref["i_e_down"].shape[1]
        ref["e_down"][blk * size:(blk + 1) * size, :] = ref["i_e_down"][blk].astype(F32)
        for name in ("embed", "d_up", "e_out"):
            size = ref["i_" + name].shape[2]
            ref[name][:, part * size:(part + 1) * size] = ref["i_" + name][blk].astype(F32)
    for name in ROW_SUMS:
        ref[name][...] = ref["i_" + name][...].astype(F32)


def local_kernel(*arguments):
    (patches, lengths, gsd_scale, visible,
     e_gain_a, e_bias_a, e_query, e_key, e_value, e_out, e_gain_b, e_bias_b, e_up, e_down,
     embed, mask,
     d_gain_a, d_bias_a, d_query, d_key, d_value, d_out, d_gain_b, d_bias_b, d_up, d_down,
     cotangent) = arguments
    width, dec_width = patches.shape[1], cotangent.shape[1]
    hidden, dec_hidden = e_up.shape[1], d_up.shape[1]
    rows = visible.shape[1]
    inputs = {
        "lengths": lengths, "gsd": gsd_scale, "visible": visible,
        "patches": patches, "cotangent": cotangent,
        "query": e_query, "key": e_key, "value": e_value, "out": e_out, "up": e_up,
        "down": e_down, "embed": embed, "dec_query": d_query, "dec_key": d_key,
        "dec_value": d_value, "dec_out": d_out, "dec_up": d_up, "dec_down": d_down,
    }
    inputs.update(zip(VECTOR_NAMES, (
        e_gain_a, e_bias_a, e_gain_b, e_bias_b, mask, d_gain_a, d_bias_a, d_gain_b, d_bias_b)))
    units = unit_shapes(width, dec_width, hidden, dec_hidden)
    shapes = {
        "decoded": (cotangent.shape, BF16), "grad_patches": (patches.shape, F32),
        "grad_vector": ((VECTORS, 128), F32),
    }
    for name in COLUMN_UNITS:
        shapes[name] = ((PARTS,) + units[name], BF16)
    for name in ROW_SUMS:
        shapes[name] = (units[name], BF16)
    shapes["e_out"] = ((PARTS, width // 8, width // PARTS), BF16)
    table = scratch_table(width, dec_width, hidden, dec_hidden, rows, SHOWN)
    names = INPUTS + tuple("o_" + name if name in MESSAGES else name for name in RESULTS)
    names = names + tuple(table) + tuple("s_" + name for name in SEMAPHORES)
    spaces = {"lengths": pltpu.SMEM, "gsd": pltpu.SMEM, "visible": pltpu.VMEM}
    spaces.update({name: pltpu.VMEM for name in VECTOR_NAMES})
    results = pl.pallas_call(
        functools.partial(main_kernel, names),
        out_shape=[jax.ShapeDtypeStruct(*shapes[name]) for name in RESULTS],
        in_specs=[pl.BlockSpec(memory_space=spaces.get(name, pl.ANY)) for name in INPUTS],
        out_specs=[
            pl.BlockSpec(memory_space=pl.ANY if name in MESSAGES else pltpu.VMEM)
            for name in RESULTS
        ],
        scratch_shapes=[pltpu.VMEM(*entry) for entry in table.values()]
        + [pltpu.SemaphoreType.DMA(shape) for shape in SEMAPHORES.values()],
        compiler_params=pltpu.CompilerParams(
            collective_id=0, has_side_effects=True, vmem_limit_bytes=62 * MIB
        ),
    )(*(inputs[name] for name in INPUTS))
    made = {"i_" + name: result for name, result in zip(RESULTS, results)}
    finals = {
        "decoded": (cotangent.shape, BF16), "grad_patches": (patches.shape, F32),
    }
    for key, wide, deep in (("e_", width, hidden), ("d_", dec_width, dec_hidden)):
        small, tall = wide // 8, deep // 8
        if key == "d_":
            finals["embed"] = ((width // 8, dec_width), F32)
            finals["mask"] = ((1, small), F32)
        for name, shape in (
            ("gain_a", (1, small)), ("bias_a", (1, small)), ("query", (small, wide)),
            ("key", (small, wide)), ("value", (small, wide)), ("out", (small, wide)),
            ("gain_b", (1, small)), ("bias_b", (1, small)), ("up", (small, deep)),
            ("down", (tall, wide)),
        ):
            finals[key + name] = (shape, F32)
    outputs = pl.pallas_call(
        functools.partial(unpack_kernel, tuple(made) + tuple(finals)),
        out_shape=[jax.ShapeDtypeStruct(*entry) for entry in finals.values()],
        in_specs=[pl.BlockSpec(memory_space=pltpu.VMEM)] * len(made),
        out_specs=[pl.BlockSpec(memory_space=pltpu.VMEM)] * len(finals),
        compiler_params=pltpu.CompilerParams(vmem_limit_bytes=62 * MIB),
    )(*made.values())
    return tuple(
        output.reshape(-1) if output.shape[0] == 1 else output for output in outputs
    )


def solution(mesh):
    both, vec, mat = P(("dp", "blk"), None), P("dp"), P("dp", None)
    block = (vec, vec, mat, mat, mat, mat, vec, vec, mat, mat)
    in_specs = (both, mat, mat, mat) + block + (mat, vec) + block + (both,)
    out_specs = (both, both) + block + (mat, vec) + block
    body = local_kernel if mesh.shape["dp"] == 8 and mesh.shape["blk"] == 4 else local
    return jax.shard_map(body, mesh=mesh, in_specs=in_specs, out_specs=out_specs, check_vma=False)
```

```python
import functools
import math

import jax
import jax.numpy as jnp
from jax import lax
from jax.experimental import pallas as pl
from jax.experimental.pallas import tpu as pltpu
from jax.sharding import PartitionSpec as P

HEADS = 16
EPSILON = 1e-06
MASKED_SCORE = -1e30
F32 = jnp.float32
BF16 = jnp.bfloat16


def dot(left, right):
    return lax.dot_general(left, right, (((1,), (0,)), ((), ())), preferred_element_type=F32)


def dot_t(left, right):
    return lax.dot_general(left, right, (((0,), (0,)), ((), ())), preferred_element_type=F32)


def dot_b(left, right):
    return lax.dot_general(left, right, (((1,), (1,)), ((), ())), preferred_element_type=F32)


def sincos(scaled, width):
    half_width = width // 2
    frequency = jnp.exp(
        jnp.arange(half_width, dtype=F32) * (-math.log(10000.0) / half_width)
    )
    angles = scaled[:, None] * frequency[None, :]
    return jnp.concatenate([jnp.sin(angles), jnp.cos(angles)], axis=1)


def norm_parts(values):
    center = values - jnp.mean(values, axis=-1, keepdims=True)
    spread = jnp.mean(center * center, axis=-1, keepdims=True)
    scale = lax.rsqrt(spread + EPSILON)
    return center * scale, scale


def norm_back(grad, unit, scale, gain):
    grad_gain = jnp.sum(grad * unit, axis=0, keepdims=True)
    grad_bias = jnp.sum(grad, axis=0, keepdims=True)
    inner = grad * gain
    mean_inner = jnp.mean(inner, axis=-1, keepdims=True)
    mean_cross = jnp.mean(inner * unit, axis=-1, keepdims=True)
    return scale * (inner - mean_inner - unit * mean_cross), grad_gain, grad_bias


def gelu_both(upper):
    phi = 0.5 * (1.0 + lax.erf(upper * math.sqrt(0.5)))
    density = jnp.exp(-0.5 * upper * upper) * (1.0 / math.sqrt(2.0 * math.pi))
    return upper * phi, phi + upper * density


def head_forward(queries, key_rows, values, allowed, scaling):
    scores = jnp.where(allowed, dot_b(queries, key_rows) * scaling, MASKED_SCORE)
    largest = jnp.max(scores, axis=-1, keepdims=True)
    exponent = jnp.exp(scores - largest)
    softmaxed = exponent / jnp.sum(exponent, axis=-1, keepdims=True)
    return softmaxed, dot(softmaxed.astype(BF16), values).astype(BF16)


def head_backward(queries, key_rows, values, softmaxed, grad_mixture, scaling):
    grad_values = dot_t(softmaxed.astype(BF16), grad_mixture).astype(BF16)
    grad_probs = dot_b(grad_mixture, values)
    delta = jnp.sum(softmaxed * grad_probs, axis=-1, keepdims=True)
    grad_scores = (softmaxed * (grad_probs - delta)).astype(BF16)
    grad_queries = (dot(grad_scores, key_rows) * scaling).astype(BF16)
    grad_keys = (dot_t(grad_scores, queries) * scaling).astype(BF16)
    return grad_queries, grad_keys, grad_values


def block_forward(residual, params, heads, allowed, total):
    gain_a, bias_a, w_query, w_key, w_value, w_out, gain_b, bias_b, w_up, w_down = params
    unit_a, scale_a = norm_parts(residual)
    normed = (unit_a * gain_a + bias_a).astype(BF16)
    queries = dot(normed, w_query).astype(BF16)
    key_rows = dot(normed, w_key).astype(BF16)
    values = dot(normed, w_value).astype(BF16)
    size = queries.shape[1] // heads
    scaling = 1.0 / math.sqrt(size)
    probs, mixed = [], []
    for head in range(heads):
        part = slice(head * size, (head + 1) * size)
        softmaxed, mixture = head_forward(
            queries[:, part], key_rows[:, part], values[:, part], allowed, scaling
        )
        probs.append(softmaxed)
        mixed.append(mixture)
    mixture = jnp.concatenate(mixed, axis=1)
    middle = residual + total(dot(mixture, w_out))
    unit_b, scale_b = norm_parts(middle)
    lifted = (unit_b * gain_b + bias_b).astype(BF16)
    hidden, slope = gelu_both(dot(lifted, w_up))
    hidden = hidden.astype(BF16)
    result = middle + total(dot(hidden, w_down))
    return result, (
        unit_a, scale_a, normed, queries, key_rows, values, probs, mixture,
        unit_b, scale_b, lifted, slope, hidden,
    )


def block_backward(grad_result, params, heads, saved, total):
    gain_a, bias_a, w_query, w_key, w_value, w_out, gain_b, bias_b, w_up, w_down = params
    (unit_a, scale_a, normed, queries, key_rows, values, probs, mixture,
     unit_b, scale_b, lifted, slope, hidden) = saved
    size = queries.shape[1] // heads
    scaling = 1.0 / math.sqrt(size)
    grad_branch = grad_result.astype(BF16)
    grad_down = dot_t(hidden, grad_branch)
    grad_upper = (dot_b(grad_branch, w_down) * slope).astype(BF16)
    grad_up = dot_t(lifted, grad_upper)
    grad_lifted = total(dot_b(grad_upper, w_up))
    grad_in, grad_gain_b, grad_bias_b = norm_back(grad_lifted, unit_b, scale_b, gain_b)
    grad_middle = grad_result + grad_in
    grad_attention = grad_middle.astype(BF16)
    grad_out = dot_t(mixture, grad_attention)
    grad_mixture = dot_b(grad_attention, w_out).astype(BF16)
    pieces = []
    for head in range(heads):
        part = slice(head * size, (head + 1) * size)
        pieces.append(
            head_backward(
                queries[:, part], key_rows[:, part], values[:, part], probs[head],
                grad_mixture[:, part], scaling,
            )
        )
    grad_queries, grad_keys, grad_values = (
        jnp.concatenate([piece[at] for piece in pieces], axis=1) for at in range(3)
    )
    grad_normed = total(
        dot_b(grad_queries, w_query) + dot_b(grad_keys, w_key) + dot_b(grad_values, w_value)
    )
    grad_in, grad_gain_a, grad_bias_a = norm_back(grad_normed, unit_a, scale_a, gain_a)
    return grad_middle + grad_in, (
        grad_gain_a, grad_bias_a, dot_t(normed, grad_queries), dot_t(normed, grad_keys),
        dot_t(normed, grad_values), grad_out, grad_gain_b, grad_bias_b, grad_up, grad_down,
    )


def layout(lengths_row, gsd_row, visible_row):
    count = visible_row.shape[0]
    positions = jnp.arange(count, dtype=jnp.int32)
    image_ends = jnp.cumsum(lengths_row)
    image_starts = image_ends - lengths_row
    image_ids = jnp.sum((positions[:, None] >= image_ends[None, :]).astype(jnp.int32), axis=1)
    onehot = image_ids[:, None] == jnp.arange(lengths_row.shape[0], dtype=jnp.int32)[None, :]
    first_row = jnp.sum(jnp.where(onehot, image_starts[None, :], 0), axis=1)
    ratio = jnp.sum(jnp.where(onehot, gsd_row[None, :], 0.0), axis=1)
    scaled = (positions - first_row).astype(F32) * ratio
    shown = visible_row > 0
    earlier = (positions[None, :] <= positions[:, None]) & shown[None, :]
    rank = jnp.where(shown, jnp.sum(earlier.astype(jnp.int32), axis=1) - 1, -1)
    return image_ids, scaled, rank


def spread_rows(grad, rank, offset, rows):
    own = lax.dynamic_slice_in_dim(rank, offset, rows)
    place = (own[:, None] == jnp.arange(grad.shape[0], dtype=jnp.int32)[None, :]).astype(BF16)
    high = grad.astype(BF16)
    low = (grad - high.astype(F32)).astype(BF16)
    return dot(place, high) + dot(place, low)


SHOWN = 128


def local(*arguments):
    patches, lengths, gsd_scale, visible = arguments[:4]
    encoder_shards = arguments[4:14]
    embed_shard, mask_shard = arguments[14:16]
    decoder_shards = arguments[16:26]
    cotangent = arguments[26]
    dp_count = lax.axis_size("dp")
    blk_count = lax.axis_size("blk")
    blk = lax.axis_index("blk")
    dp = lax.axis_index("dp")
    rows = patches.shape[0]
    offset = blk * rows
    heads = HEADS // blk_count
    image_ids, scaled, rank = layout(lengths[0], gsd_scale[0], visible[0])
    shown = rank >= 0
    places = rank[None, :] == jnp.arange(SHOWN, dtype=jnp.int32)[:, None]
    packed_ids = jnp.sum(jnp.where(places, image_ids[None, :], 0), axis=1)
    packed_scaled = jnp.sum(jnp.where(places, scaled[None, :], 0.0), axis=1)

    def gather(shard):
        return lax.all_gather(shard, "dp", axis=0, tiled=True)

    def by_columns(shard):
        width = shard.shape[1] // blk_count
        return gather(lax.dynamic_slice_in_dim(shard, blk * width, width, axis=1))

    def by_rows(shard):
        whole = gather(shard)
        height = whole.shape[0] // blk_count
        return lax.dynamic_slice_in_dim(whole, blk * height, height, axis=0)

    def vector(shard):
        return gather(shard).astype(F32)[None, :]

    def load(shards):
        kinds = (vector, vector, by_columns, by_columns, by_columns, by_rows,
                 vector, vector, by_columns, by_rows)
        return tuple(kind(shard) for kind, shard in zip(kinds, shards))

    def total(partial):
        return lax.psum(partial, "blk")

    def sum_columns(grad):
        summed = lax.psum_scatter(grad.astype(BF16), "dp", scatter_dimension=0, tiled=True)
        return lax.all_gather(summed, "blk", axis=1, tiled=True).astype(F32)

    def sum_rows(grad):
        whole = lax.all_gather(grad.astype(BF16), "blk", axis=0, tiled=True)
        return lax.psum_scatter(whole, "dp", scatter_dimension=0, tiled=True).astype(F32)

    def sum_vector(grad):
        return lax.psum_scatter(grad[0], "dp", scatter_dimension=0, tiled=True)

    def reduce(grads):
        kinds = (sum_vector, sum_vector, sum_columns, sum_columns, sum_columns, sum_rows,
                 sum_vector, sum_vector, sum_columns, sum_rows)
        return tuple(kind(grad) for kind, grad in zip(kinds, grads))

    group = lax.all_gather(patches, "blk", axis=0, tiled=True)
    picked = dot(places.astype(BF16), group)
    encoder = load(encoder_shards)
    residual = picked + sincos(packed_scaled, patches.shape[1])
    encoded, encoder_saved = block_forward(
        residual, encoder, heads, packed_ids[:, None] == packed_ids[None, :], total
    )
    embed = gather(embed_shard)
    lowered = encoded.astype(BF16)
    embedded = dot(lowered, embed)
    high = embedded.astype(BF16)
    low = (embedded - high.astype(F32)).astype(BF16)
    places_b = places.astype(BF16)
    start = jnp.where(
        shown[:, None], dot_t(places_b, high) + dot_t(places_b, low), vector(mask_shard)
    ) + sincos(scaled, embed.shape[1])
    decoder = load(decoder_shards)
    decoded, decoder_saved = block_forward(
        start, decoder, heads, image_ids[:, None] == image_ids[None, :], total
    )
    decoded_rows = lax.dynamic_slice_in_dim(decoded, offset, rows).astype(BF16)
    grad_out = lax.all_gather(cotangent, "blk", axis=0, tiled=True).astype(F32)
    grad_start, decoder_grads = block_backward(grad_out, decoder, heads, decoder_saved, total)
    grad_mask = jnp.sum(jnp.where(shown[:, None], 0.0, grad_start), axis=0, keepdims=True)
    grad_embedded = dot(places_b, grad_start.astype(BF16)).astype(BF16)
    width = embed.shape[1] // blk_count
    grad_embed = dot_t(
        lowered, lax.dynamic_slice_in_dim(grad_embedded, blk * width, width, axis=1)
    )
    grad_encoded = dot_b(grad_embedded, embed)
    grad_residual, encoder_grads = block_backward(
        grad_encoded, encoder, heads, encoder_saved, total
    )
    grad_patches = spread_rows(grad_residual, rank, offset, rows)
    return (
        (decoded_rows, grad_patches) + reduce(encoder_grads)
        + (sum_columns(grad_embed), sum_vector(grad_mask)) + reduce(decoder_grads)
    )


MIB = 2**20
DECODER_ROWS = 512
PARTS = 4
SIDES = 2
VECTORS = 16


class Split:
    def __init__(self):
        self.dp = lax.axis_index("dp")
        self.blk = lax.axis_index("blk")
        self.z = lax.div(self.dp, 2)
        self.y = lax.rem(self.dp, 2)
        self.x = lax.div(self.blk, 2)
        self.core = lax.rem(self.blk, 2)
        self.part = lax.rem(3 * self.blk, PARTS)
        self.y_peer = (self.z * 2 + 1 - self.y, self.blk)
        self.core_peer = (self.dp, self.x * 2 + 1 - self.core)
        self.x_peer = (self.dp, (1 - self.x) * 2 + self.core)
        self.far_peer = (self.dp, (1 - self.x) * 2 + 1 - self.core)
        self.blk_peers = (self.core_peer, self.x_peer, self.far_peer)

    def ahead(self, step):
        return lax.rem(self.z + step, PARTS)

    def behind(self, step):
        return lax.rem(self.z + PARTS - step, PARTS)

    def z_peer(self, step):
        return (self.ahead(step) * 2 + self.y, self.blk)

    def at_z(self, z):
        return (z * 2 + self.y, self.blk)

    def inward(self, step):
        high = lax.div(self.z, 2)
        return lax.rem(self.z + high * (PARTS - step) + (1 - high) * step, PARTS)

    @property
    def inner(self):
        return jnp.logical_or(self.z == 1, self.z == 2)

    @property
    def near_end(self):
        return jnp.where(self.inner, 3 * self.z - 3, lax.div(self.z, 3) + 1)

    @property
    def far_end(self):
        return 6 - 3 * self.z


def remote(source, target, sent, received, device):
    return pltpu.make_async_remote_copy(
        src_ref=source, dst_ref=target, send_sem=sent, recv_sem=received,
        device_id=device, device_id_type=pl.DeviceIdType.MESH,
    )


def span(at, size):
    return pl.ds(pl.multiple_of(at, size), size)


class Columns:
    def __init__(self, split, whole, rows, local, sems, columns=None):
        self.split, self.whole, self.rows, self.local = split, whole, rows, local
        self.columns = columns
        self.z_sent, self.z_got, self.y_sent, self.y_got = sems[:4]
        self.cross_sent, self.cross_got = sems[4:]

    def view(self, rows):
        if self.columns is None:
            return self.whole.at[rows]
        return self.whole.at[rows, self.columns]

    def block(self, z, y):
        return self.view(span((z * 2 + y) * self.rows, self.rows))

    def lane(self, crossed):
        s = self.split
        if crossed:
            return 1 - s.y, self.cross_sent, self.cross_got
        return s.y, self.z_sent, self.z_got

    def z_copy(self, step, crossed=False):
        s = self.split
        y, sent, got = self.lane(crossed)
        block = self.block(s.z, y)
        return remote(block, block, sent, got.at[s.z], s.at_z(s.inward(step)))

    def z_arrival(self, z, crossed=False):
        y, sent, got = self.lane(crossed)
        block = self.block(z, y)
        return remote(block, block, sent, got.at[z], self.split.y_peer)

    def relay(self, crossed=False):
        s = self.split
        y, sent, got = self.lane(crossed)
        block = self.block(s.far_end, y)
        return remote(block, block, sent, got.at[s.far_end], s.at_z(s.near_end))

    def y_copy(self, z, at):
        s = self.split
        block = self.block(z, s.y)
        return remote(block, block, self.y_sent, self.y_got.at[at], s.y_peer)

    def y_arrival(self, z, at):
        s = self.split
        block = self.block(z, 1 - s.y)
        return remote(block, block, self.y_sent, self.y_got.at[at], s.y_peer)

    def sent(self, sem, count):
        blocks = self.view(pl.ds(0, count * self.rows))
        remote(blocks, blocks, sem, self.y_got.at[0], self.split.y_peer).wait_send()

    def fetch(self):
        for copy in self.local:
            copy.start()

    def spread(self, crossed=False):
        self.z_copy(1, crossed).start()
        self.z_copy(2, crossed).start()

        @pl.when(self.split.inner)
        def _():
            self.z_copy(3, crossed).start()

    def collect(self, step, crossed=False):
        s = self.split
        z = s.inward(step)
        self.z_arrival(z, crossed).wait_recv()
        if step == 2:
            @pl.when(s.inner)
            def _():
                self.relay(crossed).start()
        return z

    def send(self, y_too=True):
        for copy in self.local:
            copy.wait()
        self.spread()
        if y_too:
            self.send_y()

    def send_y(self):
        self.y_copy(self.split.z, 0).start()

    def forward(self, steps=(1, 2, 3)):
        for step in steps:
            self.y_copy(self.collect(step), step).start()

    def finish(self):
        for step in range(PARTS):
            self.y_arrival(self.split.inward(step), step).wait_recv()

    def drain_z(self, sem):
        @pl.when(self.split.inner)
        def _():
            self.sent(sem, 4)

        @pl.when(jnp.logical_not(self.split.inner))
        def _():
            self.sent(sem, 2)

    def drain(self):
        self.drain_z(self.z_sent)
        self.sent(self.y_sent, PARTS)


class EarlyColumns(Columns):
    def cross(self):
        s = self.split
        self.y_arrival(s.z, 0).wait_recv()
        self.spread(True)

    def forward(self, steps=(1, 2, 3)):
        for step in steps:
            self.collect(step)

    def finish(self, steps=(1, 2, 3)):
        for step in steps:
            self.collect(step, True)

    def drain(self):
        self.drain_z(self.z_sent)
        self.drain_z(self.cross_sent)
        self.sent(self.y_sent, 1)


class Shared:
    def __init__(self, split, source, block, sems):
        self.split, self.source, self.block = split, source, block
        self.sents, self.gots = sems

    def copy(self, which):
        s = self.split
        if which == 2:
            block = self.block(s.x_peer[1])
            return remote(block, block, self.sents.at[2], self.gots.at[2], s.core_peer)
        return remote(self.source, self.block(s.blk), self.sents.at[which],
                      self.gots.at[which], s.blk_peers[which])

    def arrival(self, which):
        s = self.split
        block = self.block(s.blk_peers[which][1])
        return remote(block, block, self.sents.at[which], self.gots.at[which], s.core_peer)

    def start(self):
        self.copy(1).start()
        self.copy(0).start()

    def pass_on(self):
        self.arrival(1).wait_recv()
        self.copy(2).start()

    def finish(self):
        self.arrival(0).wait_recv()
        self.arrival(2).wait_recv()

    def drain(self):
        for which in range(3):
            self.copy(which).wait_send()


class Rows:
    def __init__(self, split, whole, rows, local, sems):
        self.split, self.whole, self.rows, self.local = split, whole, rows, local
        self.z_sent, self.z_got, self.y_sent, self.y_got = sems[:4]

    def block(self, y):
        return self.whole.at[span(y * self.rows, self.rows)]

    def z_copy(self, way):
        s = self.split
        return remote(self.block(s.y), self.block(s.y), self.z_got.at[1 + way],
                      self.z_got.at[0], s.at_z(s.z + 1 - 2 * way))

    def pass_on(self, act):
        s = self.split

        @pl.when(jnp.logical_and(s.z >= s.part, s.z < PARTS - 1))
        def _():
            act(self.z_copy(0))

        @pl.when(jnp.logical_and(s.z <= s.part, s.z > 0))
        def _():
            act(self.z_copy(1))

    def y_copy(self):
        s = self.split
        return remote(self.block(s.y), self.block(s.y), self.y_sent,
                      self.y_got.at[0], s.y_peer)

    def fetch(self):
        @pl.when(self.split.z == self.split.part)
        def _():
            self.local.start()

    def send(self):
        @pl.when(self.split.z == self.split.part)
        def _():
            self.local.wait()
            self.pass_on(lambda copy: copy.start())
            self.y_copy().start()

    def forward(self):
        s = self.split

        @pl.when(s.z != s.part)
        def _():
            remote(self.block(s.y), self.block(s.y), self.z_sent,
                   self.z_got.at[0], s.y_peer).wait_recv()
            self.pass_on(lambda copy: copy.start())
            self.y_copy().start()

    def finish(self):
        s = self.split
        block = self.block(1 - s.y)
        remote(block, block, self.y_sent, self.y_got.at[0], s.y_peer).wait_recv()

    def drain(self):
        self.pass_on(lambda copy: copy.wait_send())
        self.y_copy().wait_send()


def each(count, step, body, base=0):
    @pl.loop(0, count // step)
    def _(at):
        body(pl.ds(pl.multiple_of(base + at * step, step), step))


class ColumnSum:
    def __init__(self, split, grad, met, came, done, sems, step):
        self.split, self.grad, self.met, self.came, self.done = split, grad, met, came, done
        self.y_sent, self.y_got, self.z_sent, self.z_got, self.b_sent, self.b_got = sems
        self.step = step

    def y_copy(self):
        s = self.split
        return remote(self.grad.at[:, 1 - s.y], self.met, self.y_sent, self.y_got, s.y_peer)

    def z_copy(self, step):
        s = self.split
        target = s.inward(step)
        return remote(self.met.at[target], self.came.at[s.z], self.z_sent.at[step - 1],
                      self.z_got.at[s.z], s.at_z(target))

    def z_arrival(self, z):
        s = self.split
        return remote(self.met.at[z], self.came.at[z], self.z_sent.at[0], self.z_got.at[z],
                      s.y_peer)

    def relay(self):
        s = self.split
        return remote(self.met.at[3 - s.z], self.came.at[s.near_end], self.z_sent.at[2],
                      self.z_got.at[s.near_end], s.at_z(s.near_end))

    def b_copy(self, which):
        s = self.split
        if which == 2:
            block = self.done.at[s.x_peer[1]]
            return remote(block, block, self.b_sent.at[2], self.b_got.at[2], s.core_peer)
        return remote(self.met.at[s.z], self.done.at[s.blk], self.b_sent.at[which],
                      self.b_got.at[which], s.blk_peers[which])

    def b_arrival(self, which):
        s = self.split
        block = self.done.at[s.blk_peers[which][1]]
        return remote(block, block, self.b_sent.at[which], self.b_got.at[which],
                      s.blk_peers[which])

    def own_copy(self):
        s = self.split
        return pltpu.make_async_copy(self.met.at[s.z], self.done.at[s.blk], self.b_sent.at[3])

    def start(self):
        self.y_copy().start()

    def add(self, z):
        def body(rows):
            both = self.grad[z, self.split.y, rows].astype(F32) + self.met[z, rows].astype(F32)
            self.met[z, rows] = both.astype(self.met.dtype)
        each(self.met.shape[1], self.step, body)

    def arrive(self):
        self.y_copy().wait_recv()

    def middle(self):
        s = self.split
        self.arrive()

        @pl.when(s.inner)
        def _():
            self.add(s.inward(1))
            self.z_copy(1).start()
            self.add(s.inward(3))
            self.z_copy(3).start()
            self.add(s.inward(2))

        @pl.when(jnp.logical_not(s.inner))
        def _():
            self.add(3 - s.z)
            self.relay().start()
            self.add(s.inward(2))
            self.z_copy(2).start()
            self.add(s.inward(1))
            self.z_copy(1).start()
        self.add(s.z)

    def join(self):
        s = self.split

        @pl.when(s.inner)
        def _():
            target = s.inward(2)
            self.z_arrival(s.z).wait_recv()

            def body(rows):
                both = self.met[target, rows].astype(F32) + self.came[s.z, rows].astype(F32)
                self.met[target, rows] = both.astype(self.met.dtype)
            each(self.met.shape[1], self.step, body)
            self.z_copy(2).start()

    def total(self, store):
        s = self.split

        @pl.when(s.inner)
        def _():
            sources = (0, 3, 3 - s.z)
            for z in sources:
                self.z_arrival(z).wait_recv()

            def body(rows):
                whole = self.met[s.z, rows].astype(F32)
                for z in sources:
                    whole = whole + self.came[z, rows].astype(F32)
                store(rows, whole)
            each(self.met.shape[1], self.step, body)

        @pl.when(jnp.logical_not(s.inner))
        def _():
            for z in (1, 2):
                self.z_arrival(z).wait_recv()

            def body(rows):
                whole = self.met[s.z, rows].astype(F32)
                for z in (1, 2):
                    whole = whole + self.came[z, rows].astype(F32)
                store(rows, whole)
            each(self.met.shape[1], self.step, body)

    def last(self):
        s = self.split

        def store(rows, whole):
            self.met[s.z, rows] = whole.astype(self.met.dtype)
        self.total(store)
        self.b_copy(1).start()
        self.b_copy(0).start()
        self.own_copy().start()

    def pass_on(self):
        self.b_arrival(1).wait_recv()
        self.b_copy(2).start()

    def close(self):
        self.b_arrival(0).wait_recv()
        self.b_arrival(2).wait_recv()
        for which in range(3):
            self.b_copy(which).wait_send()
        self.own_copy().wait()
        self.drain()

    def drain_y(self):
        self.y_copy().wait_send()

    def drain(self):
        self.drain_y()
        for step in (1, 2, 3):
            self.z_copy(step).wait_send()


class ProductSum(ColumnSum):
    def trade(self, left, right, their_left, their_right, sems, told=None, heard=None, after=None):
        self.left, self.right = left, right
        self.their_left, self.their_right = their_left, their_right
        self.told = right if told is None else told
        self.heard = their_right if heard is None else heard
        self.tells = told is not False
        self.after = after
        self.t_sent, self.t_got = sems
        self.width = their_left.shape[2]

    def columns(self, z, y):
        return self.left.at[:, span((z * 2 + y) * self.width, self.width)]

    def left_copy(self, z):
        s = self.split
        return remote(self.columns(z, 1 - s.y), self.their_left.at[z], self.t_sent.at[0],
                      self.t_got.at[0], s.y_peer)

    def left_copies(self):
        return remote(self.their_left, self.their_left, self.t_sent.at[0], self.t_got.at[0],
                      self.split.y_peer)

    def right_copy(self):
        return remote(self.told, self.heard, self.t_sent.at[1], self.t_got.at[1],
                      self.split.y_peer)

    def start_left(self):
        for z in range(PARTS):
            self.left_copy(z).start()

    def start(self):
        self.right_copy().start()

    def add(self, z):
        both = dot_t(self.columns(z, self.split.y)[...], self.right[...]) + dot_t(
            self.their_left[z], self.their_right[...])
        self.met[z] = both.astype(self.met.dtype)

    def arrive(self):
        self.left_copies().wait_recv()
        if self.tells:
            self.right_copy().wait_recv()
        if self.after is not None:
            self.after()

    def drain_y(self):
        self.left_copies().wait_send()
        if self.tells:
            self.right_copy().wait_send()


class GatheredSum(ColumnSum):
    def gather(self, left, lefts, sems, right):
        self.left, self.lefts, self.right = left, lefts, right
        self.l_sent, self.l_got = sems
        self.count, self.width = lefts.shape[0], lefts.shape[2]

    def columns(self, owner):
        return self.left.at[:, span(owner * self.width, self.width)]

    def left_copy(self, step):
        s = self.split
        owner = lax.rem(s.dp + step, self.count)
        return remote(self.columns(owner), self.lefts.at[s.dp], self.l_sent, self.l_got,
                      (owner, s.blk))

    def left_copies(self):
        blocks = self.lefts.at[pl.ds(0, self.count - 1)]
        return remote(blocks, blocks, self.l_sent, self.l_got, self.split.y_peer)

    def start_left(self):
        for step in range(1, self.count):
            self.left_copy(step).start()
        self.lefts[self.split.dp] = self.columns(self.split.dp)[...]

    def last(self):
        s = self.split
        self.left_copies().wait_recv()
        zero = jnp.zeros(self.met.shape[1:], F32)

        def one(group, whole):
            return whole + dot_t(self.lefts[group], self.right(group))
        whole = lax.fori_loop(0, self.count, one, zero)
        self.met[s.z] = whole.astype(self.met.dtype)
        self.b_copy(1).start()
        self.b_copy(0).start()
        self.own_copy().start()

    def drain(self):
        self.left_copies().wait_send()


class RowSum:
    def __init__(self, split, grad, met, came, done, sems, step):
        self.split, self.grad, self.met, self.came, self.done = split, grad, met, came, done
        self.y_sent, self.y_got, self.z_sent, self.z_got, self.b_sent, self.b_got = sems
        self.step = step
        s = split
        self.home = lax.rem(3 * s.z, PARTS)
        self.at_home = s.z == s.part
        self.below = s.z < s.part
        self.above = s.z > s.part
        self.beside = s.x_peer[1] == self.home

    def y_copy(self):
        s = self.split
        return remote(self.grad.at[1 - s.y], self.met, self.y_sent, self.y_got, s.y_peer)

    def z_copy(self, way):
        s = self.split
        return remote(self.met, self.came.at[way], self.z_sent.at[way], self.z_got.at[way],
                      s.at_z(s.z + 1 - 2 * way))

    def z_arrival(self, way):
        return remote(self.met, self.came.at[way], self.z_sent.at[way], self.z_got.at[way],
                      self.split.y_peer)

    def b_copy(self, which):
        s = self.split
        source = self.done if which == 2 else self.met
        device = s.core_peer if which == 2 else s.blk_peers[which]
        return remote(source, self.done, self.b_sent.at[which], self.b_got.at[0], device)

    def own_copy(self):
        return pltpu.make_async_copy(self.met, self.done, self.b_sent.at[3])

    def start(self):
        self.y_copy().start()

    def send(self, act):
        @pl.when(self.below)
        def _():
            act(self.z_copy(0))

        @pl.when(self.above)
        def _():
            act(self.z_copy(1))

    def take(self, way):
        self.z_arrival(way).wait_recv()

        def body(rows):
            both = self.met[rows].astype(F32) + self.came[way, rows].astype(F32)
            self.met[rows] = both.astype(self.met.dtype)
        each(self.met.shape[0], self.step, body)

    def middle(self):
        s = self.split
        self.y_copy().wait_recv()

        def body(rows):
            both = self.grad[s.y, rows].astype(F32) + self.met[rows].astype(F32)
            self.met[rows] = both.astype(self.met.dtype)
        each(self.met.shape[0], self.step, body)

        @pl.when(jnp.logical_not(s.inner))
        def _():
            self.send(lambda copy: copy.start())

    def join(self):
        s = self.split

        @pl.when(s.inner)
        def _():
            @pl.when(self.below)
            def _():
                self.take(0)

            @pl.when(self.above)
            def _():
                self.take(1)
            self.send(lambda copy: copy.start())

    def last(self):
        s = self.split

        @pl.when(self.at_home)
        def _():
            @pl.when(s.z > 0)
            def _():
                self.take(0)

            @pl.when(s.z < PARTS - 1)
            def _():
                self.take(1)
            self.b_copy(1).start()
            self.b_copy(0).start()
            self.own_copy().start()

    def pass_on(self):
        @pl.when(self.beside)
        def _():
            self.b_copy(0).wait_recv()
            self.b_copy(2).start()

    def close(self):
        self.y_copy().wait_send()
        self.send(lambda copy: copy.wait_send())

        @pl.when(self.at_home)
        def _():
            self.b_copy(0).wait_send()
            self.b_copy(1).wait_send()
            self.own_copy().wait()

        @pl.when(self.beside)
        def _():
            self.b_copy(2).wait_send()

        @pl.when(jnp.logical_not(jnp.logical_or(self.at_home, self.beside)))
        def _():
            self.b_copy(0).wait_recv()


class Total:
    def __init__(self, split, part, met, out, came, whole, sems, slot):
        self.split, self.part, self.met, self.out = split, part, met, out
        self.came, self.whole = came.at[slot], whole
        self.sent, self.got = sems
        self.chunks = part.shape[0]
        self.high = part.shape[2]

    def first_copy(self, at):
        s = self.split
        return remote(self.part.at[at, 1 - s.core], self.met.at[at], self.sent.at[at, 0],
                      self.got.at[at, 0], s.core_peer)

    def second_copy(self, at):
        return remote(self.out.at[at], self.came.at[at], self.sent.at[at, 1],
                      self.got.at[at, 1], self.split.x_peer)

    def third_copy(self, at, half):
        s = self.split
        return remote(self.whole.at[at, half], self.whole.at[at, half], self.sent.at[at, 2],
                      self.got.at[at, 2], s.core_peer)

    def start(self, at):
        self.first_copy(at).start()

    def middle(self, at):
        s = self.split
        self.first_copy(at).wait_recv()

        def body(rows):
            both = self.part[at, s.core, rows] + self.met[at, rows]
            self.out[at, rows] = both.astype(BF16)
        each(self.high, 32, body)
        self.second_copy(at).start()

    def third(self, at):
        s = self.split
        self.second_copy(at).wait_recv()

        def body(rows):
            self.whole[at, s.core, rows] = self.out[at, rows].astype(
                F32) + self.came[at, rows].astype(F32)
        each(self.high, 32, body)
        self.third_copy(at, s.core).start()

    def fourth(self, at):
        s = self.split
        self.third_copy(at, 1 - s.core).wait_recv()
        self.first_copy(at).wait_send()
        self.second_copy(at).wait_send()
        self.third_copy(at, s.core).wait_send()

    def begin(self, produce):
        @pl.loop(0, self.chunks + 1)
        def _(at):
            @pl.when(at < self.chunks)
            def _():
                produce(at)
                self.start(at)

            @pl.when(at > 0)
            def _():
                self.middle(at - 1)

    def finish(self, consume):
        self.third(0)

        @pl.loop(0, self.chunks)
        def _(at):
            @pl.when(at + 1 < self.chunks)
            def _():
                self.third(at + 1)
            self.fourth(at)
            consume(at)


def head_mask(width, size, head):
    lanes = lax.broadcasted_iota(jnp.int32, (1, width), 1)
    return lax.div(lanes, size) == head


def keep(mask, values):
    return jnp.where(mask, values, jnp.zeros_like(values))


class Block:
    def __init__(self, rows, width, heads, size, names, refs, vectors):
        self.rows, self.width, self.heads, self.size = rows, width, heads, size
        self.share = heads * size
        self.scaling = 1.0 / math.sqrt(size)
        self.refs = refs
        self.vectors = vectors
        self.name = names
        self.tile = 32 * 1024 // width
        self.chunk = 2 * refs[names + "part"].shape[2]

    def ref(self, name):
        return self.refs[self.name + name]

    def row(self, at):
        return self.refs["gains"][self.vectors + at:self.vectors + at + 1, 0:self.width]

    def norm(self, first, base=0, count=None):
        unit, scale = self.ref("unit_a" if first else "unit_b"), self.ref(
            "scale_a" if first else "scale_b")
        out = self.ref("normed" if first else "lifted")
        gain, bias = self.row(0 if first else 2), self.row(1 if first else 3)
        residual = self.ref("residual")

        def body(rows):
            one, size = norm_parts(residual[rows])
            unit[rows] = one
            scale[rows] = size
            out[rows] = (one * gain + bias).astype(BF16)
        each(count or self.rows, self.tile, body, base)

    def project(self):
        normed, mixed, weight = self.ref("normed"), self.ref("qkv"), self.ref("w_qkv")

        def body(rows):
            mixed[rows] = dot(normed[rows], weight[...]).astype(BF16)
        each(self.rows, 128, body)

    def parts(self, rows):
        share, qkv = self.share, self.ref("qkv")
        return (qkv[rows, 0:share], qkv[rows, share:2 * share], qkv[rows, 2 * share:3 * share])

    def attend(self, ids_column, ids_row):
        probs, mixture = self.ref("probs"), self.ref("mixture")
        everything = pl.ds(0, self.rows)

        def body(queries):
            query = self.parts(queries)[0]
            unused, key_rows, values = self.parts(everything)
            allowed = ids_column[...] == ids_row[:, queries]

            def one(head, mixed):
                mask = head_mask(self.share, self.size, head)
                scores = jnp.where(
                    allowed, dot_b(keep(mask, key_rows), query) * self.scaling, MASKED_SCORE
                )
                exponent = jnp.exp(scores - jnp.max(scores, axis=0, keepdims=True))
                softmaxed = exponent * (1.0 / jnp.sum(exponent, axis=0, keepdims=True))
                probs[head, :, queries] = softmaxed
                return mixed + dot_t(keep(mask, values), softmaxed.astype(BF16))

            mixed = lax.fori_loop(0, self.heads, one, jnp.zeros((self.share, 128), F32))
            mixture[queries] = mixed.T.astype(BF16)
        each(self.rows, 128, body)

    def product(self, left, weight, back=False):
        target, deep = self.ref("part"), self.chunk

        def produce(at):
            rows = pl.ds(pl.multiple_of(at * deep, deep), deep)
            made = (dot_b if back else dot)(left[rows], weight[...])
            target[at, 0] = made[:deep // 2]
            target[at, 1] = made[deep // 2:]
        return produce

    def halves(self, rows):
        half = self.chunk // 2
        at = lax.div(rows.start, half)
        place = pl.ds(pl.multiple_of(lax.rem(rows.start, half), rows.size), rows.size)
        return self.ref("whole")[lax.div(at, 2), lax.rem(at, 2), place]

    def add_total(self, at):
        residual = self.ref("residual")

        def body(rows):
            residual[rows] = residual[rows] + self.halves(rows)
        each(self.chunk, self.tile, body, at * self.chunk)

    def expand(self, base=0, count=None):
        lifted, weight = self.ref("lifted"), self.ref("w_up")
        hidden, slope = self.ref("hidden"), self.ref("slope")

        def body(rows):
            def inner(columns):
                made, gradient = gelu_both(dot(lifted[rows], weight[:, columns]))
                hidden[rows, columns] = made.astype(BF16)
                slope[rows, columns] = gradient
            each(weight.shape[1], 256, inner)
        each(count or self.rows, 128, body, base)

    def back_hidden(self, branch, base=0, count=None):
        weight, slope, grad = self.ref("w_down"), self.ref("slope"), self.ref("grad_upper")

        def body(rows):
            def inner(columns):
                made = dot_b(branch[rows], weight[columns])
                grad[rows, columns] = (made * slope[rows, columns]).astype(BF16)
            each(weight.shape[0], 256, inner)
        each(count or self.rows, 128, body, base)

    def clear_sums(self):
        sums = self.ref("sums")
        sums[...] = jnp.zeros(sums.shape, F32)

    def norm_back(self, at, first, out):
        unit, scale = self.ref("unit_a" if first else "unit_b"), self.ref(
            "scale_a" if first else "scale_b")
        gain, grad, sums = self.row(0 if first else 2), self.ref("grad"), self.ref("sums")

        def body(rows):
            moved, gains, biases = norm_back(self.halves(rows), unit[rows], scale[rows], gain)
            new = grad[rows] + moved
            grad[rows] = new
            if out is not None:
                out[rows] = new.astype(BF16)
            sums[0:1] += gains
            sums[1:2] += biases
        each(self.chunk, self.tile, body, at * self.chunk)

    def back_mixture(self, branch, base=0, count=None):
        weight, grad = self.ref("w_out"), self.ref("grad_mixture")

        def body(rows):
            grad[rows] = dot_b(branch[rows], weight[...]).astype(BF16)
        each(count or self.rows, self.chunk, body, base)

    def attend_back(self):
        probs, grad_mixture, grads = self.ref("probs"), self.ref("grad_mixture"), self.ref(
            "grad_qkv")
        key_sum, value_sum = self.ref("key_sum"), self.ref("value_sum")
        share, everything = self.share, pl.ds(0, self.rows)
        key_sum[...] = jnp.zeros(key_sum.shape, F32)
        value_sum[...] = jnp.zeros(value_sum.shape, F32)

        def body(queries):
            query = self.parts(queries)[0]
            unused, key_rows, values = self.parts(everything)
            grad_rows = grad_mixture[queries]

            def one(head, total):
                mask = head_mask(share, self.size, head)
                softmaxed = probs[head, :, queries]
                grad_probs = dot_b(keep(mask, values), grad_rows)
                value_sum[...] += dot(softmaxed.astype(BF16), keep(mask, grad_rows))
                delta = jnp.sum(softmaxed * grad_probs, axis=0, keepdims=True)
                grad_scores = (softmaxed * (grad_probs - delta)).astype(BF16)
                key_sum[...] += dot(grad_scores, keep(mask, query))
                return total + dot_t(keep(mask, key_rows), grad_scores)

            total = lax.fori_loop(0, self.heads, one, jnp.zeros((share, 128), F32))
            grads[queries, 0:share] = (total.T * self.scaling).astype(BF16)
        each(self.rows, 128, body)

        def close(rows):
            grads[rows, share:2 * share] = (key_sum[rows] * self.scaling).astype(BF16)
            grads[rows, 2 * share:3 * share] = value_sum[rows].astype(BF16)
        each(self.rows, 128, close)


def weight_grad(left, right, target):
    if len(target.shape) == 4:
        parts, sides, rows, width = target.shape
        if rows >= 128:
            @pl.loop(0, parts * sides)
            def _(at):
                block = dot_t(left[:, span(at * rows, rows)], right[...])
                target[lax.div(at, sides), lax.rem(at, sides)] = block.astype(BF16)
        else:
            @pl.loop(0, parts)
            def _(at):
                block = dot_t(left[:, span(at * sides * rows, sides * rows)], right[...])
                target[at] = block.reshape(sides, rows, width).astype(BF16)
    else:
        sides, rows, width = target.shape
        if rows >= 128:
            @pl.loop(0, sides)
            def _(at):
                block = dot_t(left[:, span(at * rows, rows)], right[...])
                target[at] = block.astype(BF16)
        else:
            block = dot_t(left[...], right[...])
            target[...] = block.reshape(sides, rows, width).astype(BF16)


def vector_store(target, at, row, whole):
    for owner in range(8):
        block = owner if whole else owner // 2
        target[owner // 2, owner % 2, at:at + 1, :] = row[:, 128 * block:128 * block + 128]


COLUMN_UNITS = ("e_qkv", "e_up", "e_down", "embed", "d_qkv", "d_up")
ROW_UNITS = ("e_out", "d_out", "d_down")
ROW_SUMS = ("d_out", "d_down")
MESSAGES = COLUMN_UNITS + ROW_UNITS
TRADED = ("e_qkv", "e_up", "e_out")
GATHERED = ("e_down", "embed")
EARLY = ()


def unit_shapes(width, dec_width, hidden, dec_hidden):
    return {
        "e_qkv": (width // 8, 3 * width // 4),
        "e_up": (width // 8, hidden // 4),
        "e_down": (hidden // 32, width),
        "embed": (width // 8, dec_width // 4),
        "d_qkv": (dec_width // 8, 3 * dec_width // 4),
        "d_up": (dec_width // 8, dec_hidden // 4),
        "e_out": (width // 8, width),
        "d_out": (dec_width // 8, dec_width),
        "d_down": (dec_hidden // 8, dec_width),
    }


def scratch_table(width, dec_width, hidden, dec_hidden, rows, shown):
    units = unit_shapes(width, dec_width, hidden, dec_hidden)
    table = {}
    for name in COLUMN_UNITS:
        height, columns = units[name]
        if name != "embed":
            table["w_" + name] = ((8 * height, columns), BF16)
        table["g_" + name] = ((PARTS, SIDES, height, columns), BF16)
        table["m_" + name] = ((PARTS, height, columns), BF16)
        table["c_" + name] = ((PARTS, height, columns), BF16)
        if name in TRADED:
            del table["g_" + name]
            table["l_" + name] = ((PARTS, shown, 128), BF16)
            table["r_" + name] = ((shown, columns), BF16)
        if name in GATHERED:
            del table["g_" + name]
            del table["c_" + name]
            table["l_" + name] = ((8, shown, 128), BF16)
    table["w_embed"] = ((width, dec_width), BF16)
    for name in ROW_UNITS:
        height, columns = units[name]
        table["w_" + name] = ((2 * height, columns), BF16)
        if name == "e_out":
            narrow = columns // PARTS
            table["m_e_out"] = ((PARTS, height, narrow), BF16)
            table["c_e_out"] = ((PARTS, height, narrow), BF16)
            table["l_e_out"] = ((PARTS, shown, 128), BF16)
            table["r_e_out"] = ((shown, narrow), BF16)
            table["mixture_all"] = ((shown, width), BF16)
            continue
        table["g_" + name] = ((SIDES, height, columns), BF16)
        table["m_" + name] = ((height, columns), BF16)
        table["c_" + name] = ((2, height, columns), BF16)
    table["w_vector"] = ((8 * VECTORS, 128), BF16)
    table["g_vector"] = ((PARTS, SIDES, VECTORS, 128), F32)
    table["m_vector"] = ((PARTS, VECTORS, 128), F32)
    table["c_vector"] = ((PARTS, VECTORS, 128), F32)
    table["gains"] = ((VECTORS, width), F32)
    table["group"] = ((rows, width), BF16)
    table["cotangents"] = ((rows, dec_width), BF16)
    for key, count, wide, deep, heads, size, chunks in (
        ("e_", shown, width, hidden // 4, 4, 64, 1),
        ("d_", rows, dec_width, dec_hidden // 4, 4, 32, 4),
    ):
        share = heads * size
        for name, shape, kind in (
            ("residual", (count, wide), F32), ("unit_a", (count, wide), F32),
            ("unit_b", (count, wide), F32), ("scale_a", (count, 1), F32),
            ("scale_b", (count, 1), F32), ("normed", (count, wide), BF16),
            ("lifted", (count, wide), BF16), ("qkv", (count, 3 * share), BF16),
            ("probs", (heads, count, count), F32), ("mixture", (count, share), BF16),
            ("hidden", (count, deep), BF16), ("slope", (count, deep), F32),
            ("grad_upper", (count, deep), BF16), ("grad", (count, wide), F32),
            ("grad_mixture", (count, share), BF16), ("grad_qkv", (count, 3 * share), BF16),
            ("key_sum", (count, share), F32), ("value_sum", (count, share), F32),
            ("branch", (count, wide), BF16), ("branch_b", (count, wide), BF16),
            ("part", (chunks, 2, count // chunks // 2, wide), F32),
            ("met", (chunks, count // chunks // 2, wide), F32),
            ("out", (chunks, count // chunks // 2, wide), BF16),
            ("came", (2, chunks, count // chunks // 2, wide), BF16),
            ("whole", (chunks, 2, count // chunks // 2, wide), F32),
            ("sums", (8, wide), F32),
        ):
            table[key + name] = (shape, kind)
    table["last_part"] = ((2, 2, rows // 4, dec_width), F32)
    table["last_met"] = ((2, rows // 4, dec_width), F32)
    table["last_out"] = ((rows // 4, dec_width), BF16)
    table["last_came"] = ((rows // 4, dec_width), BF16)
    for name, shape, kind in (
        ("rank_row", (1, rows), jnp.int32), ("rank_column", (rows, 1), jnp.int32),
        ("ids_row", (1, rows), jnp.int32), ("ids_column", (rows, 1), jnp.int32),
        ("packed_row", (1, shown), jnp.int32), ("packed_column", (shown, 1), jnp.int32),
        ("code", (shown, width), F32), ("dec_code", (rows, dec_width), F32),
        ("staged", (VECTORS, 128), F32),
    ):
        table[name] = (shape, kind)
    table["lowered"] = ((shown, width), BF16)
    table["w_picked"] = ((8 * shown, dec_width), BF16)
    table["right"] = ((shown, width), BF16)
    return table


VECTOR_NAMES = (
    "v_gain_a", "v_bias_a", "v_gain_b", "v_bias_b", "v_mask",
    "v_dec_gain_a", "v_dec_bias_a", "v_dec_gain_b", "v_dec_bias_b",
)
INPUTS = ("lengths", "gsd", "visible") + VECTOR_NAMES + (
    "patches", "cotangent", "query", "key", "value", "out", "up", "down", "embed",
    "dec_query", "dec_key", "dec_value", "dec_out", "dec_up", "dec_down",
)
RESULTS = ("decoded", "grad_patches", "grad_vector") + MESSAGES
SEMAPHORES = {
    "local": (24,),
    "z_sent": (12,), "z_got": (12, 4), "y_sent": (12,), "y_got": (12, 4),
    "cross_sent": (1,), "cross_got": (1, 4),
    "gy_sent": (11,), "gy_got": (11,), "gz_sent": (11, 3), "gz_got": (11, 4),
    "f_sent": (5, 2), "f_got": (5, 2), "m_sent": (3,), "m_got": (3,), "gb_sent": (11, 4), "gb_got": (11, 3),
    "p_sent": (3,), "p_got": (3,), "c_sent": (3,), "c_got": (3,),
    "e_sent": (3,), "e_got": (3,), "l_sent": (2,), "l_got": (2,),
    "e_t_sent": (2, 1, 3), "e_t_got": (2, 1, 3), "d_t_sent": (2, 4, 3), "d_t_got": (2, 4, 3),
}


def place_of(ref, positions):
    ids = jnp.zeros(positions.shape, jnp.int32)
    first = jnp.zeros(positions.shape, jnp.int32)
    ratio = jnp.zeros(positions.shape, F32) + ref["gsd"][0, 0]
    end = jnp.int32(0)
    count = ref["lengths"].shape[1]
    for at in range(count - 1):
        end = end + ref["lengths"][0, at]
        later = positions >= end
        ids = ids + later.astype(jnp.int32)
        first = jnp.where(later, end, first)
        ratio = jnp.where(later, ref["gsd"][0, at + 1], ratio)
    return ids, (positions - first).astype(F32) * ratio


def lay_out(ref, rows, shown, width, dec_width):
    ids_row, scaled_row = place_of(ref, lax.broadcasted_iota(jnp.int32, (1, rows), 1))
    ids_column, scaled_column = place_of(ref, lax.broadcasted_iota(jnp.int32, (rows, 1), 0))
    ref["ids_row"][...] = ids_row
    ref["ids_column"][...] = ids_column
    visible = ref["visible"][...] > 0
    marks = jnp.broadcast_to(visible.astype(F32), (16, rows)).astype(BF16)
    down = lax.broadcasted_iota(jnp.int32, (rows, rows), 0)
    along = lax.broadcasted_iota(jnp.int32, (rows, rows), 1)
    until = (along <= down).astype(BF16)
    before = (along < down).astype(BF16)
    count_row = dot_b(marks, until)[0:1]
    rank_row = jnp.where(visible, count_row.astype(jnp.int32) - 1, -1)
    count_column = dot_b(until, marks)[:, 0:1].astype(jnp.int32)
    others = dot_b(before, marks)[:, 0:1].astype(jnp.int32)
    rank_column = jnp.where(count_column > others, others, -1)
    ref["rank_row"][...] = rank_row
    ref["rank_column"][...] = rank_column
    here = lax.broadcasted_iota(jnp.int32, (shown, rows), 0) == rank_row
    packed = jnp.sum(jnp.where(here, ids_row.astype(F32), 0.0), axis=1, keepdims=True)
    ref["packed_column"][...] = packed.astype(jnp.int32)
    packed_scaled = jnp.sum(jnp.where(here, scaled_row, 0.0), axis=1, keepdims=True)
    there = lax.broadcasted_iota(jnp.int32, (rows, shown), 1) == rank_column
    packed = jnp.sum(jnp.where(there, ids_column.astype(F32), 0.0), axis=0, keepdims=True)
    ref["packed_row"][...] = packed.astype(jnp.int32)
    for target, scaled, wide in (
        (ref["code"], packed_scaled, width), (ref["dec_code"], scaled_column, dec_width)
    ):
        half = wide // 2
        steps = lax.broadcasted_iota(jnp.int32, (1, half), 1).astype(F32)
        frequency = jnp.exp(steps * (-math.log(10000.0) / half))
        target[:, 0:1] = scaled
        tall = 16 * 1024 // half

        def body(part):
            angles = target[part, 0:1] * frequency
            made = jnp.concatenate([jnp.sin(angles), jnp.cos(angles)], axis=1)
            target[part] = made
        each(target.shape[0], tall, body)


def main_kernel(names, *refs):
    ref = dict(zip(names, refs))
    s = Split()
    shown, width = ref["code"].shape
    rows, dec_width = ref["dec_code"].shape
    own = ref["patches"].shape[0]
    sem = {name: ref["s_" + name] for name in SEMAPHORES}
    counter = [0]

    def local(source, target):
        at = counter[0]
        counter[0] = at + 1
        return pltpu.make_async_copy(source, target, sem["local"].at[at])

    barrier = pltpu.get_barrier_semaphore()
    peers = [(lax.rem(s.dp + step, 8), s.blk) for step in range(1, 8)] + list(s.blk_peers)
    for peer in peers:
        pl.semaphore_signal(barrier, inc=1, device_id=peer, device_id_type=pl.DeviceIdType.MESH)

    order = ("vector", "e_qkv", "e_out", "e_up", "embed", "e_down", "e_down_b", "d_qkv", "d_out",
             "d_up", "d_down")
    units = {}
    for at, name in enumerate(order):
        sems = tuple(sem[kind].at[at] for kind in ("z_sent", "z_got", "y_sent", "y_got"))
        sems = sems + (sem["cross_sent"].at[0], sem["cross_got"].at[0])
        whole = ref["w_e_down" if name == "e_down_b" else "w_" + name]
        if name == "vector":
            units[name] = Columns(s, whole, VECTORS, [], sems)
        elif name in ROW_UNITS:
            source = ref[{"e_out": "out", "d_out": "dec_out", "d_down": "dec_down"}[name]]
            height = source.shape[0]
            copy = local(source, whole.at[span(s.y * height, height)])
            units[name] = Rows(s, whole, height, copy, sems)
        else:
            height = ref["m_e_down" if name == "e_down_b" else "m_" + name].shape[1]
            mine = span(s.dp * height, height)
            columns = None
            if name in ("e_qkv", "d_qkv"):
                kinds = ("query", "key", "value")
                if name == "d_qkv":
                    kinds = ("dec_query", "dec_key", "dec_value")
                size = ref[kinds[0]].shape[1] // PARTS
                copies = [
                    local(ref[kind].at[:, span(s.part * size, size)],
                          whole.at[mine, pl.ds(place * size, size)])
                    for place, kind in enumerate(kinds)
                ]
            elif name == "e_up":
                size = height
                copies = [
                    local(ref["up"].at[:, span((owner * PARTS + s.blk) * size, size)],
                          whole.at[mine, pl.ds(owner * size, size)])
                    for owner in range(8)
                ]
            elif name in ("e_down", "e_down_b"):
                size = width // 2
                columns = pl.ds(size if name == "e_down_b" else 0, size)
                copies = [local(ref["down"].at[span(s.blk * height, height), columns],
                                whole.at[mine, columns])]
            elif name == "embed":
                size = dec_width // PARTS
                columns = span(s.part * size, size)
                copies = [local(ref["embed"].at[:, columns], whole.at[mine, columns])]
            else:
                size = ref["dec_up"].shape[1] // PARTS
                copies = [local(ref["dec_up"].at[:, span(s.part * size, size)], whole.at[mine])]
            kind = EarlyColumns if name in EARLY else Columns
            units[name] = kind(s, whole, height, copies, sems, columns)

    sums = {}
    for at, name in enumerate(order):
        if name == "e_down_b":
            continue
        sems = tuple(
            sem[kind].at[at]
            for kind in ("gy_sent", "gy_got", "gz_sent", "gz_got", "gb_sent", "gb_got")
        )
        kind = ColumnSum
        for names, other in ((ROW_SUMS, RowSum), (TRADED, ProductSum), (GATHERED, GatheredSum)):
            if name in names:
                kind = other
        done = None if name == "vector" else ref["o_" + name]
        wide = ref["m_" + name].shape[-1]
        sums[name] = kind(s, ref.get("g_" + name), ref["m_" + name], ref.get("c_" + name), done, sems,
                          16 if wide > 512 else 32 if name != "vector" else 8)
    all_picked = ref["w_picked"]
    embed_columns = span(s.part * (dec_width // PARTS), dec_width // PARTS)
    out_columns = span(s.part * (width // PARTS), width // PARTS)
    for at, (name, left, right, their_right) in enumerate((
        ("e_qkv", "e_normed", ref["e_grad_qkv"], ref["r_e_qkv"]),
        ("e_up", "e_lifted", ref["e_grad_upper"], ref["r_e_up"]),
        ("e_out", "mixture_all", ref["e_branch_b"].at[:, out_columns], ref["r_e_out"]),
    )):
        sums[name].trade(ref[left], right, ref["l_" + name], their_right,
                         (sem["f_sent"].at[at], sem["f_got"].at[at]))

    def of_group(group):
        return pl.ds(pl.multiple_of(group * shown, shown), shown)

    def embed_right(group):
        return all_picked[of_group(group), embed_columns]

    def down_right(group):
        def body(part):
            made = dot_b(all_picked[of_group(group)], ref["w_embed"][part])
            ref["right"][:, part] = made.astype(BF16)
        each(width, 256, body)
        return ref["right"][...]

    for at, (name, left, right) in enumerate((
        ("e_down", "e_hidden", down_right), ("embed", "lowered", embed_right),
    )):
        sums[name].gather(ref[left], ref["l_" + name],
                          (sem["f_sent"].at[3 + at, 0], sem["f_got"].at[3 + at, 0]), right)
    sems = tuple(sem[kind].at[11] for kind in ("z_sent", "z_got", "y_sent", "y_got"))
    picked_unit = Columns(s, all_picked, shown, [], sems + (None, None))

    totals = []
    for at in range(7):
        key, slot = ("e_", at % 2) if at in (0, 1, 5, 6) else ("d_", at % 2)
        totals.append(Total(
            s, *(ref[key + name] for name in ("part", "met", "out", "came", "whole")),
            (sem[key + "t_sent"].at[slot], sem[key + "t_got"].at[slot]), slot,
        ))

    encoder = Block(shown, width, 4, 64, "e_", ref, 0)
    decoder = Block(rows, dec_width, 4, 32, "d_", ref, 5)
    for block, key in ((encoder, "e_"), (decoder, "d_")):
        for short, long in (("w_qkv", "qkv"), ("w_out", "out"), ("w_up", "up"),
                            ("w_down", "down")):
            ref[key + short] = ref["w_" + key + long]

    for name in order:
        units[name].fetch()
    mine = span(s.blk * own, own)
    own_patches = local(ref["patches"], ref["group"].at[mine])
    own_cotangents = local(ref["cotangent"], ref["cotangents"].at[mine])
    own_patches.start()
    own_cotangents.start()
    staged = ref["staged"]
    staged[...] = jnp.zeros(staged.shape, F32)
    for at, name in enumerate(VECTOR_NAMES):
        row = ref[name][...].astype(F32)[None, :]
        staged[at:at + 1, 0:row.shape[1]] = row
    ref["w_vector"][span(s.dp * VECTORS, VECTORS)] = staged[...].astype(BF16)

    pl.semaphore_wait(barrier, len(peers))

    def place_in(name):
        return lambda blk: ref[name].at[span(blk * own, own)]

    def embed_block(blk):
        size = dec_width // PARTS
        return ref["w_embed"].at[:, span(lax.rem(3 * blk, PARTS) * size, size)]

    def mixture_block(blk):
        size = width // PARTS
        return ref["mixture_all"].at[:, span(lax.rem(3 * blk, PARTS) * size, size)]

    shared = {
        "p": Shared(s, ref["patches"], place_in("group"), (sem["p_sent"], sem["p_got"])),
        "c": Shared(s, ref["cotangent"], place_in("cotangents"), (sem["c_sent"], sem["c_got"])),
        "e": Shared(s, embed_block(s.blk), embed_block, (sem["e_sent"], sem["e_got"])),
        "m": Shared(s, ref["e_mixture"], mixture_block, (sem["m_sent"], sem["m_got"])),
    }
    for name in ("vector", "e_qkv", "e_out"):
        units[name].send()
    shared["p"].start()
    units["e_up"].send()

    lay_out(ref, rows, shown, width, dec_width)
    units["vector"].forward()
    units["e_qkv"].forward()
    shared["p"].pass_on()
    own_patches.wait()
    units["e_out"].forward()
    shared["p"].finish()

    places = (
        lax.broadcasted_iota(jnp.int32, (shown, rows), 0) == ref["rank_row"][...]
    ).astype(BF16)
    residual = ref["e_residual"]

    def place_patches(columns):
        residual[:, columns] = dot(places, ref["group"][:, columns]) + ref["code"][:, columns]
    each(width, 256, place_patches)

    units["e_up"].forward((1,))
    units["vector"].finish()
    vectors = ref["w_vector"][...].astype(F32)
    gains = ref["gains"]
    for at in range(9):
        for owner in range(8):
            row = vectors[VECTORS * owner + at:VECTORS * owner + at + 1, :]
            if at < 4:
                gains[at:at + 1, 128 * owner:128 * owner + 128] = row
            elif owner % 2 == 0:
                pair = VECTORS * (owner + 1) + at
                other = pltpu.roll(vectors[pair:pair + 1, :], 64, 1)
                gains[at:at + 1, 64 * owner:64 * owner + 128] = row + other
    encoder.norm(True)
    units["e_up"].forward((2,))
    units["embed"].send()
    units["e_down"].send()
    units["e_qkv"].finish()
    encoder.project()
    units["e_up"].forward((3,))
    encoder.attend(ref["packed_column"], ref["packed_row"])
    ref["mixture_all"][:, out_columns] = ref["e_mixture"][...]
    units["e_out"].finish()
    totals[0].begin(encoder.product(ref["e_mixture"], ref["w_e_out"]))
    units["embed"].forward()

    def after_attention(at):
        encoder.add_total(at)
        encoder.norm(False, at * encoder.chunk, encoder.chunk)
    totals[0].finish(after_attention)
    shared["c"].start()
    shared["m"].start()
    units["e_down"].forward()
    units["e_down_b"].send()
    units["e_up"].finish()
    encoder.expand()
    units["d_qkv"].send()
    units["d_out"].send()
    units["embed"].finish()
    shared["e"].start()
    shared["c"].pass_on()
    shared["m"].pass_on()
    units["e_down_b"].forward()
    units["d_up"].send()
    units["d_down"].send()
    units["d_qkv"].forward()
    shared["e"].pass_on()
    units["e_down"].finish()
    units["e_down_b"].finish()
    totals[1].begin(encoder.product(ref["e_hidden"], ref["w_e_down"]))
    units["d_out"].forward()
    units["d_up"].forward()
    shared["e"].finish()
    lowered = ref["lowered"]

    def after_hidden(at):
        encoder.add_total(at)
        part = pl.ds(pl.multiple_of(at * encoder.chunk, encoder.chunk), encoder.chunk)
        lowered[part] = residual[part].astype(BF16)
    totals[1].finish(after_hidden)

    embedded = dot(lowered[...], ref["w_embed"][...])
    high = embedded.astype(BF16)
    low = (embedded - high.astype(F32)).astype(BF16)
    token = gains[4:5, 0:dec_width]
    start = ref["d_residual"]

    def place_rows(part):
        rank = ref["rank_column"][part]
        here = (lax.broadcasted_iota(jnp.int32, (128, shown), 1) == rank).astype(BF16)
        made = jnp.where(rank >= 0, dot(here, high) + dot(here, low), token)
        start[part] = made + ref["dec_code"][part]
    each(rows, 128, place_rows)
    decoder.norm(True)
    units["d_down"].forward()
    units["d_qkv"].finish()
    decoder.project()
    decoder.attend(ref["ids_column"], ref["ids_row"])
    units["d_out"].finish()
    totals[2].begin(decoder.product(ref["d_mixture"], ref["w_d_out"]))
    units["d_up"].finish()
    units["d_down"].finish()
    last_part, last_met = ref["last_part"], ref["last_met"]
    quarter = rows // 4

    def decoder_rest(at):
        decoder.add_total(at)
        decoder.norm(False, at * decoder.chunk, decoder.chunk)
        decoder.expand(at * decoder.chunk, decoder.chunk)
        part = pl.ds(pl.multiple_of(at * quarter, quarter), quarter)
        made = dot(ref["d_hidden"][part], ref["w_d_down"][...])
        last_part[lax.div(at, 2), lax.rem(at, 2)] = made
    totals[2].finish(decoder_rest)
    last_sent, last_got = sem["l_sent"], sem["l_got"]
    last_first = remote(last_part.at[:, 1 - s.core], last_met, last_sent.at[0], last_got.at[0],
                        s.core_peer)
    last_second = remote(ref["last_out"], ref["last_came"], last_sent.at[1], last_got.at[1],
                         s.x_peer)
    last_first.start()

    own_cotangents.wait()
    shared["c"].finish()
    shared["m"].finish()
    for name in ("e_down", "embed", "e_up", "e_out", "e_qkv"):
        sums[name].start_left()
    cotangents, grad = ref["cotangents"], ref["d_grad"]
    multiply = decoder.product(ref["d_grad_upper"], ref["w_d_up"], back=True)

    def decoder_hidden(at):
        decoder.back_hidden(cotangents, at * decoder.chunk, decoder.chunk)
        multiply(at)
    totals[3].begin(decoder_hidden)
    last_first.wait_recv()

    def last_add(part):
        made = last_part[1 - s.x, s.core, part] + last_met[1 - s.x, part]
        ref["last_out"][part] = made.astype(BF16)
    each(quarter, 64, last_add)
    last_second.start()

    def copy_grad(part):
        grad[part] = cotangents[part].astype(F32)
    each(rows, 64, copy_grad)
    vector_grad = ref["g_vector"]
    vector_grad[...] = jnp.zeros(vector_grad.shape, F32)
    decoder.clear_sums()
    weight_grad(ref["d_hidden"], cotangents, ref["g_d_down"])
    sums["d_down"].start()
    weight_grad(ref["d_lifted"], ref["d_grad_upper"], ref["g_d_up"])
    sums["d_up"].start()

    def decoder_middle(at):
        decoder.norm_back(at, False, ref["d_branch"])
        decoder.back_mixture(ref["d_branch"], at * decoder.chunk, decoder.chunk)
    totals[3].finish(decoder_middle)
    vector_store(vector_grad, 7, ref["d_sums"][0:1], False)
    vector_store(vector_grad, 8, ref["d_sums"][1:2], False)
    decoder.attend_back()
    sums["d_down"].middle()
    totals[4].begin(decoder.product(ref["d_grad_qkv"], ref["w_d_qkv"], back=True))
    sums["d_up"].middle()

    def last_close(part):
        made = last_part[s.x, s.core, part] + last_met[s.x, part]
        before = ref["d_residual"][pl.ds(pl.multiple_of(s.blk * own + part.start, 64), 64)]
        whole = made + ref["last_came"][part].astype(F32) + before
        ref["decoded"][part] = whole.astype(BF16)
    decoder.clear_sums()
    weight_grad(ref["d_normed"], ref["d_grad_qkv"], ref["g_d_qkv"])
    sums["d_qkv"].start()
    weight_grad(ref["d_mixture"], ref["d_branch"], ref["g_d_out"])
    sums["d_out"].start()

    def decoder_first(at):
        decoder.norm_back(at, True, ref["d_branch_b"])
    totals[4].finish(decoder_first)
    picked = all_picked.at[of_group(s.dp)]
    picked[...] = dot(places, ref["d_branch_b"][...]).astype(BF16)
    picked_unit.send()
    encoder_grad = ref["e_grad"]

    def back_embed(part):
        made = dot_b(picked[...], ref["w_embed"][part])
        encoder_grad[:, part] = made
        ref["e_branch"][:, part] = made.astype(BF16)
    each(width, 256, back_embed)
    sums["d_down"].join()
    sums["d_up"].join()

    encoder.back_hidden(ref["e_branch"])
    sums["e_up"].start()
    totals[5].begin(encoder.product(ref["e_grad_upper"], ref["w_e_up"], back=True))
    picked_unit.forward((1, 2))
    encoder.clear_sums()
    sums["e_up"].middle()

    def encoder_middle(at):
        encoder.norm_back(at, False, ref["e_branch_b"])
        encoder.back_mixture(ref["e_branch_b"], at * encoder.chunk, encoder.chunk)
    totals[5].finish(encoder_middle)
    sums["e_out"].start()
    picked_unit.forward((3,))
    encoder.attend_back()
    sums["e_qkv"].start()
    totals[6].begin(encoder.product(ref["e_grad_qkv"], ref["w_e_qkv"], back=True))
    sums["d_down"].last()
    sums["d_up"].last()
    sums["e_out"].middle()
    sums["d_qkv"].middle()
    sums["d_out"].middle()
    vector_store(vector_grad, 2, ref["e_sums"][0:1], True)
    vector_store(vector_grad, 3, ref["e_sums"][1:2], True)
    encoder.clear_sums()
    sums["e_qkv"].middle()

    def encoder_first(at):
        encoder.norm_back(at, True, None)
    totals[6].finish(encoder_first)
    sums["e_up"].join()
    picked_unit.finish()
    sums["embed"].last()
    sums["e_down"].last()
    sums["d_down"].pass_on()
    sums["d_up"].pass_on()
    sums["d_qkv"].join()
    sums["d_out"].join()
    vector_store(vector_grad, 0, ref["e_sums"][0:1], True)
    vector_store(vector_grad, 1, ref["e_sums"][1:2], True)
    vector_store(vector_grad, 5, ref["d_sums"][0:1], False)
    vector_store(vector_grad, 6, ref["d_sums"][1:2], False)

    def mask_sum(at, total):
        part = pl.ds(pl.multiple_of(at * 64, 64), 64)
        hidden_row = ref["rank_column"][part] < 0
        return total + jnp.sum(jnp.where(hidden_row, grad[part], 0.0), axis=0, keepdims=True)
    token_grad = lax.fori_loop(0, rows // 64, mask_sum, jnp.zeros((1, dec_width), F32))
    vector_store(vector_grad, 4, token_grad, False)
    sums["vector"].start()
    rank = ref["rank_column"][mine]
    here = (lax.broadcasted_iota(jnp.int32, (own, shown), 1) == rank).astype(BF16)

    def place_grad(part):
        values = encoder_grad[:, part]
        top = values.astype(BF16)
        rest = (values - top.astype(F32)).astype(BF16)
        ref["grad_patches"][:, part] = dot(here, top) + dot(here, rest)
    each(width, 256, place_grad)
    last_second.wait_recv()
    each(quarter, 64, last_close)
    sums["e_out"].join()
    sums["d_qkv"].last()
    sums["d_out"].last()
    sums["vector"].middle()
    sums["e_qkv"].join()
    sums["vector"].join()
    sums["e_down"].pass_on()
    sums["e_up"].last()
    sums["e_out"].last()
    sums["d_qkv"].pass_on()
    sums["d_out"].pass_on()
    sums["e_up"].pass_on()
    sums["e_qkv"].last()
    sums["e_out"].pass_on()
    sums["embed"].pass_on()

    def vector_out(part, whole):
        ref["grad_vector"][part] = whole
    sums["vector"].total(vector_out)
    sums["vector"].drain()
    sums["e_qkv"].pass_on()
    for name in MESSAGES:
        sums[name].close()
    last_first.wait_send()
    last_second.wait_send()
    for name in order:
        units[name].drain()
    picked_unit.drain()
    for gathered in shared.values():
        gathered.drain()


def unpack_kernel(names, *refs):
    ref = dict(zip(names, refs))
    side = lax.rem(lax.axis_index("dp"), 2)
    ref["decoded"][...] = ref["i_decoded"][...]
    ref["grad_patches"][...] = ref["i_grad_patches"][...]
    vectors = ref["i_grad_vector"][...]
    for at, name in enumerate(("e_gain_a", "e_bias_a", "e_gain_b", "e_bias_b")):
        ref[name][...] = vectors[at:at + 1, :]
    for at, name in enumerate(("mask", "d_gain_a", "d_bias_a", "d_gain_b", "d_bias_b")):
        row = vectors[at + 4:at + 5, :]
        ref[name][...] = jnp.where(side == 0, row[:, 0:64], row[:, 64:128])
    for blk in range(PARTS):
        part = 3 * blk % PARTS
        for key in ("e_", "d_"):
            size = ref[key + "query"].shape[1] // PARTS
            for place, kind in enumerate(("query", "key", "value")):
                ref[key + kind][:, part * size:(part + 1) * size] = ref["i_" + key + "qkv"][
                    blk, :, place * size:(place + 1) * size].astype(F32)
        size = ref["i_e_up"].shape[1]
        for owner in range(8):
            column = (owner * PARTS + blk) * size
            ref["e_up"][:, column:column + size] = ref["i_e_up"][
                blk, :, owner * size:(owner + 1) * size].astype(F32)
        size = ref["i_e_down"].shape[1]
        ref["e_down"][blk * size:(blk + 1) * size, :] = ref["i_e_down"][blk].astype(F32)
        for name in ("embed", "d_up", "e_out"):
            size = ref["i_" + name].shape[2]
            ref[name][:, part * size:(part + 1) * size] = ref["i_" + name][blk].astype(F32)
    for name in ROW_SUMS:
        ref[name][...] = ref["i_" + name][...].astype(F32)


def local_kernel(*arguments):
    (patches, lengths, gsd_scale, visible,
     e_gain_a, e_bias_a, e_query, e_key, e_value, e_out, e_gain_b, e_bias_b, e_up, e_down,
     embed, mask,
     d_gain_a, d_bias_a, d_query, d_key, d_value, d_out, d_gain_b, d_bias_b, d_up, d_down,
     cotangent) = arguments
    width, dec_width = patches.shape[1], cotangent.shape[1]
    hidden, dec_hidden = e_up.shape[1], d_up.shape[1]
    rows = visible.shape[1]
    inputs = {
        "lengths": lengths, "gsd": gsd_scale, "visible": visible,
        "patches": patches, "cotangent": cotangent,
        "query": e_query, "key": e_key, "value": e_value, "out": e_out, "up": e_up,
        "down": e_down, "embed": embed, "dec_query": d_query, "dec_key": d_key,
        "dec_value": d_value, "dec_out": d_out, "dec_up": d_up, "dec_down": d_down,
    }
    inputs.update(zip(VECTOR_NAMES, (
        e_gain_a, e_bias_a, e_gain_b, e_bias_b, mask, d_gain_a, d_bias_a, d_gain_b, d_bias_b)))
    units = unit_shapes(width, dec_width, hidden, dec_hidden)
    shapes = {
        "decoded": (cotangent.shape, BF16), "grad_patches": (patches.shape, F32),
        "grad_vector": ((VECTORS, 128), F32),
    }
    for name in COLUMN_UNITS:
        shapes[name] = ((PARTS,) + units[name], BF16)
    for name in ROW_SUMS:
        shapes[name] = (units[name], BF16)
    shapes["e_out"] = ((PARTS, width // 8, width // PARTS), BF16)
    table = scratch_table(width, dec_width, hidden, dec_hidden, rows, SHOWN)
    names = INPUTS + tuple("o_" + name if name in MESSAGES else name for name in RESULTS)
    names = names + tuple(table) + tuple("s_" + name for name in SEMAPHORES)
    spaces = {"lengths": pltpu.SMEM, "gsd": pltpu.SMEM, "visible": pltpu.VMEM}
    spaces.update({name: pltpu.VMEM for name in VECTOR_NAMES})
    results = pl.pallas_call(
        functools.partial(main_kernel, names),
        out_shape=[jax.ShapeDtypeStruct(*shapes[name]) for name in RESULTS],
        in_specs=[pl.BlockSpec(memory_space=spaces.get(name, pl.ANY)) for name in INPUTS],
        out_specs=[
            pl.BlockSpec(memory_space=pl.ANY if name in MESSAGES else pltpu.VMEM)
            for name in RESULTS
        ],
        scratch_shapes=[pltpu.VMEM(*entry) for entry in table.values()]
        + [pltpu.SemaphoreType.DMA(shape) for shape in SEMAPHORES.values()],
        compiler_params=pltpu.CompilerParams(
            collective_id=0, has_side_effects=True, vmem_limit_bytes=62 * MIB
        ),
    )(*(inputs[name] for name in INPUTS))
    made = {"i_" + name: result for name, result in zip(RESULTS, results)}
    finals = {
        "decoded": (cotangent.shape, BF16), "grad_patches": (patches.shape, F32),
    }
    for key, wide, deep in (("e_", width, hidden), ("d_", dec_width, dec_hidden)):
        small, tall = wide // 8, deep // 8
        if key == "d_":
            finals["embed"] = ((width // 8, dec_width), F32)
            finals["mask"] = ((1, small), F32)
        for name, shape in (
            ("gain_a", (1, small)), ("bias_a", (1, small)), ("query", (small, wide)),
            ("key", (small, wide)), ("value", (small, wide)), ("out", (small, wide)),
            ("gain_b", (1, small)), ("bias_b", (1, small)), ("up", (small, deep)),
            ("down", (tall, wide)),
        ):
            finals[key + name] = (shape, F32)
    outputs = pl.pallas_call(
        functools.partial(unpack_kernel, tuple(made) + tuple(finals)),
        out_shape=[jax.ShapeDtypeStruct(*entry) for entry in finals.values()],
        in_specs=[pl.BlockSpec(memory_space=pltpu.VMEM)] * len(made),
        out_specs=[pl.BlockSpec(memory_space=pltpu.VMEM)] * len(finals),
        compiler_params=pltpu.CompilerParams(vmem_limit_bytes=62 * MIB),
    )(*made.values())
    return tuple(
        output.reshape(-1) if output.shape[0] == 1 else output for output in outputs
    )


def solution(mesh):
    both, vec, mat = P(("dp", "blk"), None), P("dp"), P("dp", None)
    block = (vec, vec, mat, mat, mat, mat, vec, vec, mat, mat)
    in_specs = (both, mat, mat, mat) + block + (mat, vec) + block + (both,)
    out_specs = (both, both) + block + (mat, vec) + block
    body = local_kernel if mesh.shape["dp"] == 8 and mesh.shape["blk"] == 4 else local
    return jax.shard_map(body, mesh=mesh, in_specs=in_specs, out_specs=out_specs, check_vma=False)
```
